32 devices in a mesh: groups: 2 (over x), dp: 16 (over z, y, core).
Axes of the slice: x: 2, y: 2, z: 4, core: 2. Of those that a mesh axis runs over, the one named last changes fastest.
Arguments:
- activations: bfloat16 [2, 32, 8192], P(None, ('groups', 'dp')), parts along dimension 1, may hold values from -6 to 6
- sample_ids: int32 [32], P(('groups', 'dp')), parts along dimension 0, may hold values from 0 to 31, as said below
- forward_exponent: int32 [2, 32, 64], P(None, ('groups', 'dp')), parts along dimension 1, may hold values from -8 to -2
- sender_base: float32 [2, 64, 8192], P(None, ('groups', 'dp')), parts along dimension 1, may hold values from -6 to 6
- receiver_base: float32 [2, 64, 8192], P(None, 'groups', 'dp'), parts along dimension 1, may hold values from -6 to 6
- norm_gain: float32 [8192], replicated, may hold values from 0.25 to 1.75
- up_weight: bfloat16 [8192, 14336], P(None, 'dp'), may hold values from -0.09375 to 0.09375
- down_weight: bfloat16 [14336, 8192], P('dp'), may hold values from -0.0625 to 0.0625
- cotangent: bfloat16 [2, 32, 8192], P(None, 'groups', 'dp'), parts along dimension 1, may hold values from -6 to 6
- backward_exponent: int32 [2, 32, 64], P(None, ('groups', 'dp')), parts along dimension 1, may hold values from -8 to -2
Outputs:
- new_sender_base: float32 [2, 64, 8192], P(None, ('groups', 'dp')), parts along dimension 1
- new_receiver_base: float32 [2, 64, 8192], P(None, 'groups', 'dp'), parts along dimension 1
- layer_out: bfloat16 [2, 32, 8192], P(None, 'groups', 'dp'), parts along dimension 1
- returned_grad: float32 [2, 32, 8192], P(None, ('groups', 'dp')), parts along dimension 1
The draws below stay inside these ranges and needn't reach their ends.
There are 2 independent parts, one for each index of `groups`. The reference program is written for one: setup_inputs(seed, part) draws one part's arguments, and reference() takes and returns one part's arrays. A program takes and returns all parts, laid end to end along the dimension named above; an argument that names none is the same for every part. Nothing has to cross between parts.
Inputs may be any that keep to these rules, and one draw needn't show every extreme that they name: sample_ids[s] lies in s * 2 to s * 2 + 1.
All inputs are finite; a program needn't handle non-finite values.
Results may differ from the reference program's by a relative error of at most 0.0057.
Values may be sent and summed in bfloat16 or wider, within the bound.
No kernel may reach another device: no remote copies, remote signals or barrier semaphores. Data moves between devices by JAX's collectives and lax.ppermute only.
A program may use at most 128 MiB of HBM per device.

```python
import jax
import jax.numpy as jnp
import numpy as np
from jax import lax

D = 8192
FF = 14336
LEN = 2
SLOT_DEV = 2
SEQS = 16
SLOTS = 32
NBLK = 64


def draw_sample_ids(key, part):
    key = jax.random.fold_in(key, 7)
    offsets = jax.random.randint(key, (SEQS,), 0, SLOT_DEV, dtype=jnp.int32)
    positions = jnp.arange(SEQS, dtype=jnp.int32)
    offsets = jnp.where(positions == 0, jnp.int32(0), offsets)
    offsets = jnp.where(positions == SEQS - 1, jnp.int32(SLOT_DEV - 1), offsets)
    return (positions * SLOT_DEV + offsets).astype(jnp.int32)


def place_ends(entries, own_key, smallest, largest):
    index_at = [jax.random.randint(jax.random.fold_in(own_key, axis), (), 0, length) for axis, length in enumerate(entries.shape)]
    longest = entries.shape.index(max(entries.shape))
    neighbour = index_at[:longest] + [(index_at[longest] + 1) % entries.shape[longest]] + index_at[longest + 1:]
    return entries.at[tuple(index_at)].set(smallest).at[tuple(neighbour)].set(largest)


def with_spikes(result, rng, source, target, shards_of, factor):
    def block_of(axis_at):
        return (jnp.arange(result.shape[axis_at]) // (result.shape[axis_at] // shards_of)).reshape((-1,) + (1,) * (result.ndim - 1 - axis_at))

    near = jax.random.permutation(rng, shards_of)[block_of(target)]
    other_side = (block_of(target) + shards_of // 2) % shards_of
    return jnp.where((block_of(source) == near) | (block_of(source) == other_side), factor * result, result)


def level_of(stream_key, extent, cuts, least, high):
    factor_of, own = 1.0, jax.random.fold_in(stream_key, 6)
    for axis_at, parts in cuts:
        draws = jnp.exp(jax.random.uniform(jax.random.fold_in(own, axis_at), (parts,), jnp.float32, least / len(cuts), high / len(cuts)))
        factor_of = factor_of * jnp.repeat(draws, extent[axis_at] // parts).reshape([-1 if axis == axis_at else 1 for axis in range(len(extent))])
    return factor_of


def noise(key, shape, scale, most, split=(), kind=jnp.bfloat16):
    result = scale * jax.random.normal(key, shape, jnp.float32)
    if split:
        result = result * level_of(key, shape, split, -0.22, 0.18)
    return jnp.clip(result, -most, most).astype(kind)


def bell_draw_with(own_key, dims, spread, limit, cuts, heavy, held_as=jnp.bfloat16):
    entries = spread * jax.random.normal(own_key, dims, jnp.float32)
    if cuts:
        entries = entries * level_of(own_key, dims, cuts, -0.22, 0.18)
    return jnp.clip(with_spikes(entries, jax.random.fold_in(own_key, 3), *heavy), -limit, limit).astype(held_as)


def setup_inputs(seed: int = 0, part: int = 0) -> dict:
    streams_of = jax.random.split(jax.random.key(seed), 11)
    part_splits = jax.random.split(jax.random.fold_in(streams_of[10], part), 11)
    return {
        "activations": noise(part_splits[0], (LEN, SEQS, D), 1.0, 6.0, ((1, 16),)),
        "sample_ids": draw_sample_ids(jax.random.fold_in(jax.random.fold_in(streams_of[10], part), 71), part),
        "forward_exponent": place_ends(jax.random.randint(part_splits[2], (LEN, SEQS, NBLK), -8, -1), jax.random.fold_in(part_splits[2], 1), -8, (-1) - 1).astype(jnp.int32),
        "sender_base": noise(part_splits[3], (LEN, SLOTS, D), 1.0, 6.0, ((1, 16),), jnp.float32),
        "receiver_base": noise(part_splits[4], (LEN, SLOTS, D), 1.0, 6.0, ((2, 16),), jnp.float32),
        "norm_gain": jnp.clip(1.0 + 0.15 * jax.random.normal(streams_of[5], (D,), jnp.float32), 0.25, 1.75),
        "up_weight": bell_draw_with(streams_of[6], (D, FF), D ** -0.5, 0.09375, ((1, 16),), (1, 0, 16, 2.0)),
        "down_weight": bell_draw_with(streams_of[7], (FF, D), FF ** -0.5, 0.0625, ((0, 16),), (0, 1, 16, 2.0)),
        "cotangent": noise(part_splits[8], (LEN, SEQS, D), 1.0, 6.0, ((2, 16),)),
        "backward_exponent": place_ends(jax.random.randint(part_splits[9], (LEN, SEQS, NBLK), -8, -1), jax.random.fold_in(part_splits[9], 1), -8, (-1) - 1).astype(jnp.int32),
    }


clip_top = 448.0
eps = 1e-05

def powers(exponent, sign):
    levels = jnp.arange(-10, 1, dtype=jnp.int32)
    table = jnp.asarray(2.0 ** (sign * np.arange(-10, 1)), jnp.float32)
    matches = exponent[..., None] == levels
    return lax.optimization_barrier(jnp.sum(jnp.where(matches, table, jnp.float32(0.0)), axis=-1))

def quantize(values, exponent):
    dims_all = values.shape
    blocks = values.reshape(dims_all[:-1] + (exponent.shape[-1], dims_all[-1] // exponent.shape[-1]))
    scaled = jnp.clip(blocks * powers(exponent, -1)[..., None], -clip_top, clip_top).astype(jnp.bfloat16)
    return (scaled.astype(jnp.float32) * powers(exponent, 1)[..., None]).reshape(dims_all)

def reference(activations, sample_ids, forward_exponent, sender_base, receiver_base, norm_gain, up_weight, down_weight, cotangent, backward_exponent):
    chosen_send = jnp.take(sender_base, sample_ids, axis=1)
    delta = activations.astype(jnp.float32) - chosen_send
    sent = quantize(delta, forward_exponent).astype(jnp.bfloat16)
    sent_wide = sent.astype(jnp.float32)
    new_sender_base = sender_base.at[:, sample_ids, :].set(chosen_send + sent_wide)
    rebuilt = jnp.take(receiver_base, sample_ids, axis=1) + sent_wide
    new_receiver_base = receiver_base.at[:, sample_ids, :].set(rebuilt)
    restored = rebuilt.astype(jnp.bfloat16).reshape(LEN * SEQS, D)
    restored_wide = restored.astype(jnp.float32)
    squares = lax.optimization_barrier(jnp.sum(restored_wide * restored_wide, axis=1))
    inv_rms = lax.rsqrt(squares / D + eps)
    scaled_in = (restored_wide * norm_gain).astype(jnp.bfloat16)
    hidden = inv_rms[:, None] * jnp.dot(scaled_in, up_weight, preferred_element_type=jnp.float32)
    active = jax.nn.silu(hidden).astype(jnp.bfloat16)
    mixed = restored_wide + jnp.dot(active, down_weight, preferred_element_type=jnp.float32)
    layer_out = mixed.astype(jnp.bfloat16).reshape(LEN, SEQS, D)
    grad_rows = cotangent.reshape(LEN * SEQS, D)
    grad_active = jnp.dot(grad_rows, down_weight.T, preferred_element_type=jnp.float32)
    sigma = jax.nn.sigmoid(hidden)
    grad_hidden = (grad_active * sigma * (1.0 + hidden * (1.0 - sigma))).astype(jnp.bfloat16)
    curvature = lax.optimization_barrier(jnp.sum(grad_hidden.astype(jnp.float32) * hidden, axis=1))
    grad_norm = jnp.dot(grad_hidden, up_weight.T, preferred_element_type=jnp.float32)
    grad_input = grad_rows.astype(jnp.float32) + inv_rms[:, None] * norm_gain * grad_norm - (curvature * inv_rms * inv_rms / D)[:, None] * restored_wide
    returned_grad = quantize(grad_input.reshape(LEN, SEQS, D), backward_exponent)
    return (new_sender_base, new_receiver_base, layer_out, returned_grad)
```

```python
import functools

import jax
import jax.numpy as jnp
from jax import lax
from jax.experimental import pallas as pl
from jax.experimental.pallas import tpu as pltpu
from jax.sharding import PartitionSpec as P

clip_top = 448.0
eps = 1e-05
LANES = 128
f32 = jnp.float32
bf16 = jnp.bfloat16
VMEM = pl.BlockSpec(memory_space=pltpu.VMEM)
SMEM = pl.BlockSpec(memory_space=pltpu.SMEM)


def powers(exponent, sign):
    total = jnp.zeros(exponent.shape, f32)
    for level in range(-10, 1):
        total = jnp.where(exponent == level, f32(2.0 ** (sign * level)), total)
    return total


def params(megabytes):
    return pltpu.CompilerParams(vmem_limit_bytes=megabytes << 20)


def send_kernel(offset_ref, act_ref, expo_ref, base_ref, out_ref, new_ref, rows_ref):
    n, rows, _ = out_ref.shape
    width = act_ref.shape[1]
    per_dev = width // LANES // n
    first = offset_ref[0] == 0
    down, up = powers(expo_ref[...], -1), powers(expo_ref[...], 1)
    old = [base_ref[p] for p in range(2)]
    chosen = jnp.concatenate([jnp.where(first, o[0:1], o[1:2]) for o in old], axis=0)
    delta = act_ref[...].astype(f32) - chosen
    fill = jnp.full((rows - 2 * per_dev, LANES), offset_ref[0].astype(f32))
    pieces = []
    for b in range(width // LANES):
        scaled = delta[:, b * LANES : (b + 1) * LANES] * down[:, b : b + 1]
        kept = jnp.clip(scaled, -clip_top, clip_top).astype(bf16).astype(f32) * up[:, b : b + 1]
        d, c = divmod(b, per_dev)
        rows_ref[d, 2 * c : 2 * c + 2, :] = kept
        pieces.append(kept)
    for d in range(n):
        rows_ref[d, 2 * per_dev :, :] = fill
    out_ref[...] = rows_ref[...].astype(bf16)
    new = chosen + jnp.concatenate(pieces, axis=1)
    for p in range(2):
        row = new[p : p + 1]
        new_ref[p, 0:1, :] = jnp.where(first, row, old[p][0:1])
        new_ref[p, 1:2, :] = jnp.where(first, old[p][1:2], row)


def rebuild_kernel(arrived_ref, base_ref, new_ref, out_ref, share_ref, rows_ref, slots_ref):
    n, rows, _ = arrived_ref.shape
    copies, _, width = out_ref.shape
    rows_ref[...] = arrived_ref[...].astype(f32).reshape(n * rows, LANES)
    per_dev = width // LANES
    first = rows_ref[pl.ds(2 * per_dev, n, stride=rows), :] == 0.0
    for p in range(2):
        for c in range(per_dev):
            cols = slice(c * LANES, (c + 1) * LANES)
            sent = rows_ref[pl.ds(2 * c + p, n, stride=rows), :]
            at = p * per_dev + c
            slots_ref[at] = base_ref[p, :, cols]
            even = slots_ref[at, pl.ds(0, n, stride=2), :]
            odd = slots_ref[at, pl.ds(1, n, stride=2), :]
            rebuilt = jnp.where(first, even, odd) + sent
            slots_ref[at, pl.ds(0, n, stride=2), :] = jnp.where(first, rebuilt, even)
            slots_ref[at, pl.ds(1, n, stride=2), :] = jnp.where(first, odd, rebuilt)
            new_ref[p, :, cols] = slots_ref[at]
            restored = rebuilt.astype(bf16)
            share_ref[p * n : (p + 1) * n, cols] = restored
            for k in range(copies):
                out_ref[k, p * n : (p + 1) * n, cols] = restored


def dot_nt(a, b):
    return lax.dot_general(a, b, (((1,), (1,)), ((), ())), preferred_element_type=f32)


def own_rows(piece_ref, own_ref, me, owner):
    n = piece_ref.shape[0] // 2
    for p in range(2):
        own_ref[pl.ds(p * n + owner, 1), :] = piece_ref[pl.ds(p * n + me, 1), :]


def grad_active_kernel(owner_of, me_ref, a_ref, b_ref, weight_ref, out_ref, own_ref, piece_ref):
    i, half = pl.program_id(0), a_ref.shape[0]
    me = me_ref[0]

    @pl.when(i == 0)
    def _():
        out_ref[...] = jnp.zeros_like(out_ref)

    k = lax.rem(i, half)
    piece = jnp.where(i < half, a_ref[k], b_ref[k])
    out_ref[...] += dot_nt(piece, weight_ref[...])
    piece_ref[...] = piece.astype(f32)
    own_rows(piece_ref, own_ref, me, owner_of(i, me))


def up_kernel(
    owner_of, width_all, me_ref, a_ref, b_ref, gain_ref, weight_ref, ga_ref,
    active_ref, gh_ref, own_ref, piece_ref, acc_ref, square_ref,
):
    i, half = pl.program_id(0), a_ref.shape[0]
    me = me_ref[0]

    @pl.when(i == 0)
    def _():
        acc_ref[...] = jnp.zeros_like(acc_ref)
        square_ref[...] = jnp.zeros_like(square_ref)

    k = lax.rem(i, half)
    piece = jnp.where(i < half, a_ref[k], b_ref[k]).astype(f32)
    piece_ref[...] = piece
    own_rows(piece_ref, own_ref, me, owner_of(i, me))
    squares = piece * piece
    for c in range(piece.shape[1] // LANES):
        square_ref[...] += squares[:, c * LANES : (c + 1) * LANES]
    scaled = (piece * gain_ref[0]).astype(bf16)
    acc_ref[...] += jnp.dot(scaled, weight_ref[...], preferred_element_type=f32)

    @pl.when(i == pl.num_programs(0) - 1)
    def _():
        total = jnp.sum(square_ref[...], axis=1, keepdims=True)
        hidden = lax.rsqrt(total / width_all + eps) * acc_ref[...]
        sigma = jax.nn.sigmoid(hidden)
        active_ref[...] = (hidden * sigma).astype(bf16)
        gh_ref[...] = (ga_ref[...] * sigma * (1.0 + hidden * (1.0 - sigma))).astype(bf16)


def down_kernel(me_ref, active_ref, weight_ref, out_ref):
    out_ref[0] = jnp.dot(active_ref[...], weight_ref[...], preferred_element_type=f32).astype(bf16)


def grad_norm_kernel(me_ref, gh_ref, weight_ref, send_ref, keep_ref, rows_ref):
    i = pl.program_id(0)
    half, tokens, width = send_ref.shape
    n = 2 * half
    terms = dot_nt(gh_ref[...], weight_ref[...])
    per_step = terms.shape[1] // width
    chunks = width // LANES
    for j in range(per_step):
        share = i * per_step + j
        for p in range(2):
            for c in range(chunks):
                at = j * width + c * LANES
                rows_ref[c, pl.ds(p * n + share, n, stride=tokens), :] = terms[
                    p * n : (p + 1) * n, at : at + LANES
                ]

    @pl.when(i == pl.num_programs(0) - 1)
    def _():
        core = lax.rem(me_ref[0], 2)
        for k in range(half):
            keep_at = pl.multiple_of((2 * k + core) * tokens, tokens)
            send_at = pl.multiple_of((2 * k + 1 - core) * tokens, tokens)
            for c in range(chunks):
                cols = slice(c * LANES, (c + 1) * LANES)
                keep_ref[k, :, cols] = rows_ref[c, pl.ds(keep_at, tokens), :].astype(bf16)
                send_ref[k, :, cols] = rows_ref[c, pl.ds(send_at, tokens), :].astype(bf16)


def pair_kernel(grad_ref, grad_in_ref, out_ref, out_in_ref, sum_ref):
    sum_ref[:, 0] = (grad_ref[...].astype(f32) + grad_in_ref[...].astype(f32)).astype(bf16)
    sum_ref[:, 1] = (out_ref[...].astype(f32) + out_in_ref[...].astype(f32)).astype(bf16)


def final_kernel(
    width_all, terms_ref, restored_ref, own_ref, cot_ref, gain_ref, expo_ref, layer_ref, grad_ref
):
    half, _, tokens, width = terms_ref.shape
    n = 2 * half
    grad = terms_ref[0, 0].astype(f32)
    layer = terms_ref[0, 1].astype(f32)
    for k in range(1, half):
        grad = grad + terms_ref[k, 0].astype(f32)
        layer = layer + terms_ref[k, 1].astype(f32)
    layer_ref[...] = (restored_ref[...].astype(f32) + layer).astype(bf16)
    down, up = powers(expo_ref[...], -1), powers(expo_ref[...], 1)
    gain = gain_ref[...]
    per_dev = width // LANES
    blocks = n * per_dev
    at_row = lax.broadcasted_iota(jnp.int32, (n, blocks), 0)
    at_lane = lax.broadcasted_iota(jnp.int32, (n, blocks), 1)
    for p in range(2):
        rows = slice(p * n, (p + 1) * n)
        own, norm = own_ref[rows, :], grad[rows, :]
        inv_rms = lax.rsqrt(jnp.sum(own * own, keepdims=True) / width_all + eps)
        scaled_in = (own * gain).astype(bf16).astype(f32)
        curvature = inv_rms * jnp.sum(scaled_in * norm, keepdims=True)
        correction = curvature * inv_rms * inv_rms / width_all
        value = cot_ref[rows, :] + inv_rms * gain * norm - correction * own
        for c in range(per_dev):
            at = at_lane == at_row * per_dev + c
            shrink = jnp.sum(jnp.where(at, down[p : p + 1], 0.0), axis=1, keepdims=True)
            grow = jnp.sum(jnp.where(at, up[p : p + 1], 0.0), axis=1, keepdims=True)
            scaled = value[:, c * LANES : (c + 1) * LANES] * shrink
            kept = jnp.clip(scaled, -clip_top, clip_top).astype(bf16).astype(f32) * grow
            grad_ref[p, pl.ds(c, n, stride=per_dev), :] = kept


def on_device(
    activations,
    sample_ids,
    forward_exponent,
    sender_base,
    receiver_base,
    norm_gain,
    up_weight,
    down_weight,
    cotangent,
    backward_exponent,
    *,
    n,
):
    half, quarter = n // 2, n // 4
    tokens = 2 * n
    width_all, hidden_dev = up_weight.shape
    width = width_all // n
    me = lax.axis_index("dp").astype(jnp.int32)
    me_in = me.reshape(1)
    core_pair = [(d, d ^ 1) for d in range(n)]
    row_pair = [(d, d ^ 2) for d in range(n)]
    same_core = [[2 * k + c for k in range(half)] for c in range(2)]

    cot = cotangent.reshape(1, tokens, width)
    line = [cot]
    for r in range(1, quarter):
        line.append(lax.ppermute(cot, "dp", [(d, (d + 4 * r) % n) for d in range(n)]))
    line = jnp.concatenate(line, axis=0)
    cot_a = jnp.concatenate([line, lax.ppermute(line, "dp", row_pair)], axis=0)
    cot_b = lax.ppermute(cot_a, "dp", core_pair)

    def cot_owner(i, who):
        core, row, along = lax.rem(who, 2), lax.rem(who // 2, 2), who // 4
        other_core, other_row, back = i // half, lax.rem(i // quarter, 2), lax.rem(i, quarter)
        at = lax.rem(along - back + quarter, quarter)
        return 4 * at + 2 * lax.rem(row + other_row, 2) + lax.rem(core + other_core, 2)

    def token_owner(i, who):
        return 2 * lax.rem(i, half) + lax.rem(who + i // half, 2)

    slots = sender_base.shape[1]
    offset = sample_ids - slots * me
    rows = -(-(2 * width // LANES + 1) // 16) * 16
    blocks, new_sender_base = pl.pallas_call(
        send_kernel,
        out_shape=(
            jax.ShapeDtypeStruct((n, rows, LANES), bf16),
            jax.ShapeDtypeStruct(sender_base.shape, f32),
        ),
        in_specs=[SMEM, VMEM, VMEM, VMEM],
        out_specs=(VMEM, VMEM),
        scratch_shapes=[pltpu.VMEM((n, rows, LANES), f32)],
        compiler_params=params(16),
    )(offset, activations.reshape(2, width_all), forward_exponent.reshape(2, -1), sender_base)
    arrived = lax.all_to_all(blocks, "dp", split_axis=0, concat_axis=0, tiled=True)

    new_receiver_base, restored, share = pl.pallas_call(
        rebuild_kernel,
        out_shape=(
            jax.ShapeDtypeStruct(receiver_base.shape, f32),
            jax.ShapeDtypeStruct((half, tokens, width), bf16),
            jax.ShapeDtypeStruct((tokens, width), bf16),
        ),
        in_specs=[VMEM, VMEM],
        out_specs=(VMEM, VMEM, VMEM),
        scratch_shapes=[
            pltpu.VMEM((n * rows, LANES), f32),
            pltpu.VMEM((2 * width // LANES, 2 * n, LANES), f32),
        ],
        compiler_params=params(16),
    )(arrived, receiver_base)
    rest_a = lax.all_to_all(
        restored, "dp", split_axis=0, concat_axis=0, axis_index_groups=same_core, tiled=True
    )
    rest_b = lax.ppermute(rest_a, "dp", core_pair)

    whole = lambda *shape: pl.BlockSpec(shape, lambda i, who: (0,) * len(shape))
    pieces = whole(half, tokens, width)

    grad_active, own_cot = pl.pallas_call(
        functools.partial(grad_active_kernel, cot_owner),
        out_shape=(
            jax.ShapeDtypeStruct((tokens, hidden_dev), f32),
            jax.ShapeDtypeStruct((tokens, width), f32),
        ),
        grid_spec=pltpu.PrefetchScalarGridSpec(
            num_scalar_prefetch=1,
            grid=(n,),
            in_specs=[
                pieces,
                pieces,
                pl.BlockSpec((hidden_dev, width), lambda i, who: (0, cot_owner(i, who[0]))),
            ],
            out_specs=(whole(tokens, hidden_dev), whole(tokens, width)),
            scratch_shapes=[pltpu.VMEM((tokens, width), f32)],
        ),
        compiler_params=params(24),
        cost_estimate=pl.CostEstimate(
            flops=2 * tokens * width_all * hidden_dev,
            bytes_accessed=2 * width_all * hidden_dev,
            transcendentals=0,
        ),
    )(me_in, cot_a, cot_b, down_weight)

    active, grad_hidden, own_restored = pl.pallas_call(
        functools.partial(up_kernel, token_owner, width_all),
        out_shape=(
            jax.ShapeDtypeStruct((tokens, hidden_dev), bf16),
            jax.ShapeDtypeStruct((tokens, hidden_dev), bf16),
            jax.ShapeDtypeStruct((tokens, width), f32),
        ),
        grid_spec=pltpu.PrefetchScalarGridSpec(
            num_scalar_prefetch=1,
            grid=(n,),
            in_specs=[
                pieces,
                pieces,
                pl.BlockSpec((1, 1, width), lambda i, who: (token_owner(i, who[0]), 0, 0)),
                pl.BlockSpec((width, hidden_dev), lambda i, who: (token_owner(i, who[0]), 0)),
                whole(tokens, hidden_dev),
            ],
            out_specs=(whole(tokens, hidden_dev), whole(tokens, hidden_dev), whole(tokens, width)),
            scratch_shapes=[
                pltpu.VMEM((tokens, width), f32),
                pltpu.VMEM((tokens, hidden_dev), f32),
                pltpu.VMEM((tokens, LANES), f32),
            ],
        ),
        compiler_params=params(24),
        cost_estimate=pl.CostEstimate(
            flops=2 * tokens * width_all * hidden_dev,
            bytes_accessed=2 * width_all * hidden_dev,
            transcendentals=0,
        ),
    )(me_in, rest_a, rest_b, norm_gain.reshape(n, 1, width), up_weight, grad_active)

    step = max(width, 1024)
    grad_send, grad_keep = pl.pallas_call(
        grad_norm_kernel,
        out_shape=(jax.ShapeDtypeStruct((half, tokens, width), bf16),) * 2,
        grid_spec=pltpu.PrefetchScalarGridSpec(
            num_scalar_prefetch=1,
            grid=(width_all // step,),
            in_specs=[
                whole(tokens, hidden_dev),
                pl.BlockSpec((step, hidden_dev), lambda i, who: (i, 0)),
            ],
            out_specs=(pieces, pieces),
            scratch_shapes=[pltpu.VMEM((width // LANES, n * tokens, LANES), f32)],
        ),
        compiler_params=params(24),
        cost_estimate=pl.CostEstimate(
            flops=2 * tokens * width_all * hidden_dev,
            bytes_accessed=2 * width_all * hidden_dev,
            transcendentals=0,
        ),
    )(me_in, grad_hidden, up_weight)
    grad_in = lax.ppermute(grad_send, "dp", core_pair)

    def down_terms(other):
        return pl.pallas_call(
            down_kernel,
            out_shape=jax.ShapeDtypeStruct((half, tokens, width), bf16),
            grid_spec=pltpu.PrefetchScalarGridSpec(
                num_scalar_prefetch=1,
                grid=(half,),
                in_specs=[
                    whole(tokens, hidden_dev),
                    pl.BlockSpec(
                        (hidden_dev, width),
                        lambda i, who: (0, 2 * i + lax.rem(who[0] + other, 2)),
                    ),
                ],
                out_specs=pl.BlockSpec((1, tokens, width), lambda i, who: (i, 0, 0)),
            ),
            compiler_params=params(24),
            cost_estimate=pl.CostEstimate(
                flops=tokens * width_all * hidden_dev,
                bytes_accessed=width_all * hidden_dev,
                transcendentals=0,
            ),
        )(me_in, active, down_weight)

    out_in = lax.ppermute(down_terms(1), "dp", core_pair)
    out_keep = down_terms(0)

    sums = pl.pallas_call(
        pair_kernel,
        out_shape=jax.ShapeDtypeStruct((half, 2, tokens, width), bf16),
        in_specs=[VMEM] * 4,
        out_specs=VMEM,
        compiler_params=params(16),
    )(grad_keep, grad_in, out_keep, out_in)
    terms = lax.all_to_all(
        sums, "dp", split_axis=0, concat_axis=0, axis_index_groups=same_core, tiled=True
    )
    layer_out, returned = pl.pallas_call(
        functools.partial(final_kernel, width_all),
        out_shape=(
            jax.ShapeDtypeStruct((tokens, width), bf16),
            jax.ShapeDtypeStruct((2, width_all // LANES, LANES), f32),
        ),
        in_specs=[VMEM] * 6,
        out_specs=(VMEM, VMEM),
        compiler_params=params(16),
    )(
        terms,
        share,
        own_restored,
        own_cot,
        norm_gain.reshape(n, width),
        backward_exponent.reshape(2, -1),
    )
    return (
        new_sender_base,
        new_receiver_base,
        layer_out.reshape(2, n, width),
        returned.reshape(2, 1, width_all),
    )


def solution(mesh):
    placed = (
        P(None, ("groups", "dp"), None),
        P(("groups", "dp")),
        P(None, ("groups", "dp"), None),
        P(None, ("groups", "dp"), None),
        P(None, "groups", "dp"),
        P(),
        P(None, "dp"),
        P("dp", None),
        P(None, "groups", "dp"),
        P(None, ("groups", "dp"), None),
    )
    return jax.shard_map(
        functools.partial(on_device, n=mesh.shape["dp"]),
        mesh=mesh,
        in_specs=placed,
        out_specs=(
            P(None, ("groups", "dp"), None),
            P(None, "groups", "dp"),
            P(None, "groups", "dp"),
            P(None, ("groups", "dp"), None),
        ),
        check_vma=False,
    )
```

```python
import functools

import jax
import jax.numpy as jnp
from jax import lax
from jax.experimental import pallas as pl
from jax.experimental.pallas import tpu as pltpu
from jax.sharding import PartitionSpec as P

clip_top = 448.0
eps = 1e-05
LANES = 128
f32 = jnp.float32
bf16 = jnp.bfloat16
VMEM = pl.BlockSpec(memory_space=pltpu.VMEM)
SMEM = pl.BlockSpec(memory_space=pltpu.SMEM)


def hbm(x):
    return pltpu.with_memory_space_constraint(x, pltpu.HBM)


def powers(exponent, sign):
    total = jnp.zeros(exponent.shape, f32)
    for level in range(-10, 1):
        total = jnp.where(exponent == level, f32(2.0 ** (sign * level)), total)
    return total


def params(megabytes):
    return pltpu.CompilerParams(vmem_limit_bytes=megabytes << 20)


def send_kernel(
    offset_ref, act_ref, expo_ref, base_ref, received_ref, cot_ref,
    out_ref, new_ref, received_out_ref, cot_out_ref, rows_ref,
):
    n, rows, _ = out_ref.shape
    width = act_ref.shape[1]
    received_out_ref[...] = received_ref[...]
    cot_out_ref[...] = cot_ref[...]
    per_dev = width // LANES // n
    first = offset_ref[0] == 0
    down, up = powers(expo_ref[...], -1), powers(expo_ref[...], 1)
    old = [base_ref[p] for p in range(2)]
    chosen = jnp.concatenate([jnp.where(first, o[0:1], o[1:2]) for o in old], axis=0)
    delta = act_ref[...].astype(f32) - chosen
    fill = jnp.full((rows - 2 * per_dev, LANES), offset_ref[0].astype(f32))
    pieces = []
    for b in range(width // LANES):
        scaled = delta[:, b * LANES : (b + 1) * LANES] * down[:, b : b + 1]
        kept = jnp.clip(scaled, -clip_top, clip_top).astype(bf16).astype(f32) * up[:, b : b + 1]
        d, c = divmod(b, per_dev)
        rows_ref[d, 2 * c : 2 * c + 2, :] = kept
        pieces.append(kept)
    for d in range(n):
        rows_ref[d, 2 * per_dev :, :] = fill
    out_ref[...] = rows_ref[...].astype(bf16)
    new = chosen + jnp.concatenate(pieces, axis=1)
    for p in range(2):
        row = new[p : p + 1]
        new_ref[p, 0:1, :] = jnp.where(first, row, old[p][0:1])
        new_ref[p, 1:2, :] = jnp.where(first, old[p][1:2], row)


def rebuild_kernel(arrived_ref, base_ref, new_ref, out_ref, share_ref, rows_ref, slots_ref):
    n, rows, _ = arrived_ref.shape
    copies, _, width = out_ref.shape
    rows_ref[...] = arrived_ref[...].astype(f32).reshape(n * rows, LANES)
    per_dev = width // LANES
    first = rows_ref[pl.ds(2 * per_dev, n, stride=rows), :] == 0.0
    for p in range(2):
        for c in range(per_dev):
            cols = slice(c * LANES, (c + 1) * LANES)
            sent = rows_ref[pl.ds(2 * c + p, n, stride=rows), :]
            at = p * per_dev + c
            slots_ref[at] = base_ref[p, :, cols]
            even = slots_ref[at, pl.ds(0, n, stride=2), :]
            odd = slots_ref[at, pl.ds(1, n, stride=2), :]
            rebuilt = jnp.where(first, even, odd) + sent
            slots_ref[at, pl.ds(0, n, stride=2), :] = jnp.where(first, rebuilt, even)
            slots_ref[at, pl.ds(1, n, stride=2), :] = jnp.where(first, odd, rebuilt)
            new_ref[p, :, cols] = slots_ref[at]
            restored = rebuilt.astype(bf16)
            share_ref[p * n : (p + 1) * n, cols] = restored
            for k in range(copies):
                out_ref[k, p * n : (p + 1) * n, cols] = restored


def dot_nt(a, b):
    return lax.dot_general(a, b, (((1,), (1,)), ((), ())), preferred_element_type=f32)


def own_rows(piece_ref, own_ref, me, owner):
    n = piece_ref.shape[0] // 2
    for p in range(2):
        own_ref[pl.ds(p * n + owner, 1), :] = piece_ref[pl.ds(p * n + me, 1), :]


def grad_active_kernel(
    owner_of, me_ref, a_ref, b_ref, c_ref, d_ref, weight_ref, out_ref, own_ref, piece_ref
):
    i, quarter = pl.program_id(0), a_ref.shape[0]
    me = me_ref[0]

    @pl.when(i == 0)
    def _():
        out_ref[...] = jnp.zeros_like(out_ref)

    k, part = lax.rem(i, quarter), i // quarter
    low = jnp.where(part == 0, a_ref[k], b_ref[k])
    piece = jnp.where(part < 2, low, jnp.where(part == 2, c_ref[k], d_ref[k]))
    out_ref[...] += dot_nt(piece, weight_ref[...])
    piece_ref[...] = piece.astype(f32)
    own_rows(piece_ref, own_ref, me, owner_of(i, me))


def up_kernel(
    owner_of, width_all, me_ref, a_ref, b_ref, gain_ref, weight_ref, ga_ref,
    active_ref, gh_ref, own_ref, piece_ref, acc_ref, square_ref,
):
    i, half = pl.program_id(0), a_ref.shape[0]
    me = me_ref[0]

    @pl.when(i == 0)
    def _():
        acc_ref[...] = jnp.zeros_like(acc_ref)
        square_ref[...] = jnp.zeros_like(square_ref)

    k = lax.rem(i, half)
    piece = jnp.where(i < half, a_ref[k], b_ref[k]).astype(f32)
    piece_ref[...] = piece
    own_rows(piece_ref, own_ref, me, owner_of(i, me))
    squares = piece * piece
    for c in range(piece.shape[1] // LANES):
        square_ref[...] += squares[:, c * LANES : (c + 1) * LANES]
    scaled = (piece * gain_ref[0]).astype(bf16)
    acc_ref[...] += jnp.dot(scaled, weight_ref[...], preferred_element_type=f32)

    @pl.when(i == pl.num_programs(0) - 1)
    def _():
        total = jnp.sum(square_ref[...], axis=1, keepdims=True)
        hidden = lax.rsqrt(total / width_all + eps) * acc_ref[...]
        sigma = jax.nn.sigmoid(hidden)
        active_ref[...] = (hidden * sigma).astype(bf16)
        gh_ref[...] = (ga_ref[...] * sigma * (1.0 + hidden * (1.0 - sigma))).astype(bf16)


def down_kernel(me_ref, active_ref, weight_ref, out_ref):
    out_ref[0] = jnp.dot(active_ref[...], weight_ref[...], preferred_element_type=f32).astype(bf16)


def grad_norm_kernel(me_ref, gh_ref, weight_ref, send_ref, keep_ref, rows_ref):
    i = pl.program_id(0)
    half, tokens, width = send_ref.shape
    n = 2 * half
    terms = dot_nt(gh_ref[...], weight_ref[...])
    per_step = terms.shape[1] // width
    chunks = width // LANES
    for j in range(per_step):
        share = i * per_step + j
        for p in range(2):
            for c in range(chunks):
                at = j * width + c * LANES
                rows_ref[c, pl.ds(p * n + share, n, stride=tokens), :] = terms[
                    p * n : (p + 1) * n, at : at + LANES
                ]

    @pl.when(i == pl.num_programs(0) - 1)
    def _():
        core = lax.rem(me_ref[0], 2)
        for k in range(half):
            keep_at = pl.multiple_of((2 * k + core) * tokens, tokens)
            send_at = pl.multiple_of((2 * k + 1 - core) * tokens, tokens)
            for c in range(chunks):
                cols = slice(c * LANES, (c + 1) * LANES)
                keep_ref[k, :, cols] = rows_ref[c, pl.ds(keep_at, tokens), :].astype(bf16)
                send_ref[k, :, cols] = rows_ref[c, pl.ds(send_at, tokens), :].astype(bf16)


def pair_kernel(me_ref, kept_ref, arrived_ref, send_ref, keep_ref):
    quarter = send_ref.shape[0]
    row = lax.rem(me_ref[0] // 2, 2)
    for k in range(quarter):
        for out_ref, at in ((send_ref, 2 * k + 1 - row), (keep_ref, 2 * k + row)):
            out_ref[k] = (kept_ref[at].astype(f32) + arrived_ref[at].astype(f32)).astype(bf16)


def line_kernel(me_ref, kept_ref, arrived_ref, *out_refs):
    quarter = len(out_refs)
    for r, out_ref in enumerate(out_refs):
        at = lax.rem(me_ref[0] // 4 + r, quarter)
        out_ref[...] = (kept_ref[at].astype(f32) + arrived_ref[at].astype(f32)).astype(bf16)


def layer_kernel(restored_ref, *refs):
    total = restored_ref[...].astype(f32)
    for ref in refs[:-1]:
        total = total + ref[...].astype(f32)
    refs[-1][...] = total.astype(bf16)


def final_kernel(width_all, own_ref, cot_ref, gain_ref, expo_ref, *refs):
    grad_ref = refs[-1]
    grad = refs[0][...].astype(f32)
    for ref in refs[1:-1]:
        grad = grad + ref[...].astype(f32)
    n, width = gain_ref.shape
    down, up = powers(expo_ref[...], -1), powers(expo_ref[...], 1)
    gain = gain_ref[...]
    per_dev = width // LANES
    blocks = n * per_dev
    at_row = lax.broadcasted_iota(jnp.int32, (n, blocks), 0)
    at_lane = lax.broadcasted_iota(jnp.int32, (n, blocks), 1)
    for p in range(2):
        rows = slice(p * n, (p + 1) * n)
        own, norm = own_ref[rows, :], grad[rows, :]
        inv_rms = lax.rsqrt(jnp.sum(own * own, keepdims=True) / width_all + eps)
        scaled_in = (own * gain).astype(bf16).astype(f32)
        curvature = inv_rms * jnp.sum(scaled_in * norm, keepdims=True)
        correction = curvature * inv_rms * inv_rms / width_all
        value = cot_ref[rows, :] + inv_rms * gain * norm - correction * own
        for c in range(per_dev):
            at = at_lane == at_row * per_dev + c
            shrink = jnp.sum(jnp.where(at, down[p : p + 1], 0.0), axis=1, keepdims=True)
            grow = jnp.sum(jnp.where(at, up[p : p + 1], 0.0), axis=1, keepdims=True)
            scaled = value[:, c * LANES : (c + 1) * LANES] * shrink
            kept = jnp.clip(scaled, -clip_top, clip_top).astype(bf16).astype(f32) * grow
            grad_ref[p, pl.ds(c, n, stride=per_dev), :] = kept


def on_device(
    activations,
    sample_ids,
    forward_exponent,
    sender_base,
    receiver_base,
    norm_gain,
    up_weight,
    down_weight,
    cotangent,
    backward_exponent,
    *,
    n,
):
    half, quarter = n // 2, n // 4
    tokens = 2 * n
    width_all, hidden_dev = up_weight.shape
    width = width_all // n
    me = lax.axis_index("dp").astype(jnp.int32)
    me_in = me.reshape(1)
    core_pair = [(d, d ^ 1) for d in range(n)]
    row_pair = [(d, d ^ 2) for d in range(n)]
    same_core = [[2 * k + c for k in range(half)] for c in range(2)]

    def cot_owner(i, who):
        core, row, along = lax.rem(who, 2), lax.rem(who // 2, 2), who // 4
        other_core, other_row, back = i // half, lax.rem(i // quarter, 2), lax.rem(i, quarter)
        at = lax.rem(along - back + quarter, quarter)
        return 4 * at + 2 * lax.rem(row + other_row, 2) + lax.rem(core + other_core, 2)

    def token_owner(i, who):
        return 2 * lax.rem(i, half) + lax.rem(who + i // half, 2)

    slots = sender_base.shape[1]
    offset = sample_ids - slots * me
    rows = -(-(2 * width // LANES + 1) // 16) * 16
    once = lambda *shape: pl.BlockSpec(shape, lambda i: (0,) * len(shape))
    share_shape = (tokens, width)
    act_shape, expo_shape = (2, width_all), (2, width_all // LANES)
    blocks, new_sender_base, received, cot = pl.pallas_call(
        send_kernel,
        out_shape=(
            jax.ShapeDtypeStruct((n, rows, LANES), bf16),
            jax.ShapeDtypeStruct(sender_base.shape, f32),
            jax.ShapeDtypeStruct(receiver_base.shape, f32),
            jax.ShapeDtypeStruct(share_shape, bf16),
        ),
        grid=(1,),
        in_specs=[
            SMEM,
            once(*act_shape),
            once(*expo_shape),
            once(*sender_base.shape),
            once(*receiver_base.shape),
            once(*share_shape),
        ],
        out_specs=(
            once(n, rows, LANES),
            once(*sender_base.shape),
            once(*receiver_base.shape),
            once(*share_shape),
        ),
        scratch_shapes=[pltpu.VMEM((n, rows, LANES), f32)],
        compiler_params=params(16),
    )(
        offset,
        hbm(activations.reshape(act_shape)),
        hbm(forward_exponent.reshape(expo_shape)),
        hbm(sender_base),
        hbm(receiver_base),
        hbm(cotangent.reshape(share_shape)),
    )
    arrived = lax.all_to_all(blocks, "dp", split_axis=0, concat_axis=0, tiled=True)

    cot = cot.reshape(1, tokens, width)
    line = [cot]
    for r in range(1, quarter):
        line.append(lax.ppermute(cot, "dp", [(d, (d + 4 * r) % n) for d in range(n)]))
    line = jnp.concatenate(line, axis=0)
    rows_both = [line, lax.ppermute(line, "dp", row_pair)]
    cots = rows_both + [lax.ppermute(x, "dp", core_pair) for x in rows_both]

    new_receiver_base, restored, share = pl.pallas_call(
        rebuild_kernel,
        out_shape=(
            jax.ShapeDtypeStruct(receiver_base.shape, f32),
            jax.ShapeDtypeStruct((half, tokens, width), bf16),
            jax.ShapeDtypeStruct((tokens, width), bf16),
        ),
        in_specs=[VMEM, VMEM],
        out_specs=(VMEM, VMEM, VMEM),
        scratch_shapes=[
            pltpu.VMEM((n * rows, LANES), f32),
            pltpu.VMEM((2 * width // LANES, 2 * n, LANES), f32),
        ],
        compiler_params=params(16),
    )(arrived, received)
    rest_a = lax.all_to_all(
        restored, "dp", split_axis=0, concat_axis=0, axis_index_groups=same_core, tiled=True
    )

    whole = lambda *shape: pl.BlockSpec(shape, lambda i, who: (0,) * len(shape))
    pieces = whole(half, tokens, width)

    grad_active, own_cot = pl.pallas_call(
        functools.partial(grad_active_kernel, cot_owner),
        out_shape=(
            jax.ShapeDtypeStruct((tokens, hidden_dev), f32),
            jax.ShapeDtypeStruct((tokens, width), f32),
        ),
        grid_spec=pltpu.PrefetchScalarGridSpec(
            num_scalar_prefetch=1,
            grid=(n,),
            in_specs=[
                *([whole(quarter, tokens, width)] * 4),
                pl.BlockSpec((hidden_dev, width), lambda i, who: (0, cot_owner(i, who[0]))),
            ],
            out_specs=(whole(tokens, hidden_dev), whole(tokens, width)),
            scratch_shapes=[pltpu.VMEM((tokens, width), f32)],
        ),
        compiler_params=params(24),
        cost_estimate=pl.CostEstimate(
            flops=2 * tokens * width_all * hidden_dev,
            bytes_accessed=2 * width_all * hidden_dev,
            transcendentals=0,
        ),
    )(me_in, *cots, hbm(down_weight))
    rest_a, grad_active = lax.optimization_barrier((rest_a, grad_active))
    rest_b = lax.ppermute(rest_a, "dp", core_pair)

    active, grad_hidden, own_restored = pl.pallas_call(
        functools.partial(up_kernel, token_owner, width_all),
        out_shape=(
            jax.ShapeDtypeStruct((tokens, hidden_dev), bf16),
            jax.ShapeDtypeStruct((tokens, hidden_dev), bf16),
            jax.ShapeDtypeStruct((tokens, width), f32),
        ),
        grid_spec=pltpu.PrefetchScalarGridSpec(
            num_scalar_prefetch=1,
            grid=(n,),
            in_specs=[
                pieces,
                pieces,
                pl.BlockSpec((1, 1, width), lambda i, who: (token_owner(i, who[0]), 0, 0)),
                pl.BlockSpec((width, hidden_dev), lambda i, who: (token_owner(i, who[0]), 0)),
                whole(tokens, hidden_dev),
            ],
            out_specs=(whole(tokens, hidden_dev), whole(tokens, hidden_dev), whole(tokens, width)),
            scratch_shapes=[
                pltpu.VMEM((tokens, width), f32),
                pltpu.VMEM((tokens, hidden_dev), f32),
                pltpu.VMEM((tokens, LANES), f32),
            ],
        ),
        compiler_params=params(24),
        cost_estimate=pl.CostEstimate(
            flops=2 * tokens * width_all * hidden_dev,
            bytes_accessed=2 * width_all * hidden_dev,
            transcendentals=0,
        ),
    )(me_in, rest_a, rest_b, norm_gain.reshape(n, 1, width), hbm(up_weight), grad_active)

    step = max(width, 1024)
    grad_send, grad_keep = pl.pallas_call(
        grad_norm_kernel,
        out_shape=(jax.ShapeDtypeStruct((half, tokens, width), bf16),) * 2,
        grid_spec=pltpu.PrefetchScalarGridSpec(
            num_scalar_prefetch=1,
            grid=(width_all // step,),
            in_specs=[
                whole(tokens, hidden_dev),
                pl.BlockSpec((step, hidden_dev), lambda i, who: (i, 0)),
            ],
            out_specs=(pieces, pieces),
            scratch_shapes=[pltpu.VMEM((width // LANES, n * tokens, LANES), f32)],
        ),
        compiler_params=params(24),
        cost_estimate=pl.CostEstimate(
            flops=2 * tokens * width_all * hidden_dev,
            bytes_accessed=2 * width_all * hidden_dev,
            transcendentals=0,
        ),
    )(me_in, grad_hidden, hbm(up_weight))

    def down_terms(other):
        return pl.pallas_call(
            down_kernel,
            out_shape=jax.ShapeDtypeStruct((half, tokens, width), bf16),
            grid_spec=pltpu.PrefetchScalarGridSpec(
                num_scalar_prefetch=1,
                grid=(half,),
                in_specs=[
                    whole(tokens, hidden_dev),
                    pl.BlockSpec(
                        (hidden_dev, width),
                        lambda i, who: (0, 2 * i + lax.rem(who[0] + other, 2)),
                    ),
                ],
                out_specs=pl.BlockSpec((1, tokens, width), lambda i, who: (i, 0, 0)),
            ),
            compiler_params=params(24),
            cost_estimate=pl.CostEstimate(
                flops=tokens * width_all * hidden_dev,
                bytes_accessed=width_all * hidden_dev,
                transcendentals=0,
            ),
        )(me_in, active, hbm(down_weight))

    def pair_sum(kept, arrived):
        send, keep = pl.pallas_call(
            pair_kernel,
            out_shape=(jax.ShapeDtypeStruct((quarter, tokens, width), bf16),) * 2,
            in_specs=[SMEM, VMEM, VMEM],
            out_specs=(VMEM, VMEM),
            compiler_params=params(16),
        )(me_in, kept, arrived)
        return keep, lax.ppermute(send, "dp", row_pair)

    def line_sum(kept, arrived):
        shares = pl.pallas_call(
            line_kernel,
            out_shape=(jax.ShapeDtypeStruct((tokens, width), bf16),) * quarter,
            in_specs=[SMEM, VMEM, VMEM],
            out_specs=(VMEM,) * quarter,
            compiler_params=params(16),
        )(me_in, kept, arrived)
        moved = [
            lax.ppermute(shares[r], "dp", [(d, (d + 4 * r) % n) for d in range(n)])
            for r in range(1, quarter)
        ]
        return [shares[0], *moved]

    grad_in = lax.ppermute(grad_send, "dp", core_pair)
    out_in = lax.ppermute(down_terms(1), "dp", core_pair)
    grad_pair = pair_sum(grad_keep, grad_in)
    out_pair = pair_sum(down_terms(0), out_in)
    grad_line = line_sum(*grad_pair)
    out_line = line_sum(*out_pair)
    returned = pl.pallas_call(
        functools.partial(final_kernel, width_all),
        out_shape=jax.ShapeDtypeStruct((2, width_all // LANES, LANES), f32),
        in_specs=[VMEM] * (4 + quarter),
        out_specs=VMEM,
        compiler_params=params(16),
    )(
        own_restored,
        own_cot,
        norm_gain.reshape(n, width),
        backward_exponent.reshape(2, -1),
        *grad_line,
    )
    layer_out = pl.pallas_call(
        layer_kernel,
        out_shape=jax.ShapeDtypeStruct((tokens, width), bf16),
        in_specs=[VMEM] * (1 + quarter),
        out_specs=VMEM,
        compiler_params=params(16),
    )(share, *out_line)
    return (
        new_sender_base,
        new_receiver_base,
        layer_out.reshape(2, n, width),
        returned.reshape(2, 1, width_all),
    )


def solution(mesh):
    placed = (
        P(None, ("groups", "dp"), None),
        P(("groups", "dp")),
        P(None, ("groups", "dp"), None),
        P(None, ("groups", "dp"), None),
        P(None, "groups", "dp"),
        P(),
        P(None, "dp"),
        P("dp", None),
        P(None, "groups", "dp"),
        P(None, ("groups", "dp"), None),
    )
    return jax.shard_map(
        functools.partial(on_device, n=mesh.shape["dp"]),
        mesh=mesh,
        in_specs=placed,
        out_specs=(
            P(None, ("groups", "dp"), None),
            P(None, "groups", "dp"),
            P(None, "groups", "dp"),
            P(None, ("groups", "dp"), None),
        ),
        check_vma=False,
    )
```

```python
import functools

import jax
import jax.numpy as jnp
from jax import lax
from jax.experimental import pallas as pl
from jax.experimental.pallas import tpu as pltpu
from jax.sharding import PartitionSpec as P

clip_top = 448.0
eps = 1e-05
LANES = 128
f32 = jnp.float32
bf16 = jnp.bfloat16
VMEM = pl.BlockSpec(memory_space=pltpu.VMEM)
SMEM = pl.BlockSpec(memory_space=pltpu.SMEM)


def hbm(x):
    return pltpu.with_memory_space_constraint(x, pltpu.HBM)


def powers(exponent, sign):
    total = jnp.zeros(exponent.shape, f32)
    for level in range(-10, 1):
        total = jnp.where(exponent == level, f32(2.0 ** (sign * level)), total)
    return total


def params(megabytes):
    return pltpu.CompilerParams(vmem_limit_bytes=megabytes << 20)


def flip(bit, by):
    return lax.rem(bit + by, 2)


def place(me):
    return me // 4, lax.rem(me // 2, 2), lax.rem(me, 2)


def owner_of(me, n, part, back):
    along, row, core = place(me)
    at = lax.rem(along - back + n // 4, n // 4)
    return 4 * at + 2 * flip(row, part % 2) + flip(core, part // 2)


def block_spot(q, tokens, rows, width):
    per_column = tokens // rows
    r, c = rows * (q % per_column), width + LANES * (q // per_column)
    return slice(r, r + rows), slice(c, c + LANES)


def send_kernel(
    me_ref, offset_ref, act_ref, expo_ref, base_ref, received_ref, cot_ref, gain_ref,
    new_ref, received_out_ref, gain_out_ref, *refs,
):
    *packed_refs, rows_ref = refs
    n, rows, _ = rows_ref.shape
    tokens, share = cot_ref.shape
    width = act_ref.shape[1]
    per_dev = width // LANES // n
    received_out_ref[...] = received_ref[...]
    for j in range(n):
        gain_out_ref[j : j + 1, :] = gain_ref[:, j * share : (j + 1) * share]
    first = offset_ref[0] == 0
    down, up = powers(expo_ref[...], -1), powers(expo_ref[...], 1)
    old = [base_ref[p] for p in range(2)]
    chosen = jnp.concatenate([jnp.where(first, o[0:1], o[1:2]) for o in old], axis=0)
    delta = act_ref[...].astype(f32) - chosen
    fill = jnp.full((rows - 2 * per_dev, LANES), offset_ref[0].astype(f32))
    pieces = []
    for b in range(width // LANES):
        scaled = delta[:, b * LANES : (b + 1) * LANES] * down[:, b : b + 1]
        kept = jnp.clip(scaled, -clip_top, clip_top).astype(bf16).astype(f32) * up[:, b : b + 1]
        d, c = divmod(b, per_dev)
        rows_ref[d, 2 * c : 2 * c + 2, :] = kept
        pieces.append(kept)
    for d in range(n):
        rows_ref[d, 2 * per_dev :, :] = fill
    along, _, _ = place(me_ref[0])
    cot = cot_ref[...]
    for r, packed_ref in enumerate(packed_refs):
        to = lax.rem(along + r, n // 4)
        packed_ref[:, :share] = cot
        for q in range(4):
            packed_ref[block_spot(q, tokens, rows, share)] = rows_ref[4 * to + q].astype(bf16)
    new = chosen + jnp.concatenate(pieces, axis=1)
    for p in range(2):
        row = new[p : p + 1]
        new_ref[p, 0:1, :] = jnp.where(first, row, old[p][0:1])
        new_ref[p, 1:2, :] = jnp.where(first, old[p][1:2], row)


def sort_kernel(me_ref, *refs):
    *packed_refs, line_ref, b0, b1, b2, b3 = refs
    quarter, tokens, share = line_ref.shape
    rows = b0.shape[1]
    _, row, core = place(me_ref[0])
    for r, packed_ref in enumerate(packed_refs):
        line_ref[r] = packed_ref[:, :share]
        block = [packed_ref[block_spot(q, tokens, rows, share)] for q in range(4)]
        for e, out_ref in enumerate((b0, b1, b2, b3)):
            to_row, to_core = flip(row, e // 2), flip(core, e % 2)
            low = jnp.where(to_core == 0, block[0], block[1])
            high = jnp.where(to_core == 0, block[2], block[3])
            out_ref[r] = jnp.where(to_row == 0, low, high)


def rebuild_kernel(me_ref, b0, b1, b2, b3, base_ref, new_ref, share_ref, rows_ref, slots_ref):
    quarter, rows, _ = b0.shape
    n, width = 4 * quarter, share_ref.shape[1]
    for e, block_ref in enumerate((b0, b1, b2, b3)):
        for r in range(quarter):
            sender = owner_of(me_ref[0], n, 2 * (e % 2) + e // 2, r)
            rows_ref[pl.ds(pl.multiple_of(sender * rows, rows), rows), :] = block_ref[r].astype(f32)
    per_dev = width // LANES
    first = rows_ref[pl.ds(2 * per_dev, n, stride=rows), :] == 0.0
    for p in range(2):
        for c in range(per_dev):
            cols = slice(c * LANES, (c + 1) * LANES)
            sent = rows_ref[pl.ds(2 * c + p, n, stride=rows), :]
            at = p * per_dev + c
            slots_ref[at] = base_ref[p, :, cols]
            even = slots_ref[at, pl.ds(0, n, stride=2), :]
            odd = slots_ref[at, pl.ds(1, n, stride=2), :]
            rebuilt = jnp.where(first, even, odd) + sent
            slots_ref[at, pl.ds(0, n, stride=2), :] = jnp.where(first, rebuilt, even)
            slots_ref[at, pl.ds(1, n, stride=2), :] = jnp.where(first, odd, rebuilt)
            new_ref[p, :, cols] = slots_ref[at]
            restored = rebuilt.astype(bf16)
            share_ref[p * n : (p + 1) * n, cols] = restored


def dot_nt(a, b):
    return lax.dot_general(a, b, (((1,), (1,)), ((), ())), preferred_element_type=f32)


def own_rows(piece_ref, own_ref, me, owner):
    n = piece_ref.shape[0] // 2
    for p in range(2):
        own_ref[pl.ds(p * n + owner, 1), :] = piece_ref[pl.ds(p * n + me, 1), :]


def grad_active_kernel(first, me_ref, a_ref, b_ref, weight_ref, acc_in_ref, own_in_ref, acc_ref, own_ref, piece_ref):
    quarter, _, width = a_ref.shape
    me = me_ref[0]
    acc_ref[...] = acc_in_ref[...]
    own_ref[...] = own_in_ref[...]
    for part, cot_ref in enumerate((a_ref, b_ref)):

        @pl.loop(0, quarter)
        def _(k):
            owner = owner_of(me, 4 * quarter, first + part, k)
            piece = cot_ref[k]
            columns = pl.ds(pl.multiple_of(owner * width, width), width)
            acc_ref[...] += dot_nt(weight_ref[:, columns], piece)
            piece_ref[...] = piece.astype(f32)
            own_rows(piece_ref, own_ref, me, owner)


def up_kernel(
    first, me_ref, a_ref, b_ref, gain_ref, weight_ref, acc_in_ref, square_in_ref, own_in_ref, *refs
):
    if first == 0:
        acc_ref, square_ref, own_ref, piece_ref = refs
    else:
        ga_ref, active_ref, gh_ref, own_ref, piece_ref, acc_ref, square_ref = refs
    quarter, _, width = a_ref.shape
    width_all = weight_ref.shape[0]
    me = me_ref[0]
    acc_ref[...] = acc_in_ref[...]
    square_ref[...] = square_in_ref[...]
    own_ref[...] = own_in_ref[...]
    for part, rest_ref in enumerate((a_ref, b_ref)):

        @pl.loop(0, quarter)
        def _(k):
            owner = owner_of(me, 4 * quarter, first + part, k)
            piece = rest_ref[k].astype(f32)
            piece_ref[...] = piece
            own_rows(piece_ref, own_ref, me, owner)
            squares = piece * piece
            total = square_ref[...]
            for c in range(width // LANES):
                total = total + squares[:, c * LANES : (c + 1) * LANES]
            square_ref[...] = total
            scaled = (piece * gain_ref[pl.ds(owner, 1), :]).astype(bf16)
            rows = pl.ds(pl.multiple_of(owner * width, width), width)
            acc_ref[...] += jnp.dot(scaled, weight_ref[rows, :], preferred_element_type=f32)

    if first == 0:
        return
    total = jnp.sum(square_ref[...], axis=1, keepdims=True)
    hidden = lax.rsqrt(total / width_all + eps) * acc_ref[...]
    sigma = jax.nn.sigmoid(hidden)
    active_ref[...] = (hidden * sigma).astype(bf16)
    grad_active = ga_ref[...].T
    gh_ref[...] = (grad_active * sigma * (1.0 + hidden * (1.0 - sigma))).astype(bf16)


def down_kernel(other, me_ref, active_ref, weight_ref, after_ref, out_ref):
    half, _, width = out_ref.shape
    core = lax.rem(me_ref[0] + other, 2)

    @pl.loop(0, half)
    def _(k):
        columns = pl.ds(pl.multiple_of((2 * k + core) * width, width), width)
        terms = jnp.dot(active_ref[...], weight_ref[:, columns], preferred_element_type=f32)
        out_ref[k] = terms.astype(bf16)


def grad_norm_kernel(me_ref, gh_ref, weight_ref, send_ref, keep_ref, rows_ref):
    half, tokens, width = send_ref.shape
    n, chunks = 2 * half, width // LANES

    @pl.loop(0, n)
    def _(share):
        block = weight_ref[pl.ds(pl.multiple_of(share * width, width), width), :]
        terms = dot_nt(gh_ref[...], block)
        for p in range(2):
            for c in range(chunks):
                rows_ref[c, pl.ds(p * n + share, n, stride=tokens), :] = terms[
                    p * n : (p + 1) * n, c * LANES : (c + 1) * LANES
                ]

    core = lax.rem(me_ref[0], 2)
    for k in range(half):
        keep_at = pl.multiple_of((2 * k + core) * tokens, tokens)
        send_at = pl.multiple_of((2 * k + 1 - core) * tokens, tokens)
        for c in range(chunks):
            cols = slice(c * LANES, (c + 1) * LANES)
            keep_ref[k, :, cols] = rows_ref[c, pl.ds(keep_at, tokens), :].astype(bf16)
            send_ref[k, :, cols] = rows_ref[c, pl.ds(send_at, tokens), :].astype(bf16)


def pair_kernel(me_ref, kept_ref, arrived_ref, send_ref, keep_ref):
    quarter = send_ref.shape[0]
    row = lax.rem(me_ref[0] // 2, 2)
    for k in range(quarter):
        for out_ref, at in ((send_ref, 2 * k + 1 - row), (keep_ref, 2 * k + row)):
            out_ref[k] = (kept_ref[at].astype(f32) + arrived_ref[at].astype(f32)).astype(bf16)


def line_kernel(me_ref, grad_ref, grad_in_ref, out_ref, out_in_ref, *refs):
    quarter = len(refs)
    for r, ref in enumerate(refs):
        at = lax.rem(me_ref[0] // 4 + r, quarter)
        ref[0] = (grad_ref[at].astype(f32) + grad_in_ref[at].astype(f32)).astype(bf16)
        ref[1] = (out_ref[at].astype(f32) + out_in_ref[at].astype(f32)).astype(bf16)


def final_kernel(width_all, share_ref, own_ref, cot_ref, gain_ref, expo_ref, *refs):
    *refs, layer_ref, grad_ref = refs
    grad = refs[0][0].astype(f32)
    layer = refs[0][1].astype(f32)
    for ref in refs[1:]:
        grad = grad + ref[0].astype(f32)
        layer = layer + ref[1].astype(f32)
    layer_ref[...] = (share_ref[...].astype(f32) + layer).astype(bf16)
    n, width = gain_ref.shape
    down, up = powers(expo_ref[...], -1), powers(expo_ref[...], 1)
    gain = gain_ref[...]
    per_dev = width // LANES
    blocks = n * per_dev
    at_row = lax.broadcasted_iota(jnp.int32, (n, blocks), 0)
    at_lane = lax.broadcasted_iota(jnp.int32, (n, blocks), 1)
    for p in range(2):
        rows = slice(p * n, (p + 1) * n)
        own, norm = own_ref[rows, :], grad[rows, :]
        inv_rms = lax.rsqrt(jnp.sum(own * own, keepdims=True) / width_all + eps)
        scaled_in = (own * gain).astype(bf16).astype(f32)
        curvature = inv_rms * jnp.sum(scaled_in * norm, keepdims=True)
        correction = curvature * inv_rms * inv_rms / width_all
        value = cot_ref[rows, :].astype(f32) + inv_rms * gain * norm - correction * own
        for c in range(per_dev):
            at = at_lane == at_row * per_dev + c
            shrink = jnp.sum(jnp.where(at, down[p : p + 1], 0.0), axis=1, keepdims=True)
            grow = jnp.sum(jnp.where(at, up[p : p + 1], 0.0), axis=1, keepdims=True)
            scaled = value[:, c * LANES : (c + 1) * LANES] * shrink
            kept = jnp.clip(scaled, -clip_top, clip_top).astype(bf16).astype(f32) * grow
            grad_ref[p, pl.ds(c, n, stride=per_dev), :] = kept


def on_device(
    activations,
    sample_ids,
    forward_exponent,
    sender_base,
    receiver_base,
    norm_gain,
    up_weight,
    down_weight,
    cotangent,
    backward_exponent,
    *,
    n,
):
    half, quarter = n // 2, n // 4
    tokens = 2 * n
    width_all, hidden_dev = up_weight.shape
    width = width_all // n
    me = lax.axis_index("dp").astype(jnp.int32)
    me_in = me.reshape(1)

    def shift(x, r):
        return lax.ppermute(x, "dp", [(d, (d + 4 * r) % n) for d in range(n)]) if r else x

    def swap(x, bits):
        return lax.ppermute(x, "dp", [(d, d ^ bits) for d in range(n)])

    struct = jax.ShapeDtypeStruct
    share_shape, hidden_shape = (tokens, width), (tokens, hidden_dev)
    line_shape = (quarter, tokens, width)

    def call(kernel, outs, ins, args, scratch=(), cost=0):
        return pl.pallas_call(
            kernel,
            out_shape=outs,
            in_specs=ins,
            out_specs=jax.tree.map(lambda _: VMEM, outs),
            scratch_shapes=list(scratch),
            compiler_params=params(8),
            cost_estimate=pl.CostEstimate(
                flops=cost * tokens * width_all * hidden_dev,
                bytes_accessed=cost * width_all * hidden_dev,
                transcendentals=0,
            ),
        )(*args)

    offset = sample_ids - sender_base.shape[1] * me
    rows = -(-(2 * width // LANES + 1) // 16) * 16
    packed_shape = (tokens, width + LANES * -(-4 * rows // tokens))
    act_shape, expo_shape = (2, width_all), (2, width_all // LANES)
    once = lambda shape: pl.BlockSpec(shape, lambda i: (0,) * len(shape))
    in_shapes = [act_shape, expo_shape, sender_base.shape, receiver_base.shape, share_shape, (1, width_all)]
    outs = (
        struct(sender_base.shape, f32),
        struct(receiver_base.shape, f32),
        struct((n, width), f32),
    ) + (struct(packed_shape, bf16),) * quarter
    new_sender_base, received, gain, *packed = pl.pallas_call(
        send_kernel,
        out_shape=outs,
        grid=(1,),
        in_specs=[SMEM, SMEM] + [once(x) for x in in_shapes],
        out_specs=tuple(once(x.shape) for x in outs),
        scratch_shapes=[pltpu.VMEM((n, rows, LANES), f32)],
        compiler_params=params(8),
    )(
        me_in,
        offset,
        hbm(activations.reshape(act_shape)),
        hbm(forward_exponent.reshape(expo_shape)),
        hbm(sender_base),
        hbm(receiver_base),
        hbm(cotangent.reshape(share_shape)),
        hbm(norm_gain.reshape(1, width_all)),
    )
    packed = [shift(x, r) for r, x in enumerate(packed)]
    cot_line, *blocks = call(
        sort_kernel,
        (struct(line_shape, bf16),) + (struct((quarter, rows, LANES), bf16),) * 4,
        [SMEM] + [VMEM] * quarter,
        [me_in, *packed],
    )
    blocks = [blocks[0]] + [swap(blocks[e], e) for e in range(1, 4)]
    cot_row = swap(cot_line, 2)
    cots = [cot_line, cot_row, swap(cot_line, 1), swap(cot_row, 1)]

    new_receiver_base, share = call(
        rebuild_kernel,
        (struct(receiver_base.shape, f32), struct(share_shape, bf16)),
        [SMEM] + [VMEM] * 5,
        [me_in, *blocks, received],
        [pltpu.VMEM((n * rows, LANES), f32), pltpu.VMEM((2 * width // LANES, 2 * n, LANES), f32)],
    )
    rest_line = jnp.stack([shift(share, r) for r in range(quarter)])
    rest_row = swap(rest_line, 2)
    rests = [rest_line, rest_row, swap(rest_line, 1), swap(rest_row, 1)]

    ga, own_cot = jnp.zeros((hidden_dev, tokens), f32), jnp.zeros(share_shape, f32)
    acc, square, own = jnp.zeros(hidden_shape, f32), jnp.zeros((tokens, LANES), f32), own_cot
    for first in (0, 2):
        ga, own_cot = call(
            functools.partial(grad_active_kernel, first),
            (struct((hidden_dev, tokens), f32), struct(share_shape, f32)),
            [SMEM] + [VMEM] * 5,
            [me_in, cots[first], cots[first + 1], down_weight, ga, own_cot],
            [pltpu.VMEM(share_shape, f32)],
            cost=1,
        )
    sums = (struct(hidden_shape, f32), struct((tokens, LANES), f32))
    acc, square, own = call(
        functools.partial(up_kernel, 0),
        sums + (struct(share_shape, f32),),
        [SMEM] + [VMEM] * 7,
        [me_in, rests[0], rests[1], gain, up_weight, acc, square, own],
        [pltpu.VMEM(share_shape, f32)],
        cost=1,
    )
    active, grad_hidden, own = call(
        functools.partial(up_kernel, 2),
        (struct(hidden_shape, bf16), struct(hidden_shape, bf16), struct(share_shape, f32)),
        [SMEM] + [VMEM] * 8,
        [me_in, rests[2], rests[3], gain, up_weight, acc, square, own, ga],
        [pltpu.VMEM(share_shape, f32)] + [pltpu.VMEM(x.shape, x.dtype) for x in sums],
        cost=1,
    )

    half_out = struct((half, tokens, width), bf16)
    grad_send, grad_keep = call(
        grad_norm_kernel,
        (half_out, half_out),
        [SMEM] + [VMEM] * 2,
        [me_in, grad_hidden, up_weight],
        [pltpu.VMEM((width // LANES, n * tokens, LANES), f32)],
        cost=2,
    )

    def down_terms(other, after):
        return call(
            functools.partial(down_kernel, other),
            half_out,
            [SMEM] + [VMEM] * 2 + [pl.BlockSpec(memory_space=pl.ANY)],
            [me_in, active, down_weight, after],
            cost=1,
        )

    def pair_sum(kept, arrived):
        pair_out = struct(line_shape, bf16)
        return call(
            pair_kernel, (pair_out, pair_out), [SMEM] + [VMEM] * 2, [me_in, kept, arrived]
        )

    grad_in = swap(grad_send, 1)
    out_in = swap(down_terms(1, grad_send), 1)
    grad_send, grad_row = pair_sum(grad_keep, grad_in)
    grad_row_in = swap(grad_send, 2)
    out_send, out_row = pair_sum(down_terms(0, grad_send), out_in)
    out_row_in = swap(out_send, 2)
    shares = call(
        line_kernel,
        (struct((2, tokens, width), bf16),) * quarter,
        [SMEM] + [VMEM] * 4,
        [me_in, grad_row, grad_row_in, out_row, out_row_in],
    )
    moved = [shift(x, r) for r, x in enumerate(shares)]
    layer_out, returned = call(
        functools.partial(final_kernel, width_all),
        (struct(share_shape, bf16), struct((2, width_all // LANES, LANES), f32)),
        [VMEM] * (5 + quarter),
        [share, own, own_cot, gain, backward_exponent.reshape(expo_shape), *moved],
    )
    return (
        new_sender_base,
        new_receiver_base,
        layer_out.reshape(2, n, width),
        returned.reshape(2, 1, width_all),
    )


def solution(mesh):
    placed = (
        P(None, ("groups", "dp"), None),
        P(("groups", "dp")),
        P(None, ("groups", "dp"), None),
        P(None, ("groups", "dp"), None),
        P(None, "groups", "dp"),
        P(),
        P(None, "dp"),
        P("dp", None),
        P(None, "groups", "dp"),
        P(None, ("groups", "dp"), None),
    )
    return jax.shard_map(
        functools.partial(on_device, n=mesh.shape["dp"]),
        mesh=mesh,
        in_specs=placed,
        out_specs=(
            P(None, ("groups", "dp"), None),
            P(None, "groups", "dp"),
            P(None, "groups", "dp"),
            P(None, ("groups", "dp"), None),
        ),
        check_vma=False,
    )
```

```python
import functools

import jax
import jax.numpy as jnp
from jax import lax
from jax.experimental import pallas as pl
from jax.experimental.pallas import tpu as pltpu
from jax.sharding import PartitionSpec as P

clip_top = 448.0
eps = 1e-05
LANES = 128
f32 = jnp.float32
bf16 = jnp.bfloat16
VMEM = pl.BlockSpec(memory_space=pltpu.VMEM)
SMEM = pl.BlockSpec(memory_space=pltpu.SMEM)


def hbm(x):
    return pltpu.with_memory_space_constraint(x, pltpu.HBM)


def powers(exponent, sign):
    total = jnp.zeros(exponent.shape, f32)
    for level in range(-10, 1):
        total = jnp.where(exponent == level, f32(2.0 ** (sign * level)), total)
    return total


def params(megabytes):
    return pltpu.CompilerParams(vmem_limit_bytes=megabytes << 20)


def flip(bit, by):
    return lax.rem(bit + by, 2)


def place(me):
    return me // 4, lax.rem(me // 2, 2), lax.rem(me, 2)


def owner_of(me, n, part, back):
    along, row, core = place(me)
    at = jnp.bitwise_xor(along, back)
    return 4 * at + 2 * flip(row, part % 2) + flip(core, part // 2)


def block_spot(q, tokens, rows, width):
    per_column = tokens // rows
    r, c = rows * (q % per_column), width + LANES * (q // per_column)
    return slice(r, r + rows), slice(c, c + LANES)


def send_kernel(
    me_ref, offset_ref, act_ref, expo_ref, base_ref, received_ref, cot_ref, gain_ref,
    new_ref, received_out_ref, gain_out_ref, *refs,
):
    *packed_refs, rows_ref = refs
    n, rows, _ = rows_ref.shape
    tokens, share = cot_ref.shape
    width = act_ref.shape[1]
    per_dev = width // LANES // n
    received_out_ref[...] = received_ref[...]
    for j in range(n):
        gain_out_ref[j : j + 1, :] = gain_ref[:, j * share : (j + 1) * share]
    first = offset_ref[0] == 0
    down, up = powers(expo_ref[...], -1), powers(expo_ref[...], 1)
    old = [base_ref[p] for p in range(2)]
    chosen = jnp.concatenate([jnp.where(first, o[0:1], o[1:2]) for o in old], axis=0)
    delta = act_ref[...].astype(f32) - chosen
    fill = jnp.full((rows - 2 * per_dev, LANES), offset_ref[0].astype(f32))
    pieces = []
    for b in range(width // LANES):
        scaled = delta[:, b * LANES : (b + 1) * LANES] * down[:, b : b + 1]
        kept = jnp.clip(scaled, -clip_top, clip_top).astype(bf16).astype(f32) * up[:, b : b + 1]
        d, c = divmod(b, per_dev)
        rows_ref[d, 2 * c : 2 * c + 2, :] = kept
        pieces.append(kept)
    for d in range(n):
        rows_ref[d, 2 * per_dev :, :] = fill
    along, _, _ = place(me_ref[0])
    cot = cot_ref[...]
    for r, packed_ref in enumerate(packed_refs):
        to = jnp.bitwise_xor(along, r)
        packed_ref[:, :share] = cot
        for q in range(4):
            packed_ref[block_spot(q, tokens, rows, share)] = rows_ref[4 * to + q].astype(bf16)
    new = chosen + jnp.concatenate(pieces, axis=1)
    for p in range(2):
        row = new[p : p + 1]
        new_ref[p, 0:1, :] = jnp.where(first, row, old[p][0:1])
        new_ref[p, 1:2, :] = jnp.where(first, old[p][1:2], row)


def sort_kernel(me_ref, *refs):
    *packed_refs, line_ref, b0, b1, b2, b3 = refs
    quarter, tokens, share = line_ref.shape
    rows = b0.shape[1]
    _, row, core = place(me_ref[0])
    for r, packed_ref in enumerate(packed_refs):
        line_ref[r] = packed_ref[:, :share]
        block = [packed_ref[block_spot(q, tokens, rows, share)] for q in range(4)]
        for e, out_ref in enumerate((b0, b1, b2, b3)):
            to_row, to_core = flip(row, e // 2), flip(core, e % 2)
            low = jnp.where(to_core == 0, block[0], block[1])
            high = jnp.where(to_core == 0, block[2], block[3])
            out_ref[r] = jnp.where(to_row == 0, low, high)


def rebuild_kernel(me_ref, b0, b1, b2, b3, base_ref, new_ref, share_ref, rows_ref, slots_ref):
    quarter, rows, _ = b0.shape
    n, width = 4 * quarter, share_ref.shape[1]
    for e, block_ref in enumerate((b0, b1, b2, b3)):
        for r in range(quarter):
            sender = owner_of(me_ref[0], n, 2 * (e % 2) + e // 2, r)
            rows_ref[pl.ds(pl.multiple_of(sender * rows, rows), rows), :] = block_ref[r].astype(f32)
    per_dev = width // LANES
    first = rows_ref[pl.ds(2 * per_dev, n, stride=rows), :] == 0.0
    for p in range(2):
        for c in range(per_dev):
            cols = slice(c * LANES, (c + 1) * LANES)
            sent = rows_ref[pl.ds(2 * c + p, n, stride=rows), :]
            at = p * per_dev + c
            slots_ref[at] = base_ref[p, :, cols]
            even = slots_ref[at, pl.ds(0, n, stride=2), :]
            odd = slots_ref[at, pl.ds(1, n, stride=2), :]
            rebuilt = jnp.where(first, even, odd) + sent
            slots_ref[at, pl.ds(0, n, stride=2), :] = jnp.where(first, rebuilt, even)
            slots_ref[at, pl.ds(1, n, stride=2), :] = jnp.where(first, odd, rebuilt)
            new_ref[p, :, cols] = slots_ref[at]
            restored = rebuilt.astype(bf16)
            share_ref[p * n : (p + 1) * n, cols] = restored


def dot_nt(a, b):
    return lax.dot_general(a, b, (((1,), (1,)), ((), ())), preferred_element_type=f32)


def own_rows(piece_ref, own_ref, me, owner):
    n = piece_ref.shape[0] // 2
    for p in range(2):
        own_ref[pl.ds(p * n + owner, 1), :] = piece_ref[pl.ds(p * n + me, 1), :]


def dot_by_halves(rows, tokens):
    middle = tokens.shape[1] // 2 // LANES * LANES
    if middle == 0:
        return dot_nt(rows, tokens)
    return dot_nt(rows[:, :middle], tokens[:, :middle]) + dot_nt(rows[:, middle:], tokens[:, middle:])


def grad_active_kernel(part, me_ref, cot_ref, weight_ref, acc_ref, own_ref, held_ref, piece_ref, sems):
    quarter, _, width = cot_ref.shape
    me = me_ref[0]
    owners = [owner_of(me, 4 * quarter, part, k) for k in range(quarter)]
    copies = []
    for k, owner in enumerate(owners):
        columns = pl.ds(pl.multiple_of(owner * width, width), width)
        copies.append(pltpu.make_async_copy(weight_ref.at[:, columns], held_ref.at[k], sems.at[k]))
        copies[-1].start()
    own_ref[...] = jnp.zeros_like(own_ref)
    for k, owner in enumerate(owners):
        piece_ref[...] = cot_ref[k].astype(f32)
        own_rows(piece_ref, own_ref, me, owner)
    for k, copy in enumerate(copies):
        copy.wait()
        terms = dot_by_halves(held_ref[k], cot_ref[k])
        acc_ref[...] = terms if k == 0 else acc_ref[...] + terms


def up_part(part, me, rest_ref, gain_ref, held_ref, waits, acc_ref, square_ref, own_ref, piece_ref):
    quarter, _, width = rest_ref.shape
    own_ref[...] = jnp.zeros_like(own_ref)
    scaled = []
    for k in range(quarter):
        owner = owner_of(me, 4 * quarter, part, k)
        piece = rest_ref[k].astype(f32)
        piece_ref[...] = piece
        own_rows(piece_ref, own_ref, me, owner)
        squares = piece * piece
        total = sum(squares[:, c * LANES : (c + 1) * LANES] for c in range(width // LANES))
        square_ref[...] = total if k == 0 else square_ref[...] + total
        scaled.append((piece * gain_ref[pl.ds(owner, 1), :]).astype(bf16))
    for k in range(quarter):
        waits[k].wait()
        terms = jnp.dot(scaled[k], held_ref[k], preferred_element_type=f32)
        acc_ref[...] = terms if k == 0 else acc_ref[...] + terms


def share_copies(part, me, weight_ref, held_ref, sems, base=0):
    quarter, width, _ = held_ref.shape
    quarter = min(quarter, weight_ref.shape[0] // width // 4)
    n = 4 * quarter
    copies = []
    for k in range(quarter):
        rows = pl.ds(pl.multiple_of(owner_of(me, n, part, k) * width, width), width)
        copies.append(
            pltpu.make_async_copy(weight_ref.at[rows], held_ref.at[base + k], sems.at[base + k])
        )
        copies[-1].start()
    return copies


def up_kernel(
    part, me_ref, rest_ref, gain_ref, weight_ref,
    acc_ref, square_ref, own_ref, held_ref, piece_ref, sems,
):
    me = me_ref[0]
    copies = share_copies(part, me, weight_ref, held_ref, sems)
    up_part(part, me, rest_ref, gain_ref, held_ref, copies, acc_ref, square_ref, own_ref, piece_ref)


def middle_kernel(me_ref, rest_ref, gain_ref, weight_ref, *refs):
    ins, refs = refs[:10], refs[10:]
    active_ref, own_ref, send_ref, keep_ref, acc_ref, square_ref, piece_ref, held_ref, rows_ref, sems = refs
    quarter, tokens, width = rest_ref.shape
    half, n, chunks = 2 * quarter, 4 * quarter, width // LANES
    width_all = weight_ref.shape[0]
    me = me_ref[0]
    parts = (3, 0, 1, 2)
    copies = []
    for i, part in enumerate(parts):
        copies += share_copies(part, me, weight_ref, held_ref, sems, i * quarter)
    up_part(3, me, rest_ref, gain_ref, held_ref, copies, acc_ref, square_ref, own_ref, piece_ref)
    product = acc_ref[...] + (ins[0][...] + ins[1][...] + ins[2][...])
    squares = square_ref[...] + (ins[3][...] + ins[4][...] + ins[5][...])
    total = jnp.sum(squares, axis=1, keepdims=True)
    hidden = lax.rsqrt(total / width_all + eps) * product
    sigma = jax.nn.sigmoid(hidden)
    active_ref[...] = (hidden * sigma).astype(bf16)
    grad_active = (ins[6][...] + ins[7][...] + (ins[8][...] + ins[9][...])).T
    gh = (grad_active * sigma * (1.0 + hidden * (1.0 - sigma))).astype(bf16)
    for i, part in enumerate(parts):
        for k in range(quarter):
            at = i * quarter + k
            if i > 0:
                copies[at].wait()
            share = owner_of(me, n, part, k)
            terms = dot_by_halves(held_ref[at], gh).T
            for p in range(2):
                for c in range(chunks):
                    rows_ref[c, pl.ds(p * n + share, n, stride=tokens), :] = terms[
                        p * n : (p + 1) * n, c * LANES : (c + 1) * LANES
                    ]
    core = lax.rem(me, 2)
    for k in range(half):
        keep_at = pl.multiple_of((2 * k + core) * tokens, tokens)
        send_at = pl.multiple_of((2 * k + 1 - core) * tokens, tokens)
        for c in range(chunks):
            cols = slice(c * LANES, (c + 1) * LANES)
            keep_ref[k, :, cols] = rows_ref[c, pl.ds(keep_at, tokens), :].astype(bf16)
            send_ref[k, :, cols] = rows_ref[c, pl.ds(send_at, tokens), :].astype(bf16)


def down_kernel(other, me_ref, active_ref, weight_ref, after_ref, out_ref):
    half, _, width = out_ref.shape
    core = lax.rem(me_ref[0] + other, 2)

    def share(k):
        columns = pl.ds(pl.multiple_of((2 * k + core) * width, width), width)
        terms = jnp.dot(active_ref[...], weight_ref[:, columns], preferred_element_type=f32)
        out_ref[k] = terms.astype(bf16)

    pl.loop(0, half, unroll=4)(share)


def pair_kernel(me_ref, kept_ref, arrived_ref, *refs):
    ins, (send_ref, keep_ref), shares = (refs[:2], refs[2:4], refs[4:]) if len(refs) > 2 else ((), refs, ())
    quarter = send_ref.shape[0]
    _, row, _ = place(me_ref[0])
    for k in range(quarter):
        for out_ref, at in ((send_ref, 2 * k + 1 - row), (keep_ref, 2 * k + row)):
            out_ref[k] = (kept_ref[at].astype(f32) + arrived_ref[at].astype(f32)).astype(bf16)
    if shares:
        line_kernel(me_ref, *ins, *shares)


def line_kernel(me_ref, kept_ref, arrived_ref, *refs):
    along, _, _ = place(me_ref[0])
    for r, ref in enumerate(refs):
        at = jnp.bitwise_xor(along, r)
        ref[...] = (kept_ref[at].astype(f32) + arrived_ref[at].astype(f32)).astype(bf16)


def added(refs):
    return functools.reduce(lambda a, b: a + b, [ref[...].astype(f32) for ref in refs])


def final_kernel(width_all, share_ref, gain_ref, expo_ref, *refs):
    *refs, layer_ref, grad_ref = refs
    quarter = (len(refs) - 8) // 2
    own_all, cot_all = added(refs[:4]), added(refs[4:8])
    grad, layer = added(refs[8 : 8 + quarter]), added(refs[8 + quarter :])
    layer_ref[...] = (share_ref[...].astype(f32) + layer).astype(bf16)
    n, width = gain_ref.shape
    down, up = powers(expo_ref[...], -1), powers(expo_ref[...], 1)
    gain = gain_ref[...]
    per_dev = width // LANES
    blocks = n * per_dev
    at_row = lax.broadcasted_iota(jnp.int32, (n, blocks), 0)
    at_lane = lax.broadcasted_iota(jnp.int32, (n, blocks), 1)
    for p in range(2):
        rows = slice(p * n, (p + 1) * n)
        own, norm = own_all[rows, :], grad[rows, :]
        inv_rms = lax.rsqrt(jnp.sum(own * own, keepdims=True) / width_all + eps)
        scaled_in = (own * gain).astype(bf16).astype(f32)
        curvature = inv_rms * jnp.sum(scaled_in * norm, keepdims=True)
        correction = curvature * inv_rms * inv_rms / width_all
        value = cot_all[rows, :] + inv_rms * gain * norm - correction * own
        for c in range(per_dev):
            at = at_lane == at_row * per_dev + c
            shrink = jnp.sum(jnp.where(at, down[p : p + 1], 0.0), axis=1, keepdims=True)
            grow = jnp.sum(jnp.where(at, up[p : p + 1], 0.0), axis=1, keepdims=True)
            scaled = value[:, c * LANES : (c + 1) * LANES] * shrink
            kept = jnp.clip(scaled, -clip_top, clip_top).astype(bf16).astype(f32) * grow
            grad_ref[p, pl.ds(c, n, stride=per_dev), :] = kept


def on_device(
    activations,
    sample_ids,
    forward_exponent,
    sender_base,
    receiver_base,
    norm_gain,
    up_weight,
    down_weight,
    cotangent,
    backward_exponent,
    *,
    n,
):
    half, quarter = n // 2, n // 4
    tokens = 2 * n
    width_all, hidden_dev = up_weight.shape
    width = width_all // n
    me = lax.axis_index("dp").astype(jnp.int32)
    me_in = me.reshape(1)

    def shift(x, r):
        return lax.ppermute(x, "dp", [(d, d ^ (4 * r)) for d in range(n)]) if r else x

    def swap(x, bits):
        return lax.ppermute(x, "dp", [(d, d ^ bits) for d in range(n)])

    struct = jax.ShapeDtypeStruct
    share_shape, hidden_shape = (tokens, width), (tokens, hidden_dev)
    line_shape = (quarter, tokens, width)

    def call(kernel, outs, ins, args, scratch=(), cost=0, grant=8):
        return pl.pallas_call(
            kernel,
            out_shape=outs,
            in_specs=ins,
            out_specs=jax.tree.map(lambda _: VMEM, outs),
            scratch_shapes=list(scratch),
            compiler_params=params(grant),
            cost_estimate=pl.CostEstimate(
                flops=int(cost * tokens * width_all * hidden_dev),
                bytes_accessed=int(cost * width_all * hidden_dev),
                transcendentals=0,
            ),
        )(*args)

    offset = sample_ids - sender_base.shape[1] * me
    rows = -(-(2 * width // LANES + 1) // 16) * 16
    packed_shape = (tokens, width + LANES * -(-4 * rows // tokens))
    act_shape, expo_shape = (2, width_all), (2, width_all // LANES)
    once = lambda shape: pl.BlockSpec(shape, lambda i: (0,) * len(shape))
    in_shapes = [act_shape, expo_shape, sender_base.shape, receiver_base.shape, share_shape, (1, width_all)]
    outs = (
        struct(sender_base.shape, f32),
        struct(receiver_base.shape, f32),
        struct((n, width), f32),
    ) + (struct(packed_shape, bf16),) * quarter
    new_sender_base, received, gain, *packed = pl.pallas_call(
        send_kernel,
        out_shape=outs,
        grid=(1,),
        in_specs=[SMEM, SMEM] + [once(x) for x in in_shapes],
        out_specs=tuple(once(x.shape) for x in outs),
        scratch_shapes=[pltpu.VMEM((n, rows, LANES), f32)],
        compiler_params=params(8),
    )(
        me_in,
        offset,
        hbm(activations.reshape(act_shape)),
        hbm(forward_exponent.reshape(expo_shape)),
        hbm(sender_base),
        hbm(receiver_base),
        hbm(cotangent.reshape(share_shape)),
        hbm(norm_gain.reshape(1, width_all)),
    )
    packed = [shift(x, r) for r, x in enumerate(packed)]
    cot_line, *blocks = call(
        sort_kernel,
        (struct(line_shape, bf16),) + (struct((quarter, rows, LANES), bf16),) * 4,
        [SMEM] + [VMEM] * quarter,
        [me_in, *packed],
    )
    blocks = [blocks[0]] + [swap(blocks[e], e) for e in range(1, 4)]
    cot_row = swap(cot_line, 2)
    cots = [cot_line, cot_row, swap(cot_line, 1), swap(cot_row, 1)]

    ANY = pl.BlockSpec(memory_space=pl.ANY)
    sems = lambda count: pltpu.SemaphoreType.DMA((count,))
    share_f32 = struct(share_shape, f32)
    sums = (struct(hidden_shape, f32), struct((tokens, LANES), f32))

    def grad_active_part(part):
        return call(
            functools.partial(grad_active_kernel, part),
            (struct((hidden_dev, tokens), f32), share_f32),
            [SMEM, VMEM, ANY],
            [me_in, cots[part], hbm(down_weight)],
            [
                pltpu.VMEM((quarter, hidden_dev, width), bf16),
                pltpu.VMEM(share_shape, f32),
                sems(quarter),
            ],
            cost=0.5,
            grant=12,
        )

    def up_product_part(part):
        return call(
            functools.partial(up_kernel, part),
            sums + (share_f32,),
            [SMEM, VMEM, VMEM, ANY],
            [me_in, rests[part], gain, hbm(up_weight)],
            [
                pltpu.VMEM((quarter, width, hidden_dev), bf16),
                pltpu.VMEM(share_shape, f32),
                sems(quarter),
            ],
            cost=0.5,
            grant=12,
        )

    together = lax.optimization_barrier
    grads = [grad_active_part(0)]
    blocks, grads[0] = together((blocks, grads[0]))

    new_receiver_base, share = call(
        rebuild_kernel,
        (struct(receiver_base.shape, f32), struct(share_shape, bf16)),
        [SMEM] + [VMEM] * 5,
        [me_in, *blocks, received],
        [pltpu.VMEM((n * rows, LANES), f32), pltpu.VMEM((2 * width // LANES, 2 * n, LANES), f32)],
    )
    lines = [shift(share, r) for r in range(quarter)]
    grads.append(grad_active_part(1))
    lines, grads[1] = together((lines, grads[1]))
    rest_line = jnp.stack(lines)
    rest_row = swap(rest_line, 2)
    rests = [rest_line, rest_row, swap(rest_line, 1)]
    grads.append(grad_active_part(2))
    products = [up_product_part(0)]
    rest_row, grads[2], products[0] = together((rest_row, grads[2], products[0]))
    rests[1] = rest_row
    rests.append(swap(rest_row, 1))
    grads.append(grad_active_part(3))
    products += [up_product_part(1), up_product_part(2)]
    gas, own_cots = zip(*grads)
    accs, squares, owns = map(list, zip(*products))

    half_out = struct((half, tokens, width), bf16)
    active, own, grad_send, grad_keep = call(
        middle_kernel,
        (struct(hidden_shape, bf16), share_f32, half_out, half_out),
        [SMEM, VMEM, VMEM, ANY] + [VMEM] * 10,
        [me_in, rests[3], gain, hbm(up_weight), *accs, *squares, *gas],
        [pltpu.VMEM(x.shape, x.dtype) for x in sums]
        + [
            pltpu.VMEM(share_shape, f32),
            pltpu.VMEM((n, width, hidden_dev), bf16),
            pltpu.VMEM((width // LANES, n * tokens, LANES), f32),
            sems(n),
        ],
        cost=2.5,
        grant=24,
    )
    owns.append(own)

    def down_terms(other, after):
        return call(
            functools.partial(down_kernel, other),
            half_out,
            [SMEM] + [VMEM] * 2 + [ANY],
            [me_in, active, down_weight, after],
            cost=1,
        )

    pair_out = (struct(line_shape, bf16),) * 2
    line_out = (struct(share_shape, bf16),) * quarter
    grad_in = swap(grad_send, 1)
    out_in = swap(down_terms(1, grad_send), 1)
    grad_send, grad_row = call(
        pair_kernel, pair_out, [SMEM] + [VMEM] * 2, [me_in, grad_keep, grad_in]
    )
    grad_row_in = swap(grad_send, 2)
    out_send, out_row, *grad_line = call(
        pair_kernel,
        pair_out + line_out,
        [SMEM] + [VMEM] * 4,
        [me_in, down_terms(0, grad_send), out_in, grad_row, grad_row_in],
    )
    out_row_in = swap(out_send, 2)
    grad_line = [shift(x, r) for r, x in enumerate(grad_line)]
    out_line = call(line_kernel, line_out, [SMEM] + [VMEM] * 2, [me_in, out_row, out_row_in])
    out_line = [shift(x, r) for r, x in enumerate(out_line)]
    layer_out, returned = call(
        functools.partial(final_kernel, width_all),
        (struct(share_shape, bf16), struct((2, width_all // LANES, LANES), f32)),
        [VMEM] * (11 + 2 * quarter),
        [
            share,
            gain,
            backward_exponent.reshape(expo_shape),
            *owns,
            *own_cots,
            *grad_line,
            *out_line,
        ],
    )
    return (
        new_sender_base,
        new_receiver_base,
        layer_out.reshape(2, n, width),
        returned.reshape(2, 1, width_all),
    )


def solution(mesh):
    placed = (
        P(None, ("groups", "dp"), None),
        P(("groups", "dp")),
        P(None, ("groups", "dp"), None),
        P(None, ("groups", "dp"), None),
        P(None, "groups", "dp"),
        P(),
        P(None, "dp"),
        P("dp", None),
        P(None, "groups", "dp"),
        P(None, ("groups", "dp"), None),
    )
    return jax.shard_map(
        functools.partial(on_device, n=mesh.shape["dp"]),
        mesh=mesh,
        in_specs=placed,
        out_specs=(
            P(None, ("groups", "dp"), None),
            P(None, "groups", "dp"),
            P(None, "groups", "dp"),
            P(None, ("groups", "dp"), None),
        ),
        check_vma=False,
    )
```

```python
import functools

import jax
import jax.numpy as jnp
from jax import lax
from jax.experimental import pallas as pl
from jax.experimental.pallas import tpu as pltpu
from jax.sharding import PartitionSpec as P

clip_top = 448.0
eps = 1e-05
LANES = 128
f32 = jnp.float32
bf16 = jnp.bfloat16
VMEM = pl.BlockSpec(memory_space=pltpu.VMEM)
SMEM = pl.BlockSpec(memory_space=pltpu.SMEM)


def hbm(x):
    return pltpu.with_memory_space_constraint(x, pltpu.HBM)


def powers(exponent, sign):
    total = jnp.zeros(exponent.shape, f32)
    for level in range(-10, 1):
        total = jnp.where(exponent == level, f32(2.0 ** (sign * level)), total)
    return total


def params(megabytes):
    return pltpu.CompilerParams(vmem_limit_bytes=megabytes << 20)


def flip(bit, by):
    return lax.rem(bit + by, 2)


def place(me):
    return me // 4, lax.rem(me // 2, 2), lax.rem(me, 2)


def owner_of(me, part, k):
    return 2 * k + flip(lax.rem(me, 2), part)


def send_kernel(
    offset_ref, act_ref, expo_ref, base_ref, received_ref, cot_ref, gain_ref,
    out_ref, new_ref, received_out_ref, gain_out_ref, cots_ref, rows_ref,
):
    n, rows, _ = rows_ref.shape
    share = cot_ref.shape[1]
    width = act_ref.shape[1]
    per_dev = width // LANES // n
    received_out_ref[...] = received_ref[...]
    for j in range(n):
        gain_out_ref[j : j + 1, :] = gain_ref[:, j * share : (j + 1) * share]
    first = offset_ref[0] == 0
    down, up = powers(expo_ref[...], -1), powers(expo_ref[...], 1)
    old = [base_ref[p] for p in range(2)]
    chosen = jnp.concatenate([jnp.where(first, o[0:1], o[1:2]) for o in old], axis=0)
    delta = act_ref[...].astype(f32) - chosen
    fill = jnp.full((rows - 2 * per_dev, LANES), offset_ref[0].astype(f32))
    pieces = []
    for b in range(width // LANES):
        scaled = delta[:, b * LANES : (b + 1) * LANES] * down[:, b : b + 1]
        kept = jnp.clip(scaled, -clip_top, clip_top).astype(bf16).astype(f32) * up[:, b : b + 1]
        d, c = divmod(b, per_dev)
        rows_ref[d, 2 * c : 2 * c + 2, :] = kept
        pieces.append(kept)
    for d in range(n):
        rows_ref[d, 2 * per_dev :, :] = fill
    out_ref[...] = rows_ref[...].astype(bf16)
    for k in range(n // 2):
        cots_ref[k] = cot_ref[...]
    new = chosen + jnp.concatenate(pieces, axis=1)
    for p in range(2):
        row = new[p : p + 1]
        new_ref[p, 0:1, :] = jnp.where(first, row, old[p][0:1])
        new_ref[p, 1:2, :] = jnp.where(first, old[p][1:2], row)


def rebuild_kernel(arrived_ref, base_ref, new_ref, share_ref, copies_ref, rows_ref, slots_ref):
    n, rows, _ = arrived_ref.shape
    width = share_ref.shape[1]
    rows_ref[...] = arrived_ref[...].astype(f32).reshape(n * rows, LANES)
    per_dev = width // LANES
    first = rows_ref[pl.ds(2 * per_dev, n, stride=rows), :] == 0.0
    for p in range(2):
        for c in range(per_dev):
            cols = slice(c * LANES, (c + 1) * LANES)
            sent = rows_ref[pl.ds(2 * c + p, n, stride=rows), :]
            at = p * per_dev + c
            slots_ref[at] = base_ref[p, :, cols]
            even = slots_ref[at, pl.ds(0, n, stride=2), :]
            odd = slots_ref[at, pl.ds(1, n, stride=2), :]
            rebuilt = jnp.where(first, even, odd) + sent
            slots_ref[at, pl.ds(0, n, stride=2), :] = jnp.where(first, rebuilt, even)
            slots_ref[at, pl.ds(1, n, stride=2), :] = jnp.where(first, odd, rebuilt)
            new_ref[p, :, cols] = slots_ref[at]
            restored = rebuilt.astype(bf16)
            share_ref[p * n : (p + 1) * n, cols] = restored
            for k in range(copies_ref.shape[0]):
                copies_ref[k, p * n : (p + 1) * n, cols] = restored


def dot_nt(a, b):
    return lax.dot_general(a, b, (((1,), (1,)), ((), ())), preferred_element_type=f32)


def own_rows(piece_ref, own_ref, me, owner):
    n = piece_ref.shape[0] // 2
    for p in range(2):
        own_ref[pl.ds(p * n + owner, 1), :] = piece_ref[pl.ds(p * n + me, 1), :]


def dot_by_halves(rows, tokens):
    middle = tokens.shape[1] // 2 // LANES * LANES
    if middle == 0:
        return dot_nt(rows, tokens)
    return dot_nt(rows[:, :middle], tokens[:, :middle]) + dot_nt(rows[:, middle:], tokens[:, middle:])


class Stream:
    flying = 4

    def __init__(self, sources, held_ref, sems):
        self.copies = [
            pltpu.make_async_copy(source, held_ref.at[i], sems.at[i])
            for i, source in enumerate(sources)
        ]
        self.held_ref = held_ref
        for copy in self.copies[: self.flying]:
            copy.start()

    def block(self, i):
        self.copies[i].wait()
        if i + self.flying < len(self.copies):
            self.copies[i + self.flying].start()
        return self.held_ref[i]


def row_blocks(weight_ref, owners, width):
    return [weight_ref.at[pl.ds(pl.multiple_of(o * width, width), width)] for o in owners]


def grad_active_kernel(part, me_ref, cot_ref, weight_ref, acc_ref, own_ref, held_ref, piece_ref, sems):
    half, _, width = cot_ref.shape
    me = me_ref[0]
    owners = [owner_of(me, part, k) for k in range(half)]
    columns = [weight_ref.at[:, pl.ds(pl.multiple_of(o * width, width), width)] for o in owners]
    stream = Stream(columns, held_ref, sems)
    own_ref[...] = jnp.zeros_like(own_ref)
    for k, owner in enumerate(owners):
        piece_ref[...] = cot_ref[k].astype(f32)
        own_rows(piece_ref, own_ref, me, owner)
    for k in range(half):
        terms = dot_by_halves(stream.block(k), cot_ref[k])
        acc_ref[...] = terms if k == 0 else acc_ref[...] + terms


def up_part(part, me, rest_ref, gain_ref, stream, acc_ref, square_ref, own_ref, piece_ref):
    half, _, width = rest_ref.shape
    own_ref[...] = jnp.zeros_like(own_ref)
    scaled = []
    for k in range(half):
        owner = owner_of(me, part, k)
        piece = rest_ref[k].astype(f32)
        piece_ref[...] = piece
        own_rows(piece_ref, own_ref, me, owner)
        squares = piece * piece
        total = sum(squares[:, c * LANES : (c + 1) * LANES] for c in range(width // LANES))
        square_ref[...] = total if k == 0 else square_ref[...] + total
        scaled.append((piece * gain_ref[pl.ds(owner, 1), :]).astype(bf16))
    for k in range(half):
        terms = jnp.dot(scaled[k], stream.block(k), preferred_element_type=f32)
        acc_ref[...] = terms if k == 0 else acc_ref[...] + terms


def up_kernel(
    me_ref, rest_ref, gain_ref, weight_ref,
    acc_ref, square_ref, own_ref, held_ref, piece_ref, sems,
):
    half, _, width = rest_ref.shape
    me = me_ref[0]
    owners = [owner_of(me, 0, k) for k in range(half)]
    stream = Stream(row_blocks(weight_ref, owners, width), held_ref, sems)
    up_part(0, me, rest_ref, gain_ref, stream, acc_ref, square_ref, own_ref, piece_ref)


def middle_kernel(
    me_ref, rest_ref, gain_ref, weight_ref, acc_in_ref, square_in_ref, ga_ref, ga_too_ref,
    active_ref, own_ref, send_ref, keep_ref, acc_ref, square_ref, piece_ref, held_ref, rows_ref, sems,
):
    half, tokens, width = rest_ref.shape
    n, chunks = 2 * half, width // LANES
    width_all = weight_ref.shape[0]
    me = me_ref[0]
    owners = [owner_of(me, part, k) for part in (1, 0) for k in range(half)]
    stream = Stream(row_blocks(weight_ref, owners, width), held_ref, sems)
    up_part(1, me, rest_ref, gain_ref, stream, acc_ref, square_ref, own_ref, piece_ref)
    product = acc_ref[...] + acc_in_ref[...]
    total = jnp.sum(square_ref[...] + square_in_ref[...], axis=1, keepdims=True)
    hidden = lax.rsqrt(total / width_all + eps) * product
    sigma = jax.nn.sigmoid(hidden)
    active_ref[...] = (hidden * sigma).astype(bf16)
    grad_active = (ga_ref[...] + ga_too_ref[...]).T
    gh = (grad_active * sigma * (1.0 + hidden * (1.0 - sigma))).astype(bf16)
    for i, share in enumerate(owners):
        block = held_ref[i] if i < half else stream.block(i)
        terms = dot_by_halves(block, gh).T
        for p in range(2):
            for c in range(chunks):
                rows_ref[c, pl.ds(p * n + share, n, stride=tokens), :] = terms[
                    p * n : (p + 1) * n, c * LANES : (c + 1) * LANES
                ]
    core = lax.rem(me, 2)
    for k in range(half):
        keep_at = pl.multiple_of((2 * k + core) * tokens, tokens)
        send_at = pl.multiple_of((2 * k + 1 - core) * tokens, tokens)
        for c in range(chunks):
            cols = slice(c * LANES, (c + 1) * LANES)
            keep_ref[k, :, cols] = rows_ref[c, pl.ds(keep_at, tokens), :].astype(bf16)
            send_ref[k, :, cols] = rows_ref[c, pl.ds(send_at, tokens), :].astype(bf16)


def down_kernel(other, me_ref, active_ref, weight_ref, after_ref, out_ref):
    half, _, width = out_ref.shape
    core = lax.rem(me_ref[0] + other, 2)

    def share(k):
        columns = pl.ds(pl.multiple_of((2 * k + core) * width, width), width)
        terms = jnp.dot(active_ref[...], weight_ref[:, columns], preferred_element_type=f32)
        out_ref[k] = terms.astype(bf16)

    pl.loop(0, half, unroll=4)(share)


def pair_kernel(me_ref, kept_ref, arrived_ref, *refs):
    ins, (send_ref, keep_ref), shares = (refs[:2], refs[2:4], refs[4:]) if len(refs) > 2 else ((), refs, ())
    quarter = send_ref.shape[0]
    _, row, _ = place(me_ref[0])
    for k in range(quarter):
        for out_ref, at in ((send_ref, 2 * k + 1 - row), (keep_ref, 2 * k + row)):
            out_ref[k] = (kept_ref[at].astype(f32) + arrived_ref[at].astype(f32)).astype(bf16)
    if shares:
        line_kernel(me_ref, *ins, *shares)


def line_kernel(me_ref, kept_ref, arrived_ref, *refs):
    along, _, _ = place(me_ref[0])
    for r, ref in enumerate(refs):
        at = jnp.bitwise_xor(along, r)
        ref[...] = (kept_ref[at].astype(f32) + arrived_ref[at].astype(f32)).astype(bf16)


def added(refs):
    return functools.reduce(lambda a, b: a + b, [ref[...].astype(f32) for ref in refs])


def final_kernel(width_all, share_ref, gain_ref, expo_ref, *refs):
    *refs, layer_ref, grad_ref = refs
    quarter = (len(refs) - 4) // 2
    own_all, cot_all = added(refs[:2]), added(refs[2:4])
    grad, layer = added(refs[4 : 4 + quarter]), added(refs[4 + quarter :])
    layer_ref[...] = (share_ref[...].astype(f32) + layer).astype(bf16)
    n, width = gain_ref.shape
    down, up = powers(expo_ref[...], -1), powers(expo_ref[...], 1)
    gain = gain_ref[...]
    per_dev = width // LANES
    blocks = n * per_dev
    at_row = lax.broadcasted_iota(jnp.int32, (n, blocks), 0)
    at_lane = lax.broadcasted_iota(jnp.int32, (n, blocks), 1)
    for p in range(2):
        rows = slice(p * n, (p + 1) * n)
        own, norm = own_all[rows, :], grad[rows, :]
        inv_rms = lax.rsqrt(jnp.sum(own * own, keepdims=True) / width_all + eps)
        scaled_in = (own * gain).astype(bf16).astype(f32)
        curvature = inv_rms * jnp.sum(scaled_in * norm, keepdims=True)
        correction = curvature * inv_rms * inv_rms / width_all
        value = cot_all[rows, :] + inv_rms * gain * norm - correction * own
        for c in range(per_dev):
            at = at_lane == at_row * per_dev + c
            shrink = jnp.sum(jnp.where(at, down[p : p + 1], 0.0), axis=1, keepdims=True)
            grow = jnp.sum(jnp.where(at, up[p : p + 1], 0.0), axis=1, keepdims=True)
            scaled = value[:, c * LANES : (c + 1) * LANES] * shrink
            kept = jnp.clip(scaled, -clip_top, clip_top).astype(bf16).astype(f32) * grow
            grad_ref[p, pl.ds(c, n, stride=per_dev), :] = kept


def on_device(
    activations,
    sample_ids,
    forward_exponent,
    sender_base,
    receiver_base,
    norm_gain,
    up_weight,
    down_weight,
    cotangent,
    backward_exponent,
    *,
    n,
):
    half, quarter = n // 2, n // 4
    tokens = 2 * n
    width_all, hidden_dev = up_weight.shape
    width = width_all // n
    me = lax.axis_index("dp").astype(jnp.int32)
    me_in = me.reshape(1)

    def shift(x, r):
        return lax.ppermute(x, "dp", [(d, d ^ (4 * r)) for d in range(n)]) if r else x

    def swap(x, bits):
        return lax.ppermute(x, "dp", [(d, d ^ bits) for d in range(n)])

    def exchange(x, among=None):
        return lax.all_to_all(
            x, "dp", split_axis=0, concat_axis=0, axis_index_groups=among, tiled=True
        )

    same_core = [[2 * k + c for k in range(half)] for c in range(2)]
    struct = jax.ShapeDtypeStruct
    share_shape, hidden_shape = (tokens, width), (tokens, hidden_dev)
    line_shape = (quarter, tokens, width)

    def call(kernel, outs, ins, args, scratch=(), cost=0, grant=8):
        return pl.pallas_call(
            kernel,
            out_shape=outs,
            in_specs=ins,
            out_specs=jax.tree.map(lambda _: VMEM, outs),
            scratch_shapes=list(scratch),
            compiler_params=params(grant),
            cost_estimate=pl.CostEstimate(
                flops=int(cost * tokens * width_all * hidden_dev),
                bytes_accessed=int(cost * width_all * hidden_dev),
                transcendentals=0,
            ),
        )(*args)

    offset = sample_ids - sender_base.shape[1] * me
    rows = -(-(2 * width // LANES + 1) // 16) * 16
    act_shape, expo_shape = (2, width_all), (2, width_all // LANES)
    once = lambda shape: pl.BlockSpec(shape, lambda i: (0,) * len(shape))
    in_shapes = [act_shape, expo_shape, sender_base.shape, receiver_base.shape, share_shape, (1, width_all)]
    outs = (
        struct((n, rows, LANES), bf16),
        struct(sender_base.shape, f32),
        struct(receiver_base.shape, f32),
        struct((n, width), f32),
        struct((half, tokens, width), bf16),
    )
    blocks, new_sender_base, received, gain, cots = pl.pallas_call(
        send_kernel,
        out_shape=outs,
        grid=(1,),
        in_specs=[SMEM] + [once(x) for x in in_shapes],
        out_specs=tuple(once(x.shape) for x in outs),
        scratch_shapes=[pltpu.VMEM((n, rows, LANES), f32)],
        compiler_params=params(8),
    )(
        offset,
        hbm(activations.reshape(act_shape)),
        hbm(forward_exponent.reshape(expo_shape)),
        hbm(sender_base),
        hbm(receiver_base),
        hbm(cotangent.reshape(share_shape)),
        hbm(norm_gain.reshape(1, width_all)),
    )
    arrived = exchange(blocks)
    cots = exchange(cots, same_core)
    cots = [cots, swap(cots, 1)]

    ANY = pl.BlockSpec(memory_space=pl.ANY)
    sems = lambda count: pltpu.SemaphoreType.DMA((count,))
    share_f32 = struct(share_shape, f32)
    sums = (struct(hidden_shape, f32), struct((tokens, LANES), f32))

    def weight_call(kernel, outs, args, weight, blocks, cost, more=(), scratch=(), grant=16):
        return call(
            kernel,
            outs,
            [SMEM] + [VMEM] * (len(args) - 1) + [ANY] + [VMEM] * len(more),
            [*args, hbm(weight), *more],
            [*scratch, pltpu.VMEM(blocks, bf16), pltpu.VMEM(share_shape, f32), sems(blocks[0])],
            cost=cost,
            grant=grant,
        )

    new_receiver_base, share, copies = call(
        rebuild_kernel,
        (
            struct(receiver_base.shape, f32),
            struct(share_shape, bf16),
            struct((half, tokens, width), bf16),
        ),
        [VMEM] * 2,
        [arrived, received],
        [pltpu.VMEM((n * rows, LANES), f32), pltpu.VMEM((2 * width // LANES, 2 * n, LANES), f32)],
    )
    rest = exchange(copies, same_core)
    gas, own_cots = zip(*[
        weight_call(
            functools.partial(grad_active_kernel, part),
            (struct((hidden_dev, tokens), f32), share_f32),
            [me_in, cots[part]],
            down_weight,
            (half, hidden_dev, width),
            1,
        )
        for part in range(2)
    ])
    rest, gas = lax.optimization_barrier((rest, gas))
    rest_other = swap(rest, 1)
    acc, square, own = weight_call(
        up_kernel,
        sums + (share_f32,),
        [me_in, rest, gain],
        up_weight,
        (half, width, hidden_dev),
        1,
    )
    half_out = struct((half, tokens, width), bf16)
    active, own_too, grad_send, grad_keep = call(
        middle_kernel,
        (struct(hidden_shape, bf16), share_f32, half_out, half_out),
        [SMEM, VMEM, VMEM, ANY] + [VMEM] * 4,
        [me_in, rest_other, gain, hbm(up_weight), acc, square, *gas],
        [pltpu.VMEM(x.shape, x.dtype) for x in sums]
        + [
            pltpu.VMEM(share_shape, f32),
            pltpu.VMEM((n, width, hidden_dev), bf16),
            pltpu.VMEM((width // LANES, n * tokens, LANES), f32),
            sems(n),
        ],
        cost=3,
        grant=24,
    )

    def down_terms(other, after):
        return call(
            functools.partial(down_kernel, other),
            half_out,
            [SMEM] + [VMEM] * 2 + [ANY],
            [me_in, active, down_weight, after],
            cost=1,
        )

    pair_out = (struct(line_shape, bf16),) * 2
    line_out = (struct(share_shape, bf16),) * quarter
    grad_in = swap(grad_send, 1)
    out_in = swap(down_terms(1, grad_send), 1)
    grad_send, grad_row = call(
        pair_kernel, pair_out, [SMEM] + [VMEM] * 2, [me_in, grad_keep, grad_in]
    )
    grad_row_in = swap(grad_send, 2)
    out_send, out_row, *grad_line = call(
        pair_kernel,
        pair_out + line_out,
        [SMEM] + [VMEM] * 4,
        [me_in, down_terms(0, grad_send), out_in, grad_row, grad_row_in],
    )
    out_row_in = swap(out_send, 2)
    grad_line = [shift(x, r) for r, x in enumerate(grad_line)]
    out_line = call(line_kernel, line_out, [SMEM] + [VMEM] * 2, [me_in, out_row, out_row_in])
    out_line = [shift(x, r) for r, x in enumerate(out_line)]
    layer_out, returned = call(
        functools.partial(final_kernel, width_all),
        (struct(share_shape, bf16), struct((2, width_all // LANES, LANES), f32)),
        [VMEM] * (7 + 2 * quarter),
        [
            share,
            gain,
            backward_exponent.reshape(expo_shape),
            own,
            own_too,
            *own_cots,
            *grad_line,
            *out_line,
        ],
    )
    return (
        new_sender_base,
        new_receiver_base,
        layer_out.reshape(2, n, width),
        returned.reshape(2, 1, width_all),
    )


def solution(mesh):
    placed = (
        P(None, ("groups", "dp"), None),
        P(("groups", "dp")),
        P(None, ("groups", "dp"), None),
        P(None, ("groups", "dp"), None),
        P(None, "groups", "dp"),
        P(),
        P(None, "dp"),
        P("dp", None),
        P(None, "groups", "dp"),
        P(None, ("groups", "dp"), None),
    )
    return jax.shard_map(
        functools.partial(on_device, n=mesh.shape["dp"]),
        mesh=mesh,
        in_specs=placed,
        out_specs=(
            P(None, ("groups", "dp"), None),
            P(None, "groups", "dp"),
            P(None, "groups", "dp"),
            P(None, ("groups", "dp"), None),
        ),
        check_vma=False,
    )
```

```python
import functools

import jax
import jax.numpy as jnp
from jax import lax
from jax.experimental import pallas as pl
from jax.experimental.pallas import tpu as pltpu
from jax.sharding import PartitionSpec as P

clip_top = 448.0
eps = 1e-05
LANES = 128
STAGE = 7
FLOPS_PER_MICRO = 1.15e9
f32 = jnp.float32
bf16 = jnp.bfloat16
VMEM = pl.BlockSpec(memory_space=pltpu.VMEM)
SMEM = pl.BlockSpec(memory_space=pltpu.SMEM)


def hbm(x):
    return pltpu.with_memory_space_constraint(x, pltpu.HBM)


def powers(exponent, sign):
    total = jnp.zeros(exponent.shape, f32)
    for level in range(-10, 1):
        total = jnp.where(exponent == level, f32(2.0 ** (sign * level)), total)
    return total


def params(megabytes):
    return pltpu.CompilerParams(vmem_limit_bytes=megabytes << 20)


def flip(bit, by):
    return lax.rem(bit + by, 2)


def place(me):
    return me // 4, lax.rem(me // 2, 2), lax.rem(me, 2)


def owner_of(me, n, part, back):
    along, row, core = place(me)
    at = jnp.bitwise_xor(along, back)
    return 4 * at + 2 * flip(row, part % 2) + flip(core, part // 2)


def block_spot(q, tokens, rows, width):
    per_column = tokens // rows
    r, c = rows * (q % per_column), width + LANES * (q // per_column)
    return slice(r, r + rows), slice(c, c + LANES)


def send_kernel(
    me_ref, offset_ref, act_ref, expo_ref, base_ref, received_ref, cot_ref, gain_ref,
    new_ref, received_out_ref, gain_out_ref, *refs,
):
    *packed_refs, rows_ref = refs
    n, rows, _ = rows_ref.shape
    tokens, share = cot_ref.shape
    width = act_ref.shape[1]
    per_dev = width // LANES // n
    received_out_ref[...] = received_ref[...]
    for j in range(n):
        gain_out_ref[j : j + 1, :] = gain_ref[:, j * share : (j + 1) * share]
    first = offset_ref[0] == 0
    down, up = powers(expo_ref[...], -1), powers(expo_ref[...], 1)
    old = [base_ref[p] for p in range(2)]
    chosen = jnp.concatenate([jnp.where(first, o[0:1], o[1:2]) for o in old], axis=0)
    delta = act_ref[...].astype(f32) - chosen
    fill = jnp.full((rows - 2 * per_dev, LANES), offset_ref[0].astype(f32))
    pieces = []
    for b in range(width // LANES):
        scaled = delta[:, b * LANES : (b + 1) * LANES] * down[:, b : b + 1]
        kept = jnp.clip(scaled, -clip_top, clip_top).astype(bf16).astype(f32) * up[:, b : b + 1]
        d, c = divmod(b, per_dev)
        rows_ref[d, 2 * c : 2 * c + 2, :] = kept
        pieces.append(kept)
    for d in range(n):
        rows_ref[d, 2 * per_dev :, :] = fill
    along, _, _ = place(me_ref[0])
    cot = cot_ref[...]
    for r, packed_ref in enumerate(packed_refs):
        to = jnp.bitwise_xor(along, r)
        packed_ref[:, :share] = cot
        for q in range(4):
            packed_ref[block_spot(q, tokens, rows, share)] = rows_ref[4 * to + q].astype(bf16)
    new = chosen + jnp.concatenate(pieces, axis=1)
    for p in range(2):
        row = new[p : p + 1]
        new_ref[p, 0:1, :] = jnp.where(first, row, old[p][0:1])
        new_ref[p, 1:2, :] = jnp.where(first, old[p][1:2], row)


def sort_kernel(me_ref, *refs):
    *packed_refs, line_ref, b0, b1, b2, b3 = refs
    quarter, tokens, share = line_ref.shape
    rows = b0.shape[1]
    _, row, core = place(me_ref[0])
    for r, packed_ref in enumerate(packed_refs):
        line_ref[r] = packed_ref[:, :share]
        block = [packed_ref[block_spot(q, tokens, rows, share)] for q in range(4)]
        for e, out_ref in enumerate((b0, b1, b2, b3)):
            to_row, to_core = flip(row, e // 2), flip(core, e % 2)
            low = jnp.where(to_core == 0, block[0], block[1])
            high = jnp.where(to_core == 0, block[2], block[3])
            out_ref[r] = jnp.where(to_row == 0, low, high)


def rebuild_kernel(me_ref, b0, b1, b2, b3, base_ref, new_ref, share_ref, rows_ref, slots_ref):
    quarter, rows, _ = b0.shape
    n, width = 4 * quarter, share_ref.shape[1]
    for e, block_ref in enumerate((b0, b1, b2, b3)):
        for r in range(quarter):
            sender = owner_of(me_ref[0], n, 2 * (e % 2) + e // 2, r)
            rows_ref[pl.ds(pl.multiple_of(sender * rows, rows), rows), :] = block_ref[r].astype(f32)
    per_dev = width // LANES
    first = rows_ref[pl.ds(2 * per_dev, n, stride=rows), :] == 0.0
    for p in range(2):
        for c in range(per_dev):
            cols = slice(c * LANES, (c + 1) * LANES)
            sent = rows_ref[pl.ds(2 * c + p, n, stride=rows), :]
            at = p * per_dev + c
            slots_ref[at] = base_ref[p, :, cols]
            even = slots_ref[at, pl.ds(0, n, stride=2), :]
            odd = slots_ref[at, pl.ds(1, n, stride=2), :]
            rebuilt = jnp.where(first, even, odd) + sent
            slots_ref[at, pl.ds(0, n, stride=2), :] = jnp.where(first, rebuilt, even)
            slots_ref[at, pl.ds(1, n, stride=2), :] = jnp.where(first, odd, rebuilt)
            new_ref[p, :, cols] = slots_ref[at]
            restored = rebuilt.astype(bf16)
            share_ref[p * n : (p + 1) * n, cols] = restored


def dot_nt(a, b):
    return lax.dot_general(a, b, (((1,), (1,)), ((), ())), preferred_element_type=f32)


def own_rows(piece_ref, own_ref, me, owner):
    n = piece_ref.shape[0] // 2
    for p in range(2):
        own_ref[pl.ds(p * n + owner, 1), :] = piece_ref[pl.ds(p * n + me, 1), :]


def dot_by_halves(rows, tokens):
    middle = tokens.shape[1] // 2 // LANES * LANES
    if middle == 0:
        return dot_nt(rows, tokens)
    return dot_nt(rows[:, :middle], tokens[:, :middle]) + dot_nt(rows[:, middle:], tokens[:, middle:])


def grad_active_kernel(part, me_ref, cot_ref, weight_ref, acc_ref, own_ref, piece_ref):
    quarter, _, width = cot_ref.shape
    me = me_ref[0]
    own_ref[...] = jnp.zeros_like(own_ref)
    for k in range(quarter):
        owner = owner_of(me, 4 * quarter, part, k)
        piece_ref[...] = cot_ref[k].astype(f32)
        own_rows(piece_ref, own_ref, me, owner)
        columns = pl.ds(pl.multiple_of(owner * width, width), width)
        terms = dot_by_halves(weight_ref[:, columns], cot_ref[k])
        acc_ref[...] = terms if k == 0 else acc_ref[...] + terms


def up_kernel(
    part, me_ref, rest_ref, gain_ref, weight_ref, acc_ref, square_ref, own_ref, piece_ref
):
    quarter, _, width = rest_ref.shape
    me = me_ref[0]
    own_ref[...] = jnp.zeros_like(own_ref)
    for k in range(quarter):
        owner = owner_of(me, 4 * quarter, part, k)
        piece = rest_ref[k].astype(f32)
        piece_ref[...] = piece
        own_rows(piece_ref, own_ref, me, owner)
        squares = piece * piece
        total = sum(squares[:, c * LANES : (c + 1) * LANES] for c in range(width // LANES))
        square_ref[...] = total if k == 0 else square_ref[...] + total
        scaled = (piece * gain_ref[pl.ds(owner, 1), :]).astype(bf16)
        rows = pl.ds(pl.multiple_of(owner * width, width), width)
        terms = jnp.dot(scaled, weight_ref[rows, :], preferred_element_type=f32)
        acc_ref[...] = terms if k == 0 else acc_ref[...] + terms


def middle_kernel(me_ref, rest_ref, gain_ref, weight_ref, *refs):
    ins, refs = refs[:10], refs[10:]
    active_ref, own_ref, send_ref, keep_ref, acc_ref, square_ref, piece_ref, rows_ref = refs
    quarter, tokens, width = rest_ref.shape
    half, n, chunks = 2 * quarter, 4 * quarter, width // LANES
    width_all = weight_ref.shape[0]
    me = me_ref[0]
    up_kernel(3, me_ref, rest_ref, gain_ref, weight_ref, acc_ref, square_ref, own_ref, piece_ref)
    product = acc_ref[...] + (ins[0][...] + ins[1][...] + ins[2][...])
    squares = square_ref[...] + (ins[3][...] + ins[4][...] + ins[5][...])
    total = jnp.sum(squares, axis=1, keepdims=True)
    hidden = lax.rsqrt(total / width_all + eps) * product
    sigma = jax.nn.sigmoid(hidden)
    active_ref[...] = (hidden * sigma).astype(bf16)
    grad_active = (ins[6][...] + ins[7][...] + (ins[8][...] + ins[9][...])).T
    gh = (grad_active * sigma * (1.0 + hidden * (1.0 - sigma))).astype(bf16)
    for share in range(n):
        block = weight_ref[share * width : (share + 1) * width, :]
        terms = dot_by_halves(block, gh).T
        for p in range(2):
            for c in range(chunks):
                rows_ref[c, pl.ds(p * n + share, n, stride=tokens), :] = terms[
                    p * n : (p + 1) * n, c * LANES : (c + 1) * LANES
                ]
    core = lax.rem(me, 2)
    for k in range(half):
        keep_at = pl.multiple_of((2 * k + core) * tokens, tokens)
        send_at = pl.multiple_of((2 * k + 1 - core) * tokens, tokens)
        for c in range(chunks):
            cols = slice(c * LANES, (c + 1) * LANES)
            keep_ref[k, :, cols] = rows_ref[c, pl.ds(keep_at, tokens), :].astype(bf16)
            send_ref[k, :, cols] = rows_ref[c, pl.ds(send_at, tokens), :].astype(bf16)


def down_kernel(other, me_ref, active_ref, weight_ref, after_ref, out_ref):
    half, _, width = out_ref.shape
    core = lax.rem(me_ref[0] + other, 2)

    def share(k):
        columns = pl.ds(pl.multiple_of((2 * k + core) * width, width), width)
        terms = jnp.dot(active_ref[...], weight_ref[:, columns], preferred_element_type=f32)
        out_ref[k] = terms.astype(bf16)

    pl.loop(0, half, unroll=4)(share)


def pair_kernel(me_ref, kept_ref, arrived_ref, *refs):
    ins, (send_ref, keep_ref), shares = (refs[:2], refs[2:4], refs[4:]) if len(refs) > 2 else ((), refs, ())
    quarter = send_ref.shape[0]
    _, row, _ = place(me_ref[0])
    for k in range(quarter):
        for out_ref, at in ((send_ref, 2 * k + 1 - row), (keep_ref, 2 * k + row)):
            out_ref[k] = (kept_ref[at].astype(f32) + arrived_ref[at].astype(f32)).astype(bf16)
    if shares:
        line_kernel(me_ref, *ins, *shares)


def line_kernel(me_ref, kept_ref, arrived_ref, *refs):
    along, _, _ = place(me_ref[0])
    for r, ref in enumerate(refs):
        at = jnp.bitwise_xor(along, r)
        ref[...] = (kept_ref[at].astype(f32) + arrived_ref[at].astype(f32)).astype(bf16)


def added(refs):
    return functools.reduce(lambda a, b: a + b, [ref[...].astype(f32) for ref in refs])


def final_kernel(width_all, share_ref, gain_ref, expo_ref, *refs):
    *refs, layer_ref, grad_ref = refs
    quarter = (len(refs) - 8) // 2
    own_all, cot_all = added(refs[:4]), added(refs[4:8])
    grad, layer = added(refs[8 : 8 + quarter]), added(refs[8 + quarter :])
    layer_ref[...] = (share_ref[...].astype(f32) + layer).astype(bf16)
    n, width = gain_ref.shape
    down, up = powers(expo_ref[...], -1), powers(expo_ref[...], 1)
    gain = gain_ref[...]
    per_dev = width // LANES
    blocks = n * per_dev
    at_row = lax.broadcasted_iota(jnp.int32, (n, blocks), 0)
    at_lane = lax.broadcasted_iota(jnp.int32, (n, blocks), 1)
    for p in range(2):
        rows = slice(p * n, (p + 1) * n)
        own, norm = own_all[rows, :], grad[rows, :]
        inv_rms = lax.rsqrt(jnp.sum(own * own, keepdims=True) / width_all + eps)
        scaled_in = (own * gain).astype(bf16).astype(f32)
        curvature = inv_rms * jnp.sum(scaled_in * norm, keepdims=True)
        correction = curvature * inv_rms * inv_rms / width_all
        value = cot_all[rows, :] + inv_rms * gain * norm - correction * own
        for c in range(per_dev):
            at = at_lane == at_row * per_dev + c
            shrink = jnp.sum(jnp.where(at, down[p : p + 1], 0.0), axis=1, keepdims=True)
            grow = jnp.sum(jnp.where(at, up[p : p + 1], 0.0), axis=1, keepdims=True)
            scaled = value[:, c * LANES : (c + 1) * LANES] * shrink
            kept = jnp.clip(scaled, -clip_top, clip_top).astype(bf16).astype(f32) * grow
            grad_ref[p, pl.ds(c, n, stride=per_dev), :] = kept


def on_device(
    activations,
    sample_ids,
    forward_exponent,
    sender_base,
    receiver_base,
    norm_gain,
    up_weight,
    down_weight,
    cotangent,
    backward_exponent,
    *,
    n,
):
    half, quarter = n // 2, n // 4
    tokens = 2 * n
    width_all, hidden_dev = up_weight.shape
    width = width_all // n
    me = lax.axis_index("dp").astype(jnp.int32)
    me_in = me.reshape(1)

    def shift(x, r):
        return lax.ppermute(x, "dp", [(d, d ^ (4 * r)) for d in range(n)]) if r else x

    def swap(x, bits):
        return lax.ppermute(x, "dp", [(d, d ^ bits) for d in range(n)])

    struct = jax.ShapeDtypeStruct
    share_shape, hidden_shape = (tokens, width), (tokens, hidden_dev)
    line_shape = (quarter, tokens, width)

    def call(kernel, outs, ins, args, scratch=(), micros=0.5):
        return pl.pallas_call(
            kernel,
            out_shape=outs,
            in_specs=ins,
            out_specs=jax.tree.map(lambda _: VMEM, outs),
            scratch_shapes=list(scratch),
            compiler_params=params(8),
            cost_estimate=pl.CostEstimate(
                flops=int(micros * FLOPS_PER_MICRO), bytes_accessed=0, transcendentals=0
            ),
        )(*args)

    offset = sample_ids - sender_base.shape[1] * me
    rows = -(-(2 * width // LANES + 1) // 16) * 16
    packed_shape = (tokens, width + LANES * -(-4 * rows // tokens))
    act_shape, expo_shape = (2, width_all), (2, width_all // LANES)
    once = lambda shape: pl.BlockSpec(shape, lambda i: (0,) * len(shape))
    in_shapes = [act_shape, expo_shape, sender_base.shape, receiver_base.shape, share_shape, (1, width_all)]
    outs = (
        struct(sender_base.shape, f32),
        struct(receiver_base.shape, f32),
        struct((n, width), f32),
    ) + (struct(packed_shape, bf16),) * quarter
    new_sender_base, received, gain, *packed = pl.pallas_call(
        send_kernel,
        out_shape=outs,
        grid=(1,),
        in_specs=[SMEM, SMEM] + [once(x) for x in in_shapes],
        out_specs=tuple(once(x.shape) for x in outs),
        scratch_shapes=[pltpu.VMEM((n, rows, LANES), f32)],
        compiler_params=params(8),
    )(
        me_in,
        offset,
        hbm(activations.reshape(act_shape)),
        hbm(forward_exponent.reshape(expo_shape)),
        hbm(sender_base),
        hbm(receiver_base),
        hbm(cotangent.reshape(share_shape)),
        hbm(norm_gain.reshape(1, width_all)),
    )
    packed = [shift(x, r) for r, x in enumerate(packed)]
    cot_line, *blocks = call(
        sort_kernel,
        (struct(line_shape, bf16),) + (struct((quarter, rows, LANES), bf16),) * 4,
        [SMEM] + [VMEM] * quarter,
        [me_in, *packed],
        micros=STAGE,
    )
    blocks = [blocks[0]] + [swap(blocks[e], e) for e in range(1, 4)]
    cot_row = swap(cot_line, 2)
    cots = [cot_line, cot_row, swap(cot_line, 1), swap(cot_row, 1)]

    ANY = pl.BlockSpec(memory_space=pl.ANY)
    share_f32 = struct(share_shape, f32)
    sums = (struct(hidden_shape, f32), struct((tokens, LANES), f32))

    def grad_active_part(part):
        return call(
            functools.partial(grad_active_kernel, part),
            (struct((hidden_dev, tokens), f32), share_f32),
            [SMEM, VMEM, VMEM],
            [me_in, cots[part], down_weight],
            [pltpu.VMEM(share_shape, f32)],
            micros=1.6,
        )

    def up_product_part(part):
        return call(
            functools.partial(up_kernel, part),
            sums + (share_f32,),
            [SMEM] + [VMEM] * 3,
            [me_in, rests[part], gain, up_weight],
            [pltpu.VMEM(share_shape, f32)],
            micros=1.2,
        )

    together = lax.optimization_barrier
    grads = [grad_active_part(0)]
    blocks, grads[0] = together((blocks, grads[0]))

    new_receiver_base, share = call(
        rebuild_kernel,
        (struct(receiver_base.shape, f32), struct(share_shape, bf16)),
        [SMEM] + [VMEM] * 5,
        [me_in, *blocks, received],
        [pltpu.VMEM((n * rows, LANES), f32), pltpu.VMEM((2 * width // LANES, 2 * n, LANES), f32)],
        micros=STAGE,
    )
    lines = [shift(share, r) for r in range(quarter)]
    grads.append(grad_active_part(1))
    lines, grads[1] = together((lines, grads[1]))
    rest_line = jnp.stack(lines)
    rest_row = swap(rest_line, 2)
    rests = [rest_line, rest_row, swap(rest_line, 1)]
    grads.append(grad_active_part(2))
    products = [up_product_part(0)]
    rest_row, grads[2], products[0] = together((rest_row, grads[2], products[0]))
    rests[1] = rest_row
    rests.append(swap(rest_row, 1))
    grads.append(grad_active_part(3))
    products += [up_product_part(1), up_product_part(2)]
    gas, own_cots = zip(*grads)
    accs, squares, owns = map(list, zip(*products))

    half_out = struct((half, tokens, width), bf16)
    active, own, grad_send, grad_keep = call(
        middle_kernel,
        (struct(hidden_shape, bf16), share_f32, half_out, half_out),
        [SMEM] + [VMEM] * 13,
        [me_in, rests[3], gain, up_weight, *accs, *squares, *gas],
        [pltpu.VMEM(x.shape, x.dtype) for x in sums]
        + [
            pltpu.VMEM(share_shape, f32),
            pltpu.VMEM((width // LANES, n * tokens, LANES), f32),
        ],
        micros=6.5,
    )
    owns.append(own)

    def down_terms(other, after):
        return call(
            functools.partial(down_kernel, other),
            half_out,
            [SMEM] + [VMEM] * 2 + [ANY],
            [me_in, active, down_weight, after],
            micros=1.5,
        )

    pair_out = (struct(line_shape, bf16),) * 2
    line_out = (struct(share_shape, bf16),) * quarter
    grad_in = swap(grad_send, 1)
    out_in = swap(down_terms(1, grad_send), 1)
    grad_send, grad_row = call(
        pair_kernel, pair_out, [SMEM] + [VMEM] * 2, [me_in, grad_keep, grad_in]
    )
    grad_row_in = swap(grad_send, 2)
    out_send, out_row, *grad_line = call(
        pair_kernel,
        pair_out + line_out,
        [SMEM] + [VMEM] * 4,
        [me_in, down_terms(0, grad_send), out_in, grad_row, grad_row_in],
    )
    out_row_in = swap(out_send, 2)
    grad_line = [shift(x, r) for r, x in enumerate(grad_line)]
    out_line = call(line_kernel, line_out, [SMEM] + [VMEM] * 2, [me_in, out_row, out_row_in])
    out_line = [shift(x, r) for r, x in enumerate(out_line)]
    layer_out, returned = call(
        functools.partial(final_kernel, width_all),
        (struct(share_shape, bf16), struct((2, width_all // LANES, LANES), f32)),
        [VMEM] * (11 + 2 * quarter),
        [
            share,
            gain,
            backward_exponent.reshape(expo_shape),
            *owns,
            *own_cots,
            *grad_line,
            *out_line,
        ],
    )
    return (
        new_sender_base,
        new_receiver_base,
        layer_out.reshape(2, n, width),
        returned.reshape(2, 1, width_all),
    )


def solution(mesh):
    placed = (
        P(None, ("groups", "dp"), None),
        P(("groups", "dp")),
        P(None, ("groups", "dp"), None),
        P(None, ("groups", "dp"), None),
        P(None, "groups", "dp"),
        P(),
        P(None, "dp"),
        P("dp", None),
        P(None, "groups", "dp"),
        P(None, ("groups", "dp"), None),
    )
    return jax.shard_map(
        functools.partial(on_device, n=mesh.shape["dp"]),
        mesh=mesh,
        in_specs=placed,
        out_specs=(
            P(None, ("groups", "dp"), None),
            P(None, "groups", "dp"),
            P(None, "groups", "dp"),
            P(None, ("groups", "dp"), None),
        ),
        check_vma=False,
    )
```

```python
import functools

import jax
import jax.numpy as jnp
from jax import lax
from jax.experimental import pallas as pl
from jax.experimental.pallas import tpu as pltpu
from jax.sharding import PartitionSpec as P

clip_top = 448.0
eps = 1e-05
LANES = 128
STAGE = 7
FLOPS_PER_MICRO = 1.15e9
f32 = jnp.float32
bf16 = jnp.bfloat16
VMEM = pl.BlockSpec(memory_space=pltpu.VMEM)
SMEM = pl.BlockSpec(memory_space=pltpu.SMEM)


def hbm(x):
    return pltpu.with_memory_space_constraint(x, pltpu.HBM)


def powers(exponent, sign):
    total = jnp.zeros(exponent.shape, f32)
    for level in range(-10, 1):
        total = jnp.where(exponent == level, f32(2.0 ** (sign * level)), total)
    return total


def params(megabytes):
    return pltpu.CompilerParams(vmem_limit_bytes=megabytes << 20)


def flip(bit, by):
    return lax.rem(bit + by, 2)


def place(me):
    return me // 4, lax.rem(me // 2, 2), lax.rem(me, 2)


def owner_of(me, n, part, back):
    along, row, core = place(me)
    at = jnp.bitwise_xor(along, back)
    return 4 * at + 2 * flip(row, part % 2) + flip(core, part // 2)


def block_spot(q, tokens, rows, width):
    per_column = tokens // rows
    r, c = rows * (q % per_column), width + LANES * (q // per_column)
    return slice(r, r + rows), slice(c, c + LANES)


def send_kernel(
    me_ref, offset_ref, act_ref, expo_ref, base_ref, received_ref, cot_ref, gain_ref,
    new_rows_ref, received_out_ref, gain_out_ref, *refs,
):
    *packed_refs, rows_ref = refs
    n, rows, _ = rows_ref.shape
    tokens, share = cot_ref.shape
    width = act_ref.shape[1]
    per_dev = width // LANES // n
    received_out_ref[...] = received_ref[...]
    for j in range(n):
        gain_out_ref[j : j + 1, :] = gain_ref[:, j * share : (j + 1) * share]
    first = offset_ref[0] == 0
    down, up = powers(expo_ref[...], -1), powers(expo_ref[...], 1)
    old = [base_ref[p] for p in range(2)]
    chosen = jnp.concatenate([jnp.where(first, o[0:1], o[1:2]) for o in old], axis=0)
    delta = act_ref[...].astype(f32) - chosen
    fill = jnp.full((rows - 2 * per_dev, LANES), offset_ref[0].astype(f32))
    pieces = []
    for b in range(width // LANES):
        scaled = delta[:, b * LANES : (b + 1) * LANES] * down[:, b : b + 1]
        kept = jnp.clip(scaled, -clip_top, clip_top).astype(bf16).astype(f32) * up[:, b : b + 1]
        d, c = divmod(b, per_dev)
        rows_ref[d, 2 * c : 2 * c + 2, :] = kept
        pieces.append(kept)
    for d in range(n):
        rows_ref[d, 2 * per_dev :, :] = fill
    along, _, _ = place(me_ref[0])
    cot = cot_ref[...]
    for r, packed_ref in enumerate(packed_refs):
        to = jnp.bitwise_xor(along, r)
        packed_ref[:, :share] = cot
        for q in range(4):
            packed_ref[block_spot(q, tokens, rows, share)] = rows_ref[4 * to + q].astype(bf16)
    new_rows_ref[...] = chosen + jnp.concatenate(pieces, axis=1)


def sender_base_kernel(offset_ref, rows_ref, base_ref, new_ref):
    first = offset_ref[0] == 0
    for p in range(2):
        row, old = rows_ref[p : p + 1, :], base_ref[p]
        new_ref[p, 0:1, :] = jnp.where(first, row, old[0:1])
        new_ref[p, 1:2, :] = jnp.where(first, old[1:2], row)


def sort_kernel(me_ref, *refs):
    *packed_refs, line_ref, b0, b1, b2, b3 = refs
    quarter, tokens, share = line_ref.shape
    rows = b0.shape[1]
    _, row, core = place(me_ref[0])
    for r, packed_ref in enumerate(packed_refs):
        line_ref[r] = packed_ref[:, :share]
        block = [packed_ref[block_spot(q, tokens, rows, share)] for q in range(4)]
        for e, out_ref in enumerate((b0, b1, b2, b3)):
            to_row, to_core = flip(row, e // 2), flip(core, e % 2)
            low = jnp.where(to_core == 0, block[0], block[1])
            high = jnp.where(to_core == 0, block[2], block[3])
            out_ref[r] = jnp.where(to_row == 0, low, high)


def rebuild_kernel(me_ref, b0, b1, b2, b3, base_ref, out_ref, rows_ref, slots_ref):
    quarter, rows, _ = b0.shape
    n, width = 4 * quarter, base_ref.shape[2]
    whole = out_ref.shape == base_ref.shape
    for e, block_ref in enumerate((b0, b1, b2, b3)):
        for r in range(quarter):
            sender = owner_of(me_ref[0], n, 2 * (e % 2) + e // 2, r)
            rows_ref[pl.ds(pl.multiple_of(sender * rows, rows), rows), :] = block_ref[r].astype(f32)
    per_dev = width // LANES
    first = rows_ref[pl.ds(2 * per_dev, n, stride=rows), :] == 0.0
    for p in range(2):
        for c in range(per_dev):
            cols = slice(c * LANES, (c + 1) * LANES)
            sent = rows_ref[pl.ds(2 * c + p, n, stride=rows), :]
            at = p * per_dev + c
            slots_ref[at] = base_ref[p, :, cols]
            even = slots_ref[at, pl.ds(0, n, stride=2), :]
            odd = slots_ref[at, pl.ds(1, n, stride=2), :]
            rebuilt = jnp.where(first, even, odd) + sent
            if not whole:
                out_ref[p * n : (p + 1) * n, cols] = rebuilt.astype(bf16)
                continue
            slots_ref[at, pl.ds(0, n, stride=2), :] = jnp.where(first, rebuilt, even)
            slots_ref[at, pl.ds(1, n, stride=2), :] = jnp.where(first, odd, rebuilt)
            out_ref[p, :, cols] = slots_ref[at]


def dot_nt(a, b):
    return lax.dot_general(a, b, (((1,), (1,)), ((), ())), preferred_element_type=f32)


def own_rows(piece_ref, own_ref, me, owner):
    n = piece_ref.shape[0] // 2
    for p in range(2):
        own_ref[pl.ds(p * n + owner, 1), :] = piece_ref[pl.ds(p * n + me, 1), :]


def dot_by_halves(rows, tokens):
    middle = tokens.shape[1] // 2 // LANES * LANES
    if middle == 0:
        return dot_nt(rows, tokens)
    return dot_nt(rows[:, :middle], tokens[:, :middle]) + dot_nt(rows[:, middle:], tokens[:, middle:])


def grad_active_kernel(part, me_ref, cot_ref, weight_ref, acc_ref, own_ref, piece_ref):
    quarter, _, width = cot_ref.shape
    me = me_ref[0]
    own_ref[...] = jnp.zeros_like(own_ref)
    for k in range(quarter):
        owner = owner_of(me, 4 * quarter, part, k)
        piece_ref[...] = cot_ref[k].astype(f32)
        own_rows(piece_ref, own_ref, me, owner)
        columns = pl.ds(pl.multiple_of(owner * width, width), width)
        terms = dot_by_halves(weight_ref[:, columns], cot_ref[k])
        acc_ref[...] = terms if k == 0 else acc_ref[...] + terms


def up_kernel(
    part, me_ref, rest_ref, gain_ref, weight_ref, acc_ref, square_ref, own_ref, piece_ref
):
    quarter, _, width = rest_ref.shape
    me = me_ref[0]
    own_ref[...] = jnp.zeros_like(own_ref)
    for k in range(quarter):
        owner = owner_of(me, 4 * quarter, part, k)
        piece = rest_ref[k].astype(f32)
        piece_ref[...] = piece
        own_rows(piece_ref, own_ref, me, owner)
        squares = piece * piece
        total = sum(squares[:, c * LANES : (c + 1) * LANES] for c in range(width // LANES))
        square_ref[...] = total if k == 0 else square_ref[...] + total
        scaled = (piece * gain_ref[pl.ds(owner, 1), :]).astype(bf16)
        rows = pl.ds(pl.multiple_of(owner * width, width), width)
        terms = jnp.dot(scaled, weight_ref[rows, :], preferred_element_type=f32)
        acc_ref[...] = terms if k == 0 else acc_ref[...] + terms


def middle_kernel(me_ref, rest_ref, gain_ref, weight_ref, *refs):
    ins, refs = refs[:10], refs[10:]
    active_ref, own_ref, send_ref, keep_ref, acc_ref, square_ref, piece_ref, rows_ref = refs
    quarter, tokens, width = rest_ref.shape
    half, n, chunks = 2 * quarter, 4 * quarter, width // LANES
    width_all = weight_ref.shape[0]
    me = me_ref[0]
    up_kernel(3, me_ref, rest_ref, gain_ref, weight_ref, acc_ref, square_ref, own_ref, piece_ref)
    product = acc_ref[...] + (ins[0][...] + ins[1][...] + ins[2][...])
    squares = square_ref[...] + (ins[3][...] + ins[4][...] + ins[5][...])
    total = jnp.sum(squares, axis=1, keepdims=True)
    hidden = lax.rsqrt(total / width_all + eps) * product
    sigma = jax.nn.sigmoid(hidden)
    active_ref[...] = (hidden * sigma).astype(bf16)
    grad_active = (ins[6][...] + ins[7][...] + (ins[8][...] + ins[9][...])).T
    gh = (grad_active * sigma * (1.0 + hidden * (1.0 - sigma))).astype(bf16)
    for share in range(n):
        block = weight_ref[share * width : (share + 1) * width, :]
        terms = dot_by_halves(block, gh).T
        for p in range(2):
            for c in range(chunks):
                rows_ref[c, pl.ds(p * n + share, n, stride=tokens), :] = terms[
                    p * n : (p + 1) * n, c * LANES : (c + 1) * LANES
                ]
    core = lax.rem(me, 2)
    for k in range(half):
        keep_at = pl.multiple_of((2 * k + core) * tokens, tokens)
        send_at = pl.multiple_of((2 * k + 1 - core) * tokens, tokens)
        for c in range(chunks):
            cols = slice(c * LANES, (c + 1) * LANES)
            keep_ref[k, :, cols] = rows_ref[c, pl.ds(keep_at, tokens), :].astype(bf16)
            send_ref[k, :, cols] = rows_ref[c, pl.ds(send_at, tokens), :].astype(bf16)


def down_kernel(other, me_ref, active_ref, weight_ref, after_ref, out_ref):
    half, _, width = out_ref.shape
    core = lax.rem(me_ref[0] + other, 2)

    def share(k):
        columns = pl.ds(pl.multiple_of((2 * k + core) * width, width), width)
        terms = jnp.dot(active_ref[...], weight_ref[:, columns], preferred_element_type=f32)
        out_ref[k] = terms.astype(bf16)

    pl.loop(0, half, unroll=4)(share)


def pair_kernel(me_ref, kept_ref, arrived_ref, *refs):
    ins, (send_ref, keep_ref), shares = (refs[:2], refs[2:4], refs[4:]) if len(refs) > 2 else ((), refs, ())
    quarter = send_ref.shape[0]
    _, row, _ = place(me_ref[0])
    for k in range(quarter):
        for out_ref, at in ((send_ref, 2 * k + 1 - row), (keep_ref, 2 * k + row)):
            out_ref[k] = (kept_ref[at].astype(f32) + arrived_ref[at].astype(f32)).astype(bf16)
    if shares:
        line_kernel(me_ref, *ins, *shares)


def line_kernel(me_ref, kept_ref, arrived_ref, *refs):
    along, _, _ = place(me_ref[0])
    for r, ref in enumerate(refs):
        at = jnp.bitwise_xor(along, r)
        ref[...] = (kept_ref[at].astype(f32) + arrived_ref[at].astype(f32)).astype(bf16)


def added(refs):
    return functools.reduce(lambda a, b: a + b, [ref[...].astype(f32) for ref in refs])


def final_kernel(width_all, share_ref, gain_ref, expo_ref, *refs):
    *refs, layer_ref, grad_ref = refs
    quarter = (len(refs) - 8) // 2
    own_all, cot_all = added(refs[:4]), added(refs[4:8])
    grad, layer = added(refs[8 : 8 + quarter]), added(refs[8 + quarter :])
    layer_ref[...] = (share_ref[...].astype(f32) + layer).astype(bf16)
    n, width = gain_ref.shape
    down, up = powers(expo_ref[...], -1), powers(expo_ref[...], 1)
    gain = gain_ref[...]
    per_dev = width // LANES
    blocks = n * per_dev
    at_row = lax.broadcasted_iota(jnp.int32, (n, blocks), 0)
    at_lane = lax.broadcasted_iota(jnp.int32, (n, blocks), 1)
    for p in range(2):
        rows = slice(p * n, (p + 1) * n)
        own, norm = own_all[rows, :], grad[rows, :]
        inv_rms = lax.rsqrt(jnp.sum(own * own, keepdims=True) / width_all + eps)
        scaled_in = (own * gain).astype(bf16).astype(f32)
        curvature = inv_rms * jnp.sum(scaled_in * norm, keepdims=True)
        correction = curvature * inv_rms * inv_rms / width_all
        value = cot_all[rows, :] + inv_rms * gain * norm - correction * own
        for c in range(per_dev):
            at = at_lane == at_row * per_dev + c
            shrink = jnp.sum(jnp.where(at, down[p : p + 1], 0.0), axis=1, keepdims=True)
            grow = jnp.sum(jnp.where(at, up[p : p + 1], 0.0), axis=1, keepdims=True)
            scaled = value[:, c * LANES : (c + 1) * LANES] * shrink
            kept = jnp.clip(scaled, -clip_top, clip_top).astype(bf16).astype(f32) * grow
            grad_ref[p, pl.ds(c, n, stride=per_dev), :] = kept


def on_device(
    activations,
    sample_ids,
    forward_exponent,
    sender_base,
    receiver_base,
    norm_gain,
    up_weight,
    down_weight,
    cotangent,
    backward_exponent,
    *,
    n,
):
    half, quarter = n // 2, n // 4
    tokens = 2 * n
    width_all, hidden_dev = up_weight.shape
    width = width_all // n
    me = lax.axis_index("dp").astype(jnp.int32)
    me_in = me.reshape(1)

    def shift(x, r):
        return lax.ppermute(x, "dp", [(d, d ^ (4 * r)) for d in range(n)]) if r else x

    def swap(x, bits):
        return lax.ppermute(x, "dp", [(d, d ^ bits) for d in range(n)])

    struct = jax.ShapeDtypeStruct
    share_shape, hidden_shape = (tokens, width), (tokens, hidden_dev)
    line_shape = (quarter, tokens, width)

    def call(kernel, outs, ins, args, scratch=(), micros=0.5):
        return pl.pallas_call(
            kernel,
            out_shape=outs,
            in_specs=ins,
            out_specs=jax.tree.map(lambda _: VMEM, outs),
            scratch_shapes=list(scratch),
            compiler_params=params(8),
            cost_estimate=pl.CostEstimate(
                flops=int(micros * FLOPS_PER_MICRO), bytes_accessed=0, transcendentals=0
            ),
        )(*args)

    offset = sample_ids - sender_base.shape[1] * me
    rows = -(-(2 * width // LANES + 1) // 16) * 16
    packed_shape = (tokens, width + LANES * -(-4 * rows // tokens))
    act_shape, expo_shape = (2, width_all), (2, width_all // LANES)
    once = lambda shape: pl.BlockSpec(shape, lambda i: (0,) * len(shape))
    in_shapes = [act_shape, expo_shape, sender_base.shape, receiver_base.shape, share_shape, (1, width_all)]
    outs = (
        struct(act_shape, f32),
        struct(receiver_base.shape, f32),
        struct((n, width), f32),
    ) + (struct(packed_shape, bf16),) * quarter
    new_rows, received, gain, *packed = pl.pallas_call(
        send_kernel,
        out_shape=outs,
        grid=(1,),
        in_specs=[SMEM, SMEM] + [once(x) for x in in_shapes],
        out_specs=(VMEM,) * len(outs),
        scratch_shapes=[pltpu.VMEM((n, rows, LANES), f32)],
        compiler_params=params(8),
    )(
        me_in,
        offset,
        hbm(activations.reshape(act_shape)),
        hbm(forward_exponent.reshape(expo_shape)),
        hbm(sender_base),
        hbm(receiver_base),
        hbm(cotangent.reshape(share_shape)),
        hbm(norm_gain.reshape(1, width_all)),
    )
    packed = [shift(x, r) for r, x in enumerate(packed)]
    cot_line, *blocks = call(
        sort_kernel,
        (struct(line_shape, bf16),) + (struct((quarter, rows, LANES), bf16),) * 4,
        [SMEM] + [VMEM] * quarter,
        [me_in, *packed],
        micros=STAGE,
    )
    blocks = [blocks[0]] + [swap(blocks[e], e) for e in range(1, 4)]
    cots = [cot_line]

    ANY = pl.BlockSpec(memory_space=pl.ANY)
    share_f32 = struct(share_shape, f32)
    sums = (struct(hidden_shape, f32), struct((tokens, LANES), f32))

    def grad_active_part(part):
        return call(
            functools.partial(grad_active_kernel, part),
            (struct((hidden_dev, tokens), f32), share_f32),
            [SMEM, VMEM, VMEM],
            [me_in, cots[part], down_weight],
            [pltpu.VMEM(share_shape, f32)],
            micros=1.6,
        )

    def up_product_part(part):
        return call(
            functools.partial(up_kernel, part),
            sums + (share_f32,),
            [SMEM] + [VMEM] * 3,
            [me_in, rests[part], gain, up_weight],
            [pltpu.VMEM(share_shape, f32)],
            micros=1.2,
        )

    together = lax.optimization_barrier
    grads = [grad_active_part(0)]
    cot_line, grads[0] = together((cot_line, grads[0]))
    cots.append(swap(cot_line, 2))
    blocks, grads[0] = together((blocks, grads[0]))

    def rebuild(out, micros):
        return call(
            rebuild_kernel,
            out,
            [SMEM] + [VMEM] * 5,
            [me_in, *blocks, received],
            [
                pltpu.VMEM((n * rows, LANES), f32),
                pltpu.VMEM((2 * width // LANES, 2 * n, LANES), f32),
            ],
            micros=micros,
        )

    share = rebuild(struct(share_shape, bf16), STAGE)
    lines = [shift(share, r) for r in range(quarter)]
    grads.append(grad_active_part(1))
    cot_line, cot_row, grads[1] = together((cot_line, cots[1], grads[1]))
    cots += [swap(cot_line, 1), swap(cot_row, 1)]
    lines, grads[1] = together((lines, grads[1]))
    rest_line = jnp.stack(lines)
    rest_row = swap(rest_line, 2)
    rests = [rest_line]
    products = [up_product_part(0)]
    rest_line, products[0] = together((rest_line, products[0]))
    rest_line_other = swap(rest_line, 1)
    grads.append(grad_active_part(2))
    new_receiver_base = rebuild(struct(receiver_base.shape, f32), 0.7)
    new_sender_base = call(
        sender_base_kernel,
        struct(sender_base.shape, f32),
        [SMEM] + [VMEM] * 2,
        [offset, new_rows, sender_base],
    )
    rest_row, grads[2], new_sender_base, new_receiver_base = together(
        (rest_row, grads[2], new_sender_base, new_receiver_base)
    )
    rests += [rest_row, rest_line_other, swap(rest_row, 1)]
    grads.append(grad_active_part(3))
    products += [up_product_part(1), up_product_part(2)]
    gas, own_cots = zip(*grads)
    accs, squares, owns = map(list, zip(*products))

    half_out = struct((half, tokens, width), bf16)
    active, own, grad_send, grad_keep = call(
        middle_kernel,
        (struct(hidden_shape, bf16), share_f32, half_out, half_out),
        [SMEM] + [VMEM] * 13,
        [me_in, rests[3], gain, up_weight, *accs, *squares, *gas],
        [pltpu.VMEM(x.shape, x.dtype) for x in sums]
        + [
            pltpu.VMEM(share_shape, f32),
            pltpu.VMEM((width // LANES, n * tokens, LANES), f32),
        ],
        micros=6.5,
    )
    owns.append(own)

    def down_terms(other, after):
        return call(
            functools.partial(down_kernel, other),
            half_out,
            [SMEM] + [VMEM] * 2 + [ANY],
            [me_in, active, down_weight, after],
            micros=1.5,
        )

    pair_out = (struct(line_shape, bf16),) * 2
    line_out = (struct(share_shape, bf16),) * quarter
    grad_in = swap(grad_send, 1)
    out_in = swap(down_terms(1, grad_send), 1)
    grad_send, grad_row = call(
        pair_kernel, pair_out, [SMEM] + [VMEM] * 2, [me_in, grad_keep, grad_in]
    )
    grad_row_in = swap(grad_send, 2)
    out_send, out_row, *grad_line = call(
        pair_kernel,
        pair_out + line_out,
        [SMEM] + [VMEM] * 4,
        [me_in, down_terms(0, grad_send), out_in, grad_row, grad_row_in],
    )
    out_row_in = swap(out_send, 2)
    grad_line = [shift(x, r) for r, x in enumerate(grad_line)]
    out_line = call(line_kernel, line_out, [SMEM] + [VMEM] * 2, [me_in, out_row, out_row_in])
    out_line = [shift(x, r) for r, x in enumerate(out_line)]
    layer_out, returned = call(
        functools.partial(final_kernel, width_all),
        (struct(share_shape, bf16), struct((2, width_all // LANES, LANES), f32)),
        [VMEM] * (11 + 2 * quarter),
        [
            share,
            gain,
            backward_exponent.reshape(expo_shape),
            *owns,
            *own_cots,
            *grad_line,
            *out_line,
        ],
    )
    return (
        new_sender_base,
        new_receiver_base,
        layer_out.reshape(2, n, width),
        returned.reshape(2, 1, width_all),
    )


def solution(mesh):
    placed = (
        P(None, ("groups", "dp"), None),
        P(("groups", "dp")),
        P(None, ("groups", "dp"), None),
        P(None, ("groups", "dp"), None),
        P(None, "groups", "dp"),
        P(),
        P(None, "dp"),
        P("dp", None),
        P(None, "groups", "dp"),
        P(None, ("groups", "dp"), None),
    )
    return jax.shard_map(
        functools.partial(on_device, n=mesh.shape["dp"]),
        mesh=mesh,
        in_specs=placed,
        out_specs=(
            P(None, ("groups", "dp"), None),
            P(None, "groups", "dp"),
            P(None, "groups", "dp"),
            P(None, ("groups", "dp"), None),
        ),
        check_vma=False,
    )
```

```python
import functools

import jax
import jax.numpy as jnp
from jax import lax
from jax.experimental import pallas as pl
from jax.experimental.pallas import tpu as pltpu
from jax.sharding import PartitionSpec as P

clip_top = 448.0
eps = 1e-05
LANES = 128
STAGE = 4
FLOPS_PER_MICRO = 1.15e9
f32 = jnp.float32
bf16 = jnp.bfloat16
VMEM = pl.BlockSpec(memory_space=pltpu.VMEM)
SMEM = pl.BlockSpec(memory_space=pltpu.SMEM)


def hbm(x):
    return pltpu.with_memory_space_constraint(x, pltpu.HBM)


def powers(exponent, sign):
    total = jnp.zeros(exponent.shape, f32)
    for level in range(-10, 1):
        total = jnp.where(exponent == level, f32(2.0 ** (sign * level)), total)
    return total


def params(megabytes):
    return pltpu.CompilerParams(vmem_limit_bytes=megabytes << 20)


def flip(bit, by):
    return lax.rem(bit + by, 2)


def place(me):
    return me // 4, lax.rem(me // 2, 2), lax.rem(me, 2)


def owner_of(me, n, part, back):
    along, row, core = place(me)
    at = jnp.bitwise_xor(along, back)
    return 4 * at + 2 * flip(row, part % 2) + flip(core, part // 2)


def block_spot(q, tokens, rows, width):
    per_column = tokens // rows
    r, c = rows * (q % per_column), width + LANES * (q // per_column)
    return slice(r, r + rows), slice(c, c + LANES)


def send_kernel(
    me_ref, offset_ref, act_ref, expo_ref, base_ref, received_ref, cot_ref, gain_ref,
    new_rows_ref, received_out_ref, gain_out_ref, *refs,
):
    *packed_refs, rows_ref = refs
    n, rows, _ = rows_ref.shape
    tokens, share = cot_ref.shape
    width = act_ref.shape[1]
    per_dev = width // LANES // n
    received_out_ref[...] = received_ref[...]
    for j in range(n):
        gain_out_ref[j : j + 1, :] = gain_ref[:, j * share : (j + 1) * share]
    first = offset_ref[0] == 0
    down, up = powers(expo_ref[...], -1), powers(expo_ref[...], 1)
    old = [base_ref[p] for p in range(2)]
    chosen = jnp.concatenate([jnp.where(first, o[0:1], o[1:2]) for o in old], axis=0)
    delta = act_ref[...].astype(f32) - chosen
    fill = jnp.full((rows - 2 * per_dev, LANES), offset_ref[0].astype(f32))
    pieces = []
    for b in range(width // LANES):
        scaled = delta[:, b * LANES : (b + 1) * LANES] * down[:, b : b + 1]
        kept = jnp.clip(scaled, -clip_top, clip_top).astype(bf16).astype(f32) * up[:, b : b + 1]
        d, c = divmod(b, per_dev)
        rows_ref[d, 2 * c : 2 * c + 2, :] = kept
        pieces.append(kept)
    for d in range(n):
        rows_ref[d, 2 * per_dev :, :] = fill
    along, _, _ = place(me_ref[0])
    cot = cot_ref[...]
    for r, packed_ref in enumerate(packed_refs):
        to = jnp.bitwise_xor(along, r)
        packed_ref[:, :share] = cot
        for q in range(4):
            packed_ref[block_spot(q, tokens, rows, share)] = rows_ref[4 * to + q].astype(bf16)
    new_rows_ref[...] = chosen + jnp.concatenate(pieces, axis=1)


def sender_base_kernel(offset_ref, rows_ref, base_ref, new_ref):
    first = offset_ref[0] == 0
    for p in range(2):
        row, old = rows_ref[p : p + 1, :], base_ref[p]
        new_ref[p, 0:1, :] = jnp.where(first, row, old[0:1])
        new_ref[p, 1:2, :] = jnp.where(first, old[1:2], row)


def sort_kernel(me_ref, *refs):
    *packed_refs, line_ref, b0, b1, b2, b3 = refs
    quarter, tokens, share = line_ref.shape
    rows = b0.shape[1]
    _, row, core = place(me_ref[0])
    for r, packed_ref in enumerate(packed_refs):
        line_ref[r] = packed_ref[:, :share]
        block = [packed_ref[block_spot(q, tokens, rows, share)] for q in range(4)]
        for e, out_ref in enumerate((b0, b1, b2, b3)):
            to_row, to_core = flip(row, e // 2), flip(core, e % 2)
            low = jnp.where(to_core == 0, block[0], block[1])
            high = jnp.where(to_core == 0, block[2], block[3])
            out_ref[r] = jnp.where(to_row == 0, low, high)


def rebuild_kernel(me_ref, b0, b1, b2, b3, base_ref, out_ref, rows_ref, slots_ref):
    quarter, rows, _ = b0.shape
    n, width = 4 * quarter, base_ref.shape[2]
    whole = out_ref.shape == base_ref.shape
    for e, block_ref in enumerate((b0, b1, b2, b3)):
        for r in range(quarter):
            sender = owner_of(me_ref[0], n, 2 * (e % 2) + e // 2, r)
            rows_ref[pl.ds(pl.multiple_of(sender * rows, rows), rows), :] = block_ref[r].astype(f32)
    per_dev = width // LANES
    first = rows_ref[pl.ds(2 * per_dev, n, stride=rows), :] == 0.0
    for p in range(2):
        for c in range(per_dev):
            cols = slice(c * LANES, (c + 1) * LANES)
            sent = rows_ref[pl.ds(2 * c + p, n, stride=rows), :]
            at = p * per_dev + c
            slots_ref[at] = base_ref[p, :, cols]
            even = slots_ref[at, pl.ds(0, n, stride=2), :]
            odd = slots_ref[at, pl.ds(1, n, stride=2), :]
            rebuilt = jnp.where(first, even, odd) + sent
            if not whole:
                out_ref[p * n : (p + 1) * n, cols] = rebuilt.astype(bf16)
                continue
            slots_ref[at, pl.ds(0, n, stride=2), :] = jnp.where(first, rebuilt, even)
            slots_ref[at, pl.ds(1, n, stride=2), :] = jnp.where(first, odd, rebuilt)
            out_ref[p, :, cols] = slots_ref[at]


def dot_nt(a, b):
    return lax.dot_general(a, b, (((1,), (1,)), ((), ())), preferred_element_type=f32)


def own_rows(piece_ref, own_ref, me, owner):
    n = piece_ref.shape[0] // 2
    for p in range(2):
        own_ref[pl.ds(p * n + owner, 1), :] = piece_ref[pl.ds(p * n + me, 1), :]


def dot_by_halves(rows, tokens):
    middle = tokens.shape[1] // 2 // LANES * LANES
    if middle == 0:
        return dot_nt(rows, tokens)
    return dot_nt(rows[:, :middle], tokens[:, :middle]) + dot_nt(rows[:, middle:], tokens[:, middle:])


def grad_active_kernel(part, me_ref, cot_ref, weight_ref, acc_ref, own_ref, piece_ref):
    quarter, _, width = cot_ref.shape
    me = me_ref[0]
    own_ref[...] = jnp.zeros_like(own_ref)
    for k in range(quarter):
        owner = owner_of(me, 4 * quarter, part, k)
        piece_ref[...] = cot_ref[k].astype(f32)
        own_rows(piece_ref, own_ref, me, owner)
        columns = pl.ds(pl.multiple_of(owner * width, width), width)
        terms = dot_by_halves(weight_ref[:, columns], cot_ref[k])
        acc_ref[...] = terms if k == 0 else acc_ref[...] + terms


def up_kernel(
    part, me_ref, rest_ref, gain_ref, weight_ref, acc_ref, square_ref, own_ref, piece_ref
):
    quarter, _, width = rest_ref.shape
    me = me_ref[0]
    own_ref[...] = jnp.zeros_like(own_ref)
    for k in range(quarter):
        owner = owner_of(me, 4 * quarter, part, k)
        piece = rest_ref[k].astype(f32)
        piece_ref[...] = piece
        own_rows(piece_ref, own_ref, me, owner)
        squares = piece * piece
        total = sum(squares[:, c * LANES : (c + 1) * LANES] for c in range(width // LANES))
        square_ref[...] = total if k == 0 else square_ref[...] + total
        scaled = (piece * gain_ref[pl.ds(owner, 1), :]).astype(bf16)
        rows = pl.ds(pl.multiple_of(owner * width, width), width)
        terms = jnp.dot(scaled, weight_ref[rows, :], preferred_element_type=f32)
        acc_ref[...] = terms if k == 0 else acc_ref[...] + terms


def activation_kernel(me_ref, rest_ref, gain_ref, weight_ref, *refs):
    ins, refs = refs[:10], refs[10:]
    active_ref, gh_ref, own_ref, acc_ref, square_ref, piece_ref = refs
    up_kernel(3, me_ref, rest_ref, gain_ref, weight_ref, acc_ref, square_ref, own_ref, piece_ref)
    product = acc_ref[...] + (ins[0][...] + ins[1][...] + ins[2][...])
    squares = square_ref[...] + (ins[3][...] + ins[4][...] + ins[5][...])
    total = jnp.sum(squares, axis=1, keepdims=True)
    hidden = lax.rsqrt(total / weight_ref.shape[0] + eps) * product
    sigma = jax.nn.sigmoid(hidden)
    active_ref[...] = (hidden * sigma).astype(bf16)
    grad_active = (ins[6][...] + ins[7][...] + (ins[8][...] + ins[9][...])).T
    gh_ref[...] = (grad_active * sigma * (1.0 + hidden * (1.0 - sigma))).astype(bf16)


def grad_norm_kernel(first, last, me_ref, gh_ref, weight_ref, *refs):
    if first:
        rows_in_ref, send_ref, keep_ref, rows_ref = refs
        rows_ref[...] = rows_in_ref[...]
    else:
        (rows_ref,) = refs
    chunks = rows_ref.shape[0]
    tokens, width = gh_ref.shape[0], chunks * LANES
    half, n = tokens // 4, tokens // 2
    gh = gh_ref[...]
    for share in range(first, last):
        block = weight_ref[share * width : (share + 1) * width, :]
        terms = dot_by_halves(block, gh).T
        for p in range(2):
            for c in range(chunks):
                rows_ref[c, pl.ds(p * n + share, n, stride=tokens), :] = terms[
                    p * n : (p + 1) * n, c * LANES : (c + 1) * LANES
                ]
    if last < n:
        return
    core = lax.rem(me_ref[0], 2)
    for k in range(half):
        keep_at = pl.multiple_of((2 * k + core) * tokens, tokens)
        send_at = pl.multiple_of((2 * k + 1 - core) * tokens, tokens)
        for c in range(chunks):
            cols = slice(c * LANES, (c + 1) * LANES)
            keep_ref[k, :, cols] = rows_ref[c, pl.ds(keep_at, tokens), :].astype(bf16)
            send_ref[k, :, cols] = rows_ref[c, pl.ds(send_at, tokens), :].astype(bf16)


def down_kernel(other, me_ref, active_ref, weight_ref, out_ref):
    half, _, width = out_ref.shape
    core = lax.rem(me_ref[0] + other, 2)

    def share(k):
        columns = pl.ds(pl.multiple_of((2 * k + core) * width, width), width)
        terms = jnp.dot(active_ref[...], weight_ref[:, columns], preferred_element_type=f32)
        out_ref[k] = terms.astype(bf16)

    pl.loop(0, half, unroll=4)(share)


def pair_kernel(me_ref, kept_ref, arrived_ref, send_ref, keep_ref):
    _, row, _ = place(me_ref[0])
    for k in range(send_ref.shape[0]):
        for out_ref, at in ((send_ref, 2 * k + 1 - row), (keep_ref, 2 * k + row)):
            out_ref[k] = (kept_ref[at].astype(f32) + arrived_ref[at].astype(f32)).astype(bf16)


def line_kernel(me_ref, kept_ref, arrived_ref, *refs):
    along, _, _ = place(me_ref[0])
    for r, ref in enumerate(refs):
        at = jnp.bitwise_xor(along, r)
        ref[...] = (kept_ref[at].astype(f32) + arrived_ref[at].astype(f32)).astype(bf16)


def added(refs):
    return functools.reduce(lambda a, b: a + b, [ref[...].astype(f32) for ref in refs])


def final_kernel(width_all, share_ref, gain_ref, expo_ref, *refs):
    *refs, layer_ref, grad_ref = refs
    quarter = (len(refs) - 8) // 2
    own_all, cot_all = added(refs[:4]), added(refs[4:8])
    grad, layer = added(refs[8 : 8 + quarter]), added(refs[8 + quarter :])
    layer_ref[...] = (share_ref[...].astype(f32) + layer).astype(bf16)
    n, width = gain_ref.shape
    down, up = powers(expo_ref[...], -1), powers(expo_ref[...], 1)
    gain = gain_ref[...]
    per_dev = width // LANES
    blocks = n * per_dev
    at_row = lax.broadcasted_iota(jnp.int32, (n, blocks), 0)
    at_lane = lax.broadcasted_iota(jnp.int32, (n, blocks), 1)
    for p in range(2):
        rows = slice(p * n, (p + 1) * n)
        own, norm = own_all[rows, :], grad[rows, :]
        inv_rms = lax.rsqrt(jnp.sum(own * own, keepdims=True) / width_all + eps)
        scaled_in = (own * gain).astype(bf16).astype(f32)
        curvature = inv_rms * jnp.sum(scaled_in * norm, keepdims=True)
        correction = curvature * inv_rms * inv_rms / width_all
        value = cot_all[rows, :] + inv_rms * gain * norm - correction * own
        for c in range(per_dev):
            at = at_lane == at_row * per_dev + c
            shrink = jnp.sum(jnp.where(at, down[p : p + 1], 0.0), axis=1, keepdims=True)
            grow = jnp.sum(jnp.where(at, up[p : p + 1], 0.0), axis=1, keepdims=True)
            scaled = value[:, c * LANES : (c + 1) * LANES] * shrink
            kept = jnp.clip(scaled, -clip_top, clip_top).astype(bf16).astype(f32) * grow
            grad_ref[p, pl.ds(c, n, stride=per_dev), :] = kept


def on_device(
    activations,
    sample_ids,
    forward_exponent,
    sender_base,
    receiver_base,
    norm_gain,
    up_weight,
    down_weight,
    cotangent,
    backward_exponent,
    *,
    n,
):
    half, quarter = n // 2, n // 4
    tokens = 2 * n
    width_all, hidden_dev = up_weight.shape
    width = width_all // n
    me = lax.axis_index("dp").astype(jnp.int32)
    me_in = me.reshape(1)

    def shift(x, r):
        return lax.ppermute(x, "dp", [(d, d ^ (4 * r)) for d in range(n)]) if r else x

    def swap(x, bits):
        return lax.ppermute(x, "dp", [(d, d ^ bits) for d in range(n)])

    struct = jax.ShapeDtypeStruct
    share_shape, hidden_shape = (tokens, width), (tokens, hidden_dev)
    line_shape = (quarter, tokens, width)

    def call(kernel, outs, ins, args, scratch=(), micros=0.5):
        return pl.pallas_call(
            kernel,
            out_shape=outs,
            in_specs=ins,
            out_specs=jax.tree.map(lambda _: VMEM, outs),
            scratch_shapes=list(scratch),
            compiler_params=params(8),
            cost_estimate=pl.CostEstimate(
                flops=int(micros * FLOPS_PER_MICRO), bytes_accessed=0, transcendentals=0
            ),
        )(*args)

    offset = sample_ids - sender_base.shape[1] * me
    rows = -(-(2 * width // LANES + 1) // 16) * 16
    packed_shape = (tokens, width + LANES * -(-4 * rows // tokens))
    act_shape, expo_shape = (2, width_all), (2, width_all // LANES)
    once = lambda shape: pl.BlockSpec(shape, lambda i: (0,) * len(shape))
    in_shapes = [act_shape, expo_shape, sender_base.shape, receiver_base.shape, share_shape, (1, width_all)]
    outs = (
        struct(act_shape, f32),
        struct(receiver_base.shape, f32),
        struct((n, width), f32),
    ) + (struct(packed_shape, bf16),) * quarter
    new_rows, received, gain, *packed = pl.pallas_call(
        send_kernel,
        out_shape=outs,
        grid=(1,),
        in_specs=[SMEM, SMEM] + [once(x) for x in in_shapes],
        out_specs=(VMEM,) * len(outs),
        scratch_shapes=[pltpu.VMEM((n, rows, LANES), f32)],
        compiler_params=params(8),
    )(
        me_in,
        offset,
        hbm(activations.reshape(act_shape)),
        hbm(forward_exponent.reshape(expo_shape)),
        hbm(sender_base),
        hbm(receiver_base),
        hbm(cotangent.reshape(share_shape)),
        hbm(norm_gain.reshape(1, width_all)),
    )
    packed = [shift(x, r) for r, x in enumerate(packed)]
    cot_line, *blocks = call(
        sort_kernel,
        (struct(line_shape, bf16),) + (struct((quarter, rows, LANES), bf16),) * 4,
        [SMEM] + [VMEM] * quarter,
        [me_in, *packed],
        micros=STAGE,
    )
    blocks = [blocks[0]] + [swap(blocks[e], e) for e in range(1, 4)]
    cots = [cot_line]

    ANY = pl.BlockSpec(memory_space=pl.ANY)
    share_f32 = struct(share_shape, f32)
    sums = (struct(hidden_shape, f32), struct((tokens, LANES), f32))

    def grad_active_part(part):
        return call(
            functools.partial(grad_active_kernel, part),
            (struct((hidden_dev, tokens), f32), share_f32),
            [SMEM, VMEM, VMEM],
            [me_in, cots[part], down_weight],
            [pltpu.VMEM(share_shape, f32)],
            micros=1.6,
        )

    def up_product_part(part):
        return call(
            functools.partial(up_kernel, part),
            sums + (share_f32,),
            [SMEM] + [VMEM] * 3,
            [me_in, rests[part], gain, up_weight],
            [pltpu.VMEM(share_shape, f32)],
            micros=1.2,
        )

    together = lax.optimization_barrier
    def rebuild(out, micros):
        return call(
            rebuild_kernel,
            out,
            [SMEM] + [VMEM] * 5,
            [me_in, *blocks, received],
            [
                pltpu.VMEM((n * rows, LANES), f32),
                pltpu.VMEM((2 * width // LANES, 2 * n, LANES), f32),
            ],
            micros=micros,
        )

    share = rebuild(struct(share_shape, bf16), STAGE)
    lines = [shift(share, r) for r in range(quarter)]
    cots[0], share_after = together((cot_line, share))
    cot_row = swap(cots[0], 2)
    grads = [grad_active_part(0)]
    new_receiver_base = rebuild(struct(receiver_base.shape, f32), 0.7)
    lines, grads[0], new_receiver_base = together((lines, grads[0], new_receiver_base))
    rest_line = jnp.stack(lines)
    rest_row = swap(rest_line, 2)
    rests = [rest_line]
    products = [up_product_part(0)]
    rest_line, cot_line, cot_row, products[0] = together((rest_line, cots[0], cot_row, products[0]))
    rest_line_other = swap(rest_line, 1)
    cots += [cot_row, swap(cot_line, 1)]
    grads += [grad_active_part(1), grad_active_part(2)]
    new_sender_base = call(
        sender_base_kernel,
        struct(sender_base.shape, f32),
        [SMEM] + [VMEM] * 2,
        [offset, new_rows, sender_base],
    )
    rest_row, cot_row, grads[1], grads[2], new_sender_base = together(
        (rest_row, cot_row, grads[1], grads[2], new_sender_base)
    )
    rests += [rest_row, rest_line_other, swap(rest_row, 1)]
    cots.append(swap(cot_row, 1))
    grads.append(grad_active_part(3))
    products += [up_product_part(1), up_product_part(2)]
    gas, own_cots = zip(*grads)
    accs, squares, owns = map(list, zip(*products))

    half_out = struct((half, tokens, width), bf16)
    active, grad_hidden, own = call(
        activation_kernel,
        (struct(hidden_shape, bf16), struct(hidden_shape, bf16), share_f32),
        [SMEM] + [VMEM] * 13,
        [me_in, rests[3], gain, up_weight, *accs, *squares, *gas],
        [pltpu.VMEM(x.shape, x.dtype) for x in sums] + [pltpu.VMEM(share_shape, f32)],
        micros=1.5,
    )
    owns.append(own)

    def down_terms(other, active):
        return call(
            functools.partial(down_kernel, other),
            half_out,
            [SMEM] + [VMEM] * 2,
            [me_in, active, down_weight],
            micros=1.5,
        )

    def pair_sum(kept, arrived):
        return call(
            pair_kernel,
            (struct(line_shape, bf16),) * 2,
            [SMEM] + [VMEM] * 2,
            [me_in, kept, arrived],
        )

    def line_sum(kept, arrived):
        shares = call(
            line_kernel,
            (struct(share_shape, bf16),) * quarter,
            [SMEM] + [VMEM] * 2,
            [me_in, kept, arrived],
        )
        return [shift(x, r) for r, x in enumerate(shares)]

    out_send = down_terms(1, active)
    out_in = swap(out_send, 1)
    active, out_send = together((active, out_send))
    out_send, out_row = pair_sum(down_terms(0, active), out_in)
    out_row_in = swap(out_send, 2)
    grad_hidden, out_row = together((grad_hidden, out_row))
    rows_out = struct((width // LANES, n * tokens, LANES), f32)
    most = n - n // 8
    grad_rows = call(
        functools.partial(grad_norm_kernel, 0, most),
        rows_out,
        [SMEM] + [VMEM] * 2,
        [me_in, grad_hidden, up_weight],
        micros=4,
    )
    grad_rows, out_row_in = together((grad_rows, out_row_in))
    grad_send, grad_keep = call(
        functools.partial(grad_norm_kernel, most, n),
        (half_out, half_out),
        [SMEM] + [VMEM] * 3,
        [me_in, grad_hidden, up_weight, grad_rows],
        [pltpu.VMEM(rows_out.shape, f32)],
        micros=0.7,
    )
    grad_in = swap(grad_send, 1)
    grad_send, grad_row = pair_sum(grad_keep, grad_in)
    grad_row_in = swap(grad_send, 2)
    out_row, grad_row = together((out_row, grad_row))
    out_line = line_sum(out_row, out_row_in)
    grad_line = line_sum(grad_row, grad_row_in)
    layer_out, returned = call(
        functools.partial(final_kernel, width_all),
        (struct(share_shape, bf16), struct((2, width_all // LANES, LANES), f32)),
        [VMEM] * (11 + 2 * quarter),
        [
            share,
            gain,
            backward_exponent.reshape(expo_shape),
            *owns,
            *own_cots,
            *grad_line,
            *out_line,
        ],
    )
    return (
        new_sender_base,
        new_receiver_base,
        layer_out.reshape(2, n, width),
        returned.reshape(2, 1, width_all),
    )


def solution(mesh):
    placed = (
        P(None, ("groups", "dp"), None),
        P(("groups", "dp")),
        P(None, ("groups", "dp"), None),
        P(None, ("groups", "dp"), None),
        P(None, "groups", "dp"),
        P(),
        P(None, "dp"),
        P("dp", None),
        P(None, "groups", "dp"),
        P(None, ("groups", "dp"), None),
    )
    return jax.shard_map(
        functools.partial(on_device, n=mesh.shape["dp"]),
        mesh=mesh,
        in_specs=placed,
        out_specs=(
            P(None, ("groups", "dp"), None),
            P(None, "groups", "dp"),
            P(None, "groups", "dp"),
            P(None, ("groups", "dp"), None),
        ),
        check_vma=False,
    )
```

```python
import functools

import jax
import jax.numpy as jnp
from jax import lax
from jax.experimental import pallas as pl
from jax.experimental.pallas import tpu as pltpu
from jax.sharding import PartitionSpec as P

clip_top = 448.0
eps = 1e-05
LANES = 128
STAGE = 4
FLOPS_PER_MICRO = 1.15e9
f32 = jnp.float32
bf16 = jnp.bfloat16
VMEM = pl.BlockSpec(memory_space=pltpu.VMEM)
SMEM = pl.BlockSpec(memory_space=pltpu.SMEM)


def hbm(x):
    return pltpu.with_memory_space_constraint(x, pltpu.HBM)


def powers(exponent, sign):
    total = jnp.zeros(exponent.shape, f32)
    for level in range(-10, 1):
        total = jnp.where(exponent == level, f32(2.0 ** (sign * level)), total)
    return total


def params(megabytes):
    return pltpu.CompilerParams(vmem_limit_bytes=megabytes << 20)


def flip(bit, by):
    return lax.rem(bit + by, 2)


def place(me):
    return me // 4, lax.rem(me // 2, 2), lax.rem(me, 2)


def owner_of(me, n, part, back):
    along, row, core = place(me)
    at = jnp.bitwise_xor(along, back)
    return 4 * at + 2 * flip(row, part % 2) + flip(core, part // 2)


def send_kernel(
    me_ref, offset_ref, act_ref, expo_ref, base_ref, received_ref, gain_ref,
    new_rows_ref, received_out_ref, gain_out_ref, *refs,
):
    *packed_refs, rows_ref = refs
    n, rows, _ = rows_ref.shape
    width = act_ref.shape[1]
    share = width // n
    per_dev = width // LANES // n
    received_out_ref[...] = received_ref[...]
    for j in range(n):
        gain_out_ref[j : j + 1, :] = gain_ref[:, j * share : (j + 1) * share]
    first = offset_ref[0] == 0
    down, up = powers(expo_ref[...], -1), powers(expo_ref[...], 1)
    old = [base_ref[p] for p in range(2)]
    chosen = jnp.concatenate([jnp.where(first, o[0:1], o[1:2]) for o in old], axis=0)
    delta = act_ref[...].astype(f32) - chosen
    fill = jnp.full((rows - 2 * per_dev, LANES), offset_ref[0].astype(f32))
    pieces = []
    for b in range(width // LANES):
        scaled = delta[:, b * LANES : (b + 1) * LANES] * down[:, b : b + 1]
        kept = jnp.clip(scaled, -clip_top, clip_top).astype(bf16).astype(f32) * up[:, b : b + 1]
        d, c = divmod(b, per_dev)
        rows_ref[d, 2 * c : 2 * c + 2, :] = kept
        pieces.append(kept)
    for d in range(n):
        rows_ref[d, 2 * per_dev :, :] = fill
    along, _, _ = place(me_ref[0])
    for r, packed_ref in enumerate(packed_refs):
        to = jnp.bitwise_xor(along, r)
        for q in range(4):
            packed_ref[q] = rows_ref[4 * to + q].astype(bf16)
    new_rows_ref[...] = chosen + jnp.concatenate(pieces, axis=1)


def sender_base_kernel(offset_ref, rows_ref, base_ref, new_ref):
    first = offset_ref[0] == 0
    for p in range(2):
        row, old = rows_ref[p : p + 1, :], base_ref[p]
        new_ref[p, 0:1, :] = jnp.where(first, row, old[0:1])
        new_ref[p, 1:2, :] = jnp.where(first, old[1:2], row)


def sort_kernel(me_ref, *refs):
    *packed_refs, b0, b1, b2, b3 = refs
    _, row, core = place(me_ref[0])
    for r, packed_ref in enumerate(packed_refs):
        for e, out_ref in enumerate((b0, b1, b2, b3)):
            out_ref[r] = packed_ref[2 * flip(row, e // 2) + flip(core, e % 2)]


def interleave_kernel(a_ref, b_ref, out_ref):
    for k in range(a_ref.shape[0]):
        out_ref[2 * k], out_ref[2 * k + 1] = a_ref[k], b_ref[k]


def rebuild_kernel(me_ref, b0, b1, b2, b3, base_ref, out_ref, rows_ref, slots_ref):
    quarter, rows, _ = b0.shape
    n, width = 4 * quarter, base_ref.shape[2]
    whole = out_ref.shape == base_ref.shape
    for e, block_ref in enumerate((b0, b1, b2, b3)):
        for r in range(quarter):
            sender = owner_of(me_ref[0], n, 2 * (e % 2) + e // 2, r)
            rows_ref[pl.ds(pl.multiple_of(sender * rows, rows), rows), :] = block_ref[r].astype(f32)
    per_dev = width // LANES
    first = rows_ref[pl.ds(2 * per_dev, n, stride=rows), :] == 0.0
    for p in range(2):
        for c in range(per_dev):
            cols = slice(c * LANES, (c + 1) * LANES)
            sent = rows_ref[pl.ds(2 * c + p, n, stride=rows), :]
            at = p * per_dev + c
            slots_ref[at] = base_ref[p, :, cols]
            even = slots_ref[at, pl.ds(0, n, stride=2), :]
            odd = slots_ref[at, pl.ds(1, n, stride=2), :]
            rebuilt = jnp.where(first, even, odd) + sent
            if not whole:
                out_ref[p * n : (p + 1) * n, cols] = rebuilt.astype(bf16)
                continue
            slots_ref[at, pl.ds(0, n, stride=2), :] = jnp.where(first, rebuilt, even)
            slots_ref[at, pl.ds(1, n, stride=2), :] = jnp.where(first, odd, rebuilt)
            out_ref[p, :, cols] = slots_ref[at]


def dot_nt(a, b):
    return lax.dot_general(a, b, (((1,), (1,)), ((), ())), preferred_element_type=f32)


def own_rows(piece_ref, own_ref, me, owner):
    n = piece_ref.shape[0] // 2
    for p in range(2):
        own_ref[pl.ds(p * n + owner, 1), :] = piece_ref[pl.ds(p * n + me, 1), :]


def dot_by_halves(rows, tokens):
    middle = tokens.shape[1] // 2 // LANES * LANES
    if middle == 0:
        return dot_nt(rows, tokens)
    return dot_nt(rows[:, :middle], tokens[:, :middle]) + dot_nt(rows[:, middle:], tokens[:, middle:])


def grad_active_kernel(part, me_ref, cot_ref, weight_ref, acc_ref, own_ref, piece_ref):
    quarter, _, width = cot_ref.shape
    me = me_ref[0]
    own_ref[...] = jnp.zeros_like(own_ref)
    for k in range(quarter):
        owner = owner_of(me, 4 * quarter, part, k)
        piece_ref[...] = cot_ref[k].astype(f32)
        own_rows(piece_ref, own_ref, me, owner)
        columns = pl.ds(pl.multiple_of(owner * width, width), width)
        terms = dot_by_halves(weight_ref[:, columns], cot_ref[k])
        acc_ref[...] = terms if k == 0 else acc_ref[...] + terms


def up_kernel(
    part, me_ref, rest_ref, gain_ref, weight_ref, acc_ref, square_ref, own_ref, piece_ref
):
    quarter, _, width = rest_ref.shape
    me = me_ref[0]
    own_ref[...] = jnp.zeros_like(own_ref)
    for k in range(quarter):
        owner = owner_of(me, 4 * quarter, part, k)
        piece = rest_ref[k].astype(f32)
        piece_ref[...] = piece
        own_rows(piece_ref, own_ref, me, owner)
        squares = piece * piece
        total = sum(squares[:, c * LANES : (c + 1) * LANES] for c in range(width // LANES))
        square_ref[...] = total if k == 0 else square_ref[...] + total
        scaled = (piece * gain_ref[pl.ds(owner, 1), :]).astype(bf16)
        rows = pl.ds(pl.multiple_of(owner * width, width), width)
        terms = jnp.dot(scaled, weight_ref[rows, :], preferred_element_type=f32)
        acc_ref[...] = terms if k == 0 else acc_ref[...] + terms


def activation_kernel(me_ref, rest_ref, gain_ref, weight_ref, *refs):
    ins, refs = refs[:10], refs[10:]
    active_ref, gh_ref, own_ref, acc_ref, square_ref, piece_ref = refs
    up_kernel(3, me_ref, rest_ref, gain_ref, weight_ref, acc_ref, square_ref, own_ref, piece_ref)
    product = acc_ref[...] + (ins[0][...] + ins[1][...] + ins[2][...])
    squares = square_ref[...] + (ins[3][...] + ins[4][...] + ins[5][...])
    total = jnp.sum(squares, axis=1, keepdims=True)
    hidden = lax.rsqrt(total / weight_ref.shape[0] + eps) * product
    sigma = jax.nn.sigmoid(hidden)
    active_ref[...] = (hidden * sigma).astype(bf16)
    grad_active = (ins[6][...] + ins[7][...] + (ins[8][...] + ins[9][...])).T
    gh_ref[...] = (grad_active * sigma * (1.0 + hidden * (1.0 - sigma))).astype(bf16)


def grad_norm_kernel(first, last, me_ref, gh_ref, weight_ref, *refs):
    if first:
        rows_in_ref, send_ref, keep_ref, rows_ref = refs
        rows_ref[...] = rows_in_ref[...]
    else:
        (rows_ref,) = refs
    chunks = rows_ref.shape[0]
    tokens, width = gh_ref.shape[0], chunks * LANES
    half, n = tokens // 4, tokens // 2
    gh = gh_ref[...]
    for share in range(first, last):
        block = weight_ref[share * width : (share + 1) * width, :]
        middle = width // 2
        terms = jnp.concatenate([dot_nt(block[:middle], gh), dot_nt(block[middle:], gh)], axis=0).T
        for p in range(2):
            for c in range(chunks):
                rows_ref[c, pl.ds(p * n + share, n, stride=tokens), :] = terms[
                    p * n : (p + 1) * n, c * LANES : (c + 1) * LANES
                ]
    if last < n:
        return
    core = lax.rem(me_ref[0], 2)
    for k in range(half):
        keep_at = pl.multiple_of((2 * k + core) * tokens, tokens)
        send_at = pl.multiple_of((2 * k + 1 - core) * tokens, tokens)
        for c in range(chunks):
            cols = slice(c * LANES, (c + 1) * LANES)
            keep_ref[k, :, cols] = rows_ref[c, pl.ds(keep_at, tokens), :].astype(bf16)
            send_ref[k, :, cols] = rows_ref[c, pl.ds(send_at, tokens), :].astype(bf16)


def down_kernel(other, me_ref, active_ref, weight_ref, out_ref):
    half, _, width = out_ref.shape
    core = lax.rem(me_ref[0] + other, 2)

    def share(k):
        columns = pl.ds(pl.multiple_of((2 * k + core) * width, width), width)
        terms = jnp.dot(active_ref[...], weight_ref[:, columns], preferred_element_type=f32)
        out_ref[k] = terms.astype(bf16)

    pl.loop(0, half, unroll=4)(share)


def pair_kernel(me_ref, kept_ref, arrived_ref, send_ref, keep_ref):
    _, row, _ = place(me_ref[0])
    for k in range(send_ref.shape[0]):
        for out_ref, at in ((send_ref, 2 * k + 1 - row), (keep_ref, 2 * k + row)):
            out_ref[k] = (kept_ref[at].astype(f32) + arrived_ref[at].astype(f32)).astype(bf16)


def line_kernel(me_ref, kept_ref, arrived_ref, send_ref, keep_ref):
    along, _, _ = place(me_ref[0])
    for k in range(send_ref.shape[0]):
        for ref, r in ((keep_ref, 2 * k), (send_ref, 2 * k + 1)):
            at = jnp.bitwise_xor(along, r)
            ref[k] = (kept_ref[at].astype(f32) + arrived_ref[at].astype(f32)).astype(bf16)


def halve_kernel(kept_ref, arrived_ref, send_ref, keep_ref):
    for k in range(send_ref.shape[0]):
        for ref, at in ((keep_ref, 2 * k), (send_ref, 2 * k + 1)):
            ref[k] = (kept_ref[at].astype(f32) + arrived_ref[at].astype(f32)).astype(bf16)


def added(refs):
    return functools.reduce(lambda a, b: a + b, [ref[...].astype(f32) for ref in refs])


def final_kernel(width_all, share_ref, gain_ref, expo_ref, *refs):
    *refs, layer_ref, grad_ref = refs
    own_all, cot_all = added(refs[:4]), added(refs[4:8])
    grad, layer = added(refs[8:10])[0], added(refs[10:12])[0]
    layer_ref[...] = (share_ref[...].astype(f32) + layer).astype(bf16)
    n, width = gain_ref.shape
    down, up = powers(expo_ref[...], -1), powers(expo_ref[...], 1)
    gain = gain_ref[...]
    per_dev = width // LANES
    blocks = n * per_dev
    at_row = lax.broadcasted_iota(jnp.int32, (n, blocks), 0)
    at_lane = lax.broadcasted_iota(jnp.int32, (n, blocks), 1)
    for p in range(2):
        rows = slice(p * n, (p + 1) * n)
        own, norm = own_all[rows, :], grad[rows, :]
        inv_rms = lax.rsqrt(jnp.sum(own * own, keepdims=True) / width_all + eps)
        scaled_in = (own * gain).astype(bf16).astype(f32)
        curvature = inv_rms * jnp.sum(scaled_in * norm, keepdims=True)
        correction = curvature * inv_rms * inv_rms / width_all
        value = cot_all[rows, :] + inv_rms * gain * norm - correction * own
        for c in range(per_dev):
            at = at_lane == at_row * per_dev + c
            shrink = jnp.sum(jnp.where(at, down[p : p + 1], 0.0), axis=1, keepdims=True)
            grow = jnp.sum(jnp.where(at, up[p : p + 1], 0.0), axis=1, keepdims=True)
            scaled = value[:, c * LANES : (c + 1) * LANES] * shrink
            kept = jnp.clip(scaled, -clip_top, clip_top).astype(bf16).astype(f32) * grow
            grad_ref[p, pl.ds(c, n, stride=per_dev), :] = kept


def on_device(
    activations,
    sample_ids,
    forward_exponent,
    sender_base,
    receiver_base,
    norm_gain,
    up_weight,
    down_weight,
    cotangent,
    backward_exponent,
    *,
    n,
):
    half, quarter = n // 2, n // 4
    tokens = 2 * n
    width_all, hidden_dev = up_weight.shape
    width = width_all // n
    me = lax.axis_index("dp").astype(jnp.int32)
    me_in = me.reshape(1)

    def shift(x, r):
        return lax.ppermute(x, "dp", [(d, d ^ (4 * r)) for d in range(n)]) if r else x

    def swap(x, bits):
        return lax.ppermute(x, "dp", [(d, d ^ bits) for d in range(n)])

    struct = jax.ShapeDtypeStruct
    share_shape, hidden_shape = (tokens, width), (tokens, hidden_dev)
    line_shape = (quarter, tokens, width)

    def call(kernel, outs, ins, args, scratch=(), micros=0.5):
        return pl.pallas_call(
            kernel,
            out_shape=outs,
            in_specs=ins,
            out_specs=jax.tree.map(lambda _: VMEM, outs),
            scratch_shapes=list(scratch),
            compiler_params=params(8),
            cost_estimate=pl.CostEstimate(
                flops=int(micros * FLOPS_PER_MICRO), bytes_accessed=0, transcendentals=0
            ),
        )(*args)

    offset = sample_ids - sender_base.shape[1] * me
    rows = -(-(2 * width // LANES + 1) // 16) * 16
    packed_shape = (4, rows, LANES)
    act_shape, expo_shape = (2, width_all), (2, width_all // LANES)
    once = lambda shape: pl.BlockSpec(shape, lambda i: (0,) * len(shape))
    in_shapes = [act_shape, expo_shape, sender_base.shape, receiver_base.shape, (1, width_all)]
    outs = (
        struct(act_shape, f32),
        struct(receiver_base.shape, f32),
        struct((n, width), f32),
    ) + (struct(packed_shape, bf16),) * quarter
    new_rows, received, gain, *packed = pl.pallas_call(
        send_kernel,
        out_shape=outs,
        grid=(1,),
        in_specs=[SMEM, SMEM] + [once(x) for x in in_shapes],
        out_specs=(VMEM,) * len(outs),
        scratch_shapes=[pltpu.VMEM((n, rows, LANES), f32)],
        compiler_params=params(8),
    )(
        me_in,
        offset,
        hbm(activations.reshape(act_shape)),
        hbm(forward_exponent.reshape(expo_shape)),
        hbm(sender_base),
        hbm(receiver_base),
        hbm(norm_gain.reshape(1, width_all)),
    )
    packed = [shift(x, r) for r, x in enumerate(packed)]
    blocks = call(
        sort_kernel,
        (struct((quarter, rows, LANES), bf16),) * 4,
        [SMEM] + [VMEM] * quarter,
        [me_in, *packed],
        micros=STAGE,
    )
    blocks = [blocks[0]] + [swap(blocks[e], e) for e in range(1, 4)]

    cot_line, blocks[0] = lax.optimization_barrier(
        (cotangent.reshape(1, tokens, width), blocks[0])
    )
    bit = quarter // 2
    while bit:
        cot_line = call(
            interleave_kernel,
            struct((2 * cot_line.shape[0], tokens, width), bf16),
            [VMEM] * 2,
            [cot_line, shift(cot_line, bit)],
        )
        bit //= 2

    ANY = pl.BlockSpec(memory_space=pl.ANY)
    share_f32 = struct(share_shape, f32)
    sums = (struct(hidden_shape, f32), struct((tokens, LANES), f32))

    def grad_active_part(part):
        return call(
            functools.partial(grad_active_kernel, part),
            (struct((hidden_dev, tokens), f32), share_f32),
            [SMEM, VMEM, VMEM],
            [me_in, cots[part], down_weight],
            [pltpu.VMEM(share_shape, f32)],
            micros=1.6,
        )

    def up_product_part(part):
        return call(
            functools.partial(up_kernel, part),
            sums + (share_f32,),
            [SMEM] + [VMEM] * 3,
            [me_in, rests[part], gain, up_weight],
            [pltpu.VMEM(share_shape, f32)],
            micros=1.2,
        )

    together = lax.optimization_barrier
    def rebuild(out, micros):
        return call(
            rebuild_kernel,
            out,
            [SMEM] + [VMEM] * 5,
            [me_in, *blocks, received],
            [
                pltpu.VMEM((n * rows, LANES), f32),
                pltpu.VMEM((2 * width // LANES, 2 * n, LANES), f32),
            ],
            micros=micros,
        )

    share = rebuild(struct(share_shape, bf16), STAGE)
    lines = [shift(share, r) for r in range(quarter)]
    cots = [cot_line]
    cot_row = swap(cot_line, 2)
    grads = [grad_active_part(0)]
    lines, grads[0] = together((lines, grads[0]))
    rest_line = jnp.stack(lines)
    rest_row = swap(rest_line, 2)
    rests = [rest_line]
    products = [up_product_part(0)]
    rest_line, cot_line, cot_row, products[0] = together((rest_line, cots[0], cot_row, products[0]))
    rest_line_other = swap(rest_line, 1)
    cots += [cot_row, swap(cot_line, 1)]
    grads += [grad_active_part(1), grad_active_part(2)]
    new_sender_base = call(
        sender_base_kernel,
        struct(sender_base.shape, f32),
        [SMEM] + [VMEM] * 2,
        [offset, new_rows, sender_base],
    )
    rest_row, cot_row, grads[1], grads[2], new_sender_base = together(
        (rest_row, cot_row, grads[1], grads[2], new_sender_base)
    )
    rests += [rest_row, rest_line_other, swap(rest_row, 1)]
    cots.append(swap(cot_row, 1))
    grads.append(grad_active_part(3))
    products += [up_product_part(1), up_product_part(2)]
    gas, own_cots = zip(*grads)
    accs, squares, owns = map(list, zip(*products))

    half_out = struct((half, tokens, width), bf16)
    active, grad_hidden, own = call(
        activation_kernel,
        (struct(hidden_shape, bf16), struct(hidden_shape, bf16), share_f32),
        [SMEM] + [VMEM] * 13,
        [me_in, rests[3], gain, up_weight, *accs, *squares, *gas],
        [pltpu.VMEM(x.shape, x.dtype) for x in sums] + [pltpu.VMEM(share_shape, f32)],
        micros=1.5,
    )
    owns.append(own)

    def down_terms(other, active):
        return call(
            functools.partial(down_kernel, other),
            half_out,
            [SMEM] + [VMEM] * 2,
            [me_in, active, down_weight],
            micros=1.5,
        )

    def pair_sum(kept, arrived):
        return call(
            pair_kernel,
            (struct(line_shape, bf16),) * 2,
            [SMEM] + [VMEM] * 2,
            [me_in, kept, arrived],
        )

    def line_sum(kept, arrived):
        half_line = lambda parts: (struct((parts, tokens, width), bf16),) * 2
        parts, bit = quarter // 2, 1
        send, keep = call(
            line_kernel, half_line(parts), [SMEM] + [VMEM] * 2, [me_in, kept, arrived]
        )
        arrived = shift(send, bit)
        while parts > 1:
            parts, bit = parts // 2, 2 * bit
            send, keep = call(halve_kernel, half_line(parts), [VMEM] * 2, [keep, arrived])
            arrived = shift(send, bit)
        return [keep, arrived]

    out_send = down_terms(1, active)
    out_in = swap(out_send, 1)
    active, out_send = together((active, out_send))
    out_send, out_row = pair_sum(down_terms(0, active), out_in)
    out_row_in = swap(out_send, 2)
    grad_hidden, out_row = together((grad_hidden, out_row))
    rows_out = struct((width // LANES, n * tokens, LANES), f32)
    most = n - n // 8
    grad_rows = call(
        functools.partial(grad_norm_kernel, 0, most),
        rows_out,
        [SMEM] + [VMEM] * 2,
        [me_in, grad_hidden, up_weight],
        micros=4,
    )
    grad_rows, out_row_in = together((grad_rows, out_row_in))
    grad_send, grad_keep = call(
        functools.partial(grad_norm_kernel, most, n),
        (half_out, half_out),
        [SMEM] + [VMEM] * 3,
        [me_in, grad_hidden, up_weight, grad_rows],
        [pltpu.VMEM(rows_out.shape, f32)],
        micros=0.7,
    )
    grad_in = swap(grad_send, 1)
    received, blocks, grad_send = together((received, blocks, grad_send))
    new_receiver_base = rebuild(struct(receiver_base.shape, f32), 0.7)
    grad_in, new_receiver_base = together((grad_in, new_receiver_base))
    grad_send, grad_row = pair_sum(grad_keep, grad_in)
    grad_row_in = swap(grad_send, 2)
    out_row, grad_row = together((out_row, grad_row))
    out_line = line_sum(out_row, out_row_in)
    grad_line = line_sum(grad_row, grad_row_in)
    layer_out, returned = call(
        functools.partial(final_kernel, width_all),
        (struct(share_shape, bf16), struct((2, width_all // LANES, LANES), f32)),
        [VMEM] * 15,
        [
            share,
            gain,
            backward_exponent.reshape(expo_shape),
            *owns,
            *own_cots,
            *grad_line,
            *out_line,
        ],
    )
    return (
        new_sender_base,
        new_receiver_base,
        layer_out.reshape(2, n, width),
        returned.reshape(2, 1, width_all),
    )


def solution(mesh):
    placed = (
        P(None, ("groups", "dp"), None),
        P(("groups", "dp")),
        P(None, ("groups", "dp"), None),
        P(None, ("groups", "dp"), None),
        P(None, "groups", "dp"),
        P(),
        P(None, "dp"),
        P("dp", None),
        P(None, "groups", "dp"),
        P(None, ("groups", "dp"), None),
    )
    return jax.shard_map(
        functools.partial(on_device, n=mesh.shape["dp"]),
        mesh=mesh,
        in_specs=placed,
        out_specs=(
            P(None, ("groups", "dp"), None),
            P(None, "groups", "dp"),
            P(None, "groups", "dp"),
            P(None, ("groups", "dp"), None),
        ),
        check_vma=False,
    )
```

```python
import functools

import jax
import jax.numpy as jnp
from jax import lax
from jax.experimental import pallas as pl
from jax.experimental.pallas import tpu as pltpu
from jax.sharding import PartitionSpec as P

clip_top = 448.0
eps = 1e-05
LANES = 128
STAGE = 4
FLOPS_PER_MICRO = 1.15e9
f32 = jnp.float32
bf16 = jnp.bfloat16
VMEM = pl.BlockSpec(memory_space=pltpu.VMEM)
SMEM = pl.BlockSpec(memory_space=pltpu.SMEM)


def hbm(x):
    return pltpu.with_memory_space_constraint(x, pltpu.HBM)


def powers(exponent, sign):
    total = jnp.zeros(exponent.shape, f32)
    for level in range(-10, 1):
        total = jnp.where(exponent == level, f32(2.0 ** (sign * level)), total)
    return total


def params(megabytes):
    return pltpu.CompilerParams(vmem_limit_bytes=megabytes << 20)


def flip(bit, by):
    return lax.rem(bit + by, 2)


def place(me):
    return me // 4, lax.rem(me // 2, 2), lax.rem(me, 2)


def owner_of(me, n, part, back):
    along, row, core = place(me)
    at = jnp.bitwise_xor(along, back)
    return 4 * at + 2 * flip(row, part % 2) + flip(core, part // 2)


def block_spot(q, tokens, rows, width):
    per_column = tokens // rows
    r, c = rows * (q % per_column), width + LANES * (q // per_column)
    return slice(r, r + rows), slice(c, c + LANES)


def send_kernel(
    me_ref, ids_ref, act_ref, expo_ref, base_ref, received_ref, cot_ref, gain_ref,
    new_rows_ref, received_out_ref, gain_out_ref, *refs,
):
    *packed_refs, rows_ref = refs
    n, rows, _ = rows_ref.shape
    tokens, share = cot_ref.shape
    width = act_ref.shape[1]
    per_dev = width // LANES // n
    received_out_ref[...] = received_ref[...]
    for j in range(n):
        gain_out_ref[j : j + 1, :] = gain_ref[:, j * share : (j + 1) * share]
    offset = ids_ref[0] - base_ref.shape[1] * me_ref[0]
    first = offset == 0
    down, up = powers(expo_ref[...], -1), powers(expo_ref[...], 1)
    old = [base_ref[p] for p in range(2)]
    chosen = jnp.concatenate([jnp.where(first, o[0:1], o[1:2]) for o in old], axis=0)
    delta = act_ref[...].astype(f32) - chosen
    fill = jnp.full((rows - 2 * per_dev, LANES), offset.astype(f32))
    pieces = []
    for b in range(width // LANES):
        scaled = delta[:, b * LANES : (b + 1) * LANES] * down[:, b : b + 1]
        kept = jnp.clip(scaled, -clip_top, clip_top).astype(bf16).astype(f32) * up[:, b : b + 1]
        d, c = divmod(b, per_dev)
        rows_ref[d, 2 * c : 2 * c + 2, :] = kept
        pieces.append(kept)
    for d in range(n):
        rows_ref[d, 2 * per_dev :, :] = fill
    along, _, _ = place(me_ref[0])
    cot = cot_ref[...]
    for r, packed_ref in enumerate(packed_refs):
        to = jnp.bitwise_xor(along, r)
        packed_ref[:, :share] = cot
        for q in range(4):
            packed_ref[block_spot(q, tokens, rows, share)] = rows_ref[4 * to + q].astype(bf16)
    new_rows_ref[...] = chosen + jnp.concatenate(pieces, axis=1)


def sender_base_kernel(me_ref, ids_ref, rows_ref, base_ref, new_ref):
    first = ids_ref[0] == base_ref.shape[1] * me_ref[0]
    for p in range(2):
        row, old = rows_ref[p : p + 1, :], base_ref[p]
        new_ref[p, 0:1, :] = jnp.where(first, row, old[0:1])
        new_ref[p, 1:2, :] = jnp.where(first, old[1:2], row)


def sort_kernel(me_ref, *refs):
    *packed_refs, line_ref, b0, b1, b2, b3 = refs
    quarter, tokens, share = line_ref.shape
    rows = b0.shape[1]
    _, row, core = place(me_ref[0])
    for r, packed_ref in enumerate(packed_refs):
        line_ref[r] = packed_ref[:, :share]
        block = [packed_ref[block_spot(q, tokens, rows, share)] for q in range(4)]
        for e, out_ref in enumerate((b0, b1, b2, b3)):
            to_row, to_core = flip(row, e // 2), flip(core, e % 2)
            low = jnp.where(to_core == 0, block[0], block[1])
            high = jnp.where(to_core == 0, block[2], block[3])
            out_ref[r] = jnp.where(to_row == 0, low, high)


def rebuild_kernel(me_ref, b0, b1, b2, b3, base_ref, out_ref, rows_ref, slots_ref):
    quarter, rows, _ = b0.shape
    n, width = 4 * quarter, base_ref.shape[2]
    whole = out_ref.shape == base_ref.shape
    for e, block_ref in enumerate((b0, b1, b2, b3)):
        for r in range(quarter):
            sender = owner_of(me_ref[0], n, 2 * (e % 2) + e // 2, r)
            rows_ref[pl.ds(pl.multiple_of(sender * rows, rows), rows), :] = block_ref[r].astype(f32)
    per_dev = width // LANES
    first = rows_ref[pl.ds(2 * per_dev, n, stride=rows), :] == 0.0
    for p in range(2):
        for c in range(per_dev):
            cols = slice(c * LANES, (c + 1) * LANES)
            sent = rows_ref[pl.ds(2 * c + p, n, stride=rows), :]
            at = p * per_dev + c
            slots_ref[at] = base_ref[p, :, cols]
            even = slots_ref[at, pl.ds(0, n, stride=2), :]
            odd = slots_ref[at, pl.ds(1, n, stride=2), :]
            rebuilt = jnp.where(first, even, odd) + sent
            if not whole:
                out_ref[p * n : (p + 1) * n, cols] = rebuilt.astype(bf16)
                continue
            slots_ref[at, pl.ds(0, n, stride=2), :] = jnp.where(first, rebuilt, even)
            slots_ref[at, pl.ds(1, n, stride=2), :] = jnp.where(first, odd, rebuilt)
            out_ref[p, :, cols] = slots_ref[at]


def dot_nt(a, b):
    return lax.dot_general(a, b, (((1,), (1,)), ((), ())), preferred_element_type=f32)


def own_rows(piece_ref, own_ref, me, owner):
    n = piece_ref.shape[0] // 2
    for p in range(2):
        own_ref[pl.ds(p * n + owner, 1), :] = piece_ref[pl.ds(p * n + me, 1), :]


def dot_by_halves(rows, tokens):
    middle = tokens.shape[1] // 2 // LANES * LANES
    if middle == 0:
        return dot_nt(rows, tokens)
    return dot_nt(rows[:, :middle], tokens[:, :middle]) + dot_nt(rows[:, middle:], tokens[:, middle:])


def grad_active_kernel(part, me_ref, cot_ref, weight_ref, acc_ref, own_ref, piece_ref):
    quarter, _, width = cot_ref.shape
    me = me_ref[0]
    own_ref[...] = jnp.zeros_like(own_ref)
    for k in range(quarter):
        owner = owner_of(me, 4 * quarter, part, k)
        piece_ref[...] = cot_ref[k].astype(f32)
        own_rows(piece_ref, own_ref, me, owner)
        columns = pl.ds(pl.multiple_of(owner * width, width), width)
        terms = dot_by_halves(weight_ref[:, columns], cot_ref[k])
        acc_ref[...] = terms if k == 0 else acc_ref[...] + terms


def up_kernel(
    part, me_ref, rest_ref, gain_ref, weight_ref, acc_ref, square_ref, own_ref, piece_ref
):
    quarter, _, width = rest_ref.shape
    me = me_ref[0]
    own_ref[...] = jnp.zeros_like(own_ref)
    for k in range(quarter):
        owner = owner_of(me, 4 * quarter, part, k)
        piece = rest_ref[k].astype(f32)
        piece_ref[...] = piece
        own_rows(piece_ref, own_ref, me, owner)
        squares = piece * piece
        total = sum(squares[:, c * LANES : (c + 1) * LANES] for c in range(width // LANES))
        square_ref[...] = total if k == 0 else square_ref[...] + total
        scaled = (piece * gain_ref[pl.ds(owner, 1), :]).astype(bf16)
        rows = pl.ds(pl.multiple_of(owner * width, width), width)
        terms = jnp.dot(scaled, weight_ref[rows, :], preferred_element_type=f32)
        acc_ref[...] = terms if k == 0 else acc_ref[...] + terms


def activation_kernel(me_ref, rest_ref, gain_ref, weight_ref, *refs):
    ins, refs = refs[:10], refs[10:]
    active_ref, gh_ref, own_ref, acc_ref, square_ref, piece_ref = refs
    up_kernel(3, me_ref, rest_ref, gain_ref, weight_ref, acc_ref, square_ref, own_ref, piece_ref)
    product = acc_ref[...] + (ins[0][...] + ins[1][...] + ins[2][...])
    squares = square_ref[...] + (ins[3][...] + ins[4][...] + ins[5][...])
    total = jnp.sum(squares, axis=1, keepdims=True)
    hidden = lax.rsqrt(total / weight_ref.shape[0] + eps) * product
    sigma = jax.nn.sigmoid(hidden)
    active_ref[...] = (hidden * sigma).astype(bf16)
    grad_active = (ins[6][...] + ins[7][...] + (ins[8][...] + ins[9][...])).T
    gh_ref[...] = (grad_active * sigma * (1.0 + hidden * (1.0 - sigma))).astype(bf16)


def grad_norm_kernel(me_ref, gh_ref, weight_ref, rows_ref):
    chunks = rows_ref.shape[0]
    tokens, width = gh_ref.shape[0], chunks * LANES
    n = tokens // 2
    gh = gh_ref[...]
    for share in range(n):
        block = weight_ref[share * width : (share + 1) * width, :]
        terms = dot_by_halves(block, gh).T
        for p in range(2):
            for c in range(chunks):
                rows_ref[c, pl.ds(p * n + share, n, stride=tokens), :] = terms[
                    p * n : (p + 1) * n, c * LANES : (c + 1) * LANES
                ]


def split_kernel(me_ref, rows_ref, send_ref, keep_ref):
    half, tokens, _ = send_ref.shape
    core = lax.rem(me_ref[0], 2)
    for k in range(half):
        keep_at = pl.multiple_of((2 * k + core) * tokens, tokens)
        send_at = pl.multiple_of((2 * k + 1 - core) * tokens, tokens)
        for c in range(rows_ref.shape[0]):
            cols = slice(c * LANES, (c + 1) * LANES)
            keep_ref[k, :, cols] = rows_ref[c, pl.ds(keep_at, tokens), :].astype(bf16)
            send_ref[k, :, cols] = rows_ref[c, pl.ds(send_at, tokens), :].astype(bf16)


def down_kernel(other, me_ref, active_ref, weight_ref, out_ref):
    half, _, width = out_ref.shape
    core = lax.rem(me_ref[0] + other, 2)

    def share(k):
        columns = pl.ds(pl.multiple_of((2 * k + core) * width, width), width)
        terms = jnp.dot(active_ref[...], weight_ref[:, columns], preferred_element_type=f32)
        out_ref[k] = terms.astype(bf16)

    pl.loop(0, half, unroll=4)(share)


def pair_kernel(me_ref, kept_ref, arrived_ref, send_ref, keep_ref):
    _, row, _ = place(me_ref[0])
    for k in range(send_ref.shape[0]):
        for out_ref, at in ((send_ref, 2 * k + 1 - row), (keep_ref, 2 * k + row)):
            out_ref[k] = (kept_ref[at].astype(f32) + arrived_ref[at].astype(f32)).astype(bf16)


def line_kernel(me_ref, kept_ref, arrived_ref, *refs):
    along, _, _ = place(me_ref[0])
    for r, ref in enumerate(refs):
        at = jnp.bitwise_xor(along, r)
        ref[...] = (kept_ref[at].astype(f32) + arrived_ref[at].astype(f32)).astype(bf16)


def added(refs):
    return functools.reduce(lambda a, b: a + b, [ref[...].astype(f32) for ref in refs])


def final_kernel(width_all, share_ref, gain_ref, expo_ref, *refs):
    *refs, layer_ref, grad_ref = refs
    quarter = (len(refs) - 8) // 2
    own_all, cot_all = added(refs[:4]), added(refs[4:8])
    grad, layer = added(refs[8 : 8 + quarter]), added(refs[8 + quarter :])
    layer_ref[...] = (share_ref[...].astype(f32) + layer).astype(bf16)
    n, width = gain_ref.shape
    down, up = powers(expo_ref[...], -1), powers(expo_ref[...], 1)
    gain = gain_ref[...]
    per_dev = width // LANES
    blocks = n * per_dev
    at_row = lax.broadcasted_iota(jnp.int32, (n, blocks), 0)
    at_lane = lax.broadcasted_iota(jnp.int32, (n, blocks), 1)
    for p in range(2):
        rows = slice(p * n, (p + 1) * n)
        own, norm = own_all[rows, :], grad[rows, :]
        inv_rms = lax.rsqrt(jnp.sum(own * own, keepdims=True) / width_all + eps)
        scaled_in = (own * gain).astype(bf16).astype(f32)
        curvature = inv_rms * jnp.sum(scaled_in * norm, keepdims=True)
        correction = curvature * inv_rms * inv_rms / width_all
        value = cot_all[rows, :] + inv_rms * gain * norm - correction * own
        for c in range(per_dev):
            at = at_lane == at_row * per_dev + c
            shrink = jnp.sum(jnp.where(at, down[p : p + 1], 0.0), axis=1, keepdims=True)
            grow = jnp.sum(jnp.where(at, up[p : p + 1], 0.0), axis=1, keepdims=True)
            scaled = value[:, c * LANES : (c + 1) * LANES] * shrink
            kept = jnp.clip(scaled, -clip_top, clip_top).astype(bf16).astype(f32) * grow
            grad_ref[p, pl.ds(c, n, stride=per_dev), :] = kept


def on_device(
    activations,
    sample_ids,
    forward_exponent,
    sender_base,
    receiver_base,
    norm_gain,
    up_weight,
    down_weight,
    cotangent,
    backward_exponent,
    *,
    n,
):
    half, quarter = n // 2, n // 4
    tokens = 2 * n
    width_all, hidden_dev = up_weight.shape
    width = width_all // n
    me = lax.axis_index("dp").astype(jnp.int32)
    me_in = me.reshape(1)

    def shift(x, r):
        return lax.ppermute(x, "dp", [(d, d ^ (4 * r)) for d in range(n)]) if r else x

    def swap(x, bits):
        return lax.ppermute(x, "dp", [(d, d ^ bits) for d in range(n)])

    struct = jax.ShapeDtypeStruct
    share_shape, hidden_shape = (tokens, width), (tokens, hidden_dev)
    line_shape = (quarter, tokens, width)

    def call(kernel, outs, ins, args, scratch=(), micros=0.5):
        return pl.pallas_call(
            kernel,
            out_shape=outs,
            in_specs=ins,
            out_specs=jax.tree.map(lambda _: VMEM, outs),
            scratch_shapes=list(scratch),
            compiler_params=params(8),
            cost_estimate=pl.CostEstimate(
                flops=int(micros * FLOPS_PER_MICRO), bytes_accessed=0, transcendentals=0
            ),
        )(*args)

    rows = -(-(2 * width // LANES + 1) // 16) * 16
    packed_shape = (tokens, width + LANES * -(-4 * rows // tokens))
    act_shape, expo_shape = (2, width_all), (2, width_all // LANES)
    once = lambda shape: pl.BlockSpec(shape, lambda i: (0,) * len(shape))
    in_shapes = [act_shape, expo_shape, sender_base.shape, receiver_base.shape, share_shape, (1, width_all)]
    outs = (
        struct(act_shape, f32),
        struct(receiver_base.shape, f32),
        struct((n, width), f32),
    ) + (struct(packed_shape, bf16),) * quarter
    new_rows, received, gain, *packed = pl.pallas_call(
        send_kernel,
        out_shape=outs,
        grid=(1,),
        in_specs=[SMEM, SMEM] + [once(x) for x in in_shapes],
        out_specs=(VMEM,) * len(outs),
        scratch_shapes=[pltpu.VMEM((n, rows, LANES), f32)],
        compiler_params=params(8),
    )(
        me_in,
        sample_ids,
        hbm(activations.reshape(act_shape)),
        hbm(forward_exponent.reshape(expo_shape)),
        hbm(sender_base),
        hbm(receiver_base),
        hbm(cotangent.reshape(share_shape)),
        hbm(norm_gain.reshape(1, width_all)),
    )
    packed = [shift(x, r) for r, x in enumerate(packed)]
    cot_line, *blocks = call(
        sort_kernel,
        (struct(line_shape, bf16),) + (struct((quarter, rows, LANES), bf16),) * 4,
        [SMEM] + [VMEM] * quarter,
        [me_in, *packed],
        micros=STAGE,
    )
    blocks = [blocks[0]] + [swap(blocks[e], e) for e in range(1, 4)]
    cots = [cot_line]

    ANY = pl.BlockSpec(memory_space=pl.ANY)
    share_f32 = struct(share_shape, f32)
    sums = (struct(hidden_shape, f32), struct((tokens, LANES), f32))

    def grad_active_part(part):
        return call(
            functools.partial(grad_active_kernel, part),
            (struct((hidden_dev, tokens), f32), share_f32),
            [SMEM, VMEM, VMEM],
            [me_in, cots[part], down_weight],
            [pltpu.VMEM(share_shape, f32)],
            micros=1.6,
        )

    def up_product_part(part):
        return call(
            functools.partial(up_kernel, part),
            sums + (share_f32,),
            [SMEM] + [VMEM] * 3,
            [me_in, rests[part], gain, up_weight],
            [pltpu.VMEM(share_shape, f32)],
            micros=1.2,
        )

    together = lax.optimization_barrier
    def rebuild(out, micros):
        return call(
            rebuild_kernel,
            out,
            [SMEM] + [VMEM] * 5,
            [me_in, *blocks, received],
            [
                pltpu.VMEM((n * rows, LANES), f32),
                pltpu.VMEM((2 * width // LANES, 2 * n, LANES), f32),
            ],
            micros=micros,
        )

    share = rebuild(struct(share_shape, bf16), STAGE)
    lines = [shift(share, r) for r in range(quarter)]
    cots[0], share_after = together((cot_line, share))
    cot_row = swap(cots[0], 2)
    grads = [grad_active_part(0)]
    lines, grads[0] = together((lines, grads[0]))
    rest_line = jnp.stack(lines)
    rest_row = swap(rest_line, 2)
    rests = [rest_line]
    products = [up_product_part(0)]
    rest_line, cot_line, cot_row, products[0] = together((rest_line, cots[0], cot_row, products[0]))
    rest_line_other = swap(rest_line, 1)
    cots += [cot_row, swap(cot_line, 1)]
    grads += [grad_active_part(1), grad_active_part(2)]
    new_sender_base = call(
        sender_base_kernel,
        struct(sender_base.shape, f32),
        [SMEM, SMEM] + [VMEM] * 2,
        [me_in, sample_ids, new_rows, sender_base],
    )
    rest_row, cot_row, grads[1], grads[2], new_sender_base = together(
        (rest_row, cot_row, grads[1], grads[2], new_sender_base)
    )
    rests += [rest_row, rest_line_other, swap(rest_row, 1)]
    cots.append(swap(cot_row, 1))
    grads.append(grad_active_part(3))
    products += [up_product_part(1), up_product_part(2)]
    gas, own_cots = zip(*grads)
    accs, squares, owns = map(list, zip(*products))

    half_out = struct((half, tokens, width), bf16)
    active, grad_hidden, own = call(
        activation_kernel,
        (struct(hidden_shape, bf16), struct(hidden_shape, bf16), share_f32),
        [SMEM] + [VMEM] * 13,
        [me_in, rests[3], gain, up_weight, *accs, *squares, *gas],
        [pltpu.VMEM(x.shape, x.dtype) for x in sums] + [pltpu.VMEM(share_shape, f32)],
        micros=1.5,
    )
    owns.append(own)

    def down_terms(other, active):
        return call(
            functools.partial(down_kernel, other),
            half_out,
            [SMEM] + [VMEM] * 2,
            [me_in, active, down_weight],
            micros=1.5,
        )

    def pair_sum(kept, arrived):
        return call(
            pair_kernel,
            (struct(line_shape, bf16),) * 2,
            [SMEM] + [VMEM] * 2,
            [me_in, kept, arrived],
        )

    def line_sum(kept, arrived):
        shares = call(
            line_kernel,
            (struct(share_shape, bf16),) * quarter,
            [SMEM] + [VMEM] * 2,
            [me_in, kept, arrived],
        )
        far_first = [shift(shares[r], r) for r in reversed(range(quarter))]
        return far_first

    out_send = down_terms(1, active)
    out_in = swap(out_send, 1)
    active, out_send = together((active, out_send))
    out_send, out_row = pair_sum(down_terms(0, active), out_in)
    out_row_in = swap(out_send, 2)
    grad_hidden, out_row = together((grad_hidden, out_row))
    rows_out = struct((width // LANES, n * tokens, LANES), f32)
    grad_rows = call(
        grad_norm_kernel,
        rows_out,
        [SMEM] + [VMEM] * 2,
        [me_in, grad_hidden, up_weight],
        micros=4.5,
    )
    grad_rows, out_row_in = together((grad_rows, out_row_in))
    grad_send, grad_keep = call(
        split_kernel, (half_out, half_out), [SMEM, VMEM], [me_in, grad_rows], micros=0.4
    )
    grad_in = swap(grad_send, 1)
    received, blocks, grad_send = together((received, blocks, grad_send))
    new_receiver_base = rebuild(struct(receiver_base.shape, f32), 0.7)
    grad_in, new_receiver_base = together((grad_in, new_receiver_base))
    grad_send, grad_row = pair_sum(grad_keep, grad_in)
    grad_row_in = swap(grad_send, 2)
    out_row, grad_row = together((out_row, grad_row))
    out_line = line_sum(out_row, out_row_in)
    grad_line = line_sum(grad_row, grad_row_in)
    layer_out, returned = call(
        functools.partial(final_kernel, width_all),
        (struct(share_shape, bf16), struct((2, width_all // LANES, LANES), f32)),
        [VMEM] * (11 + 2 * quarter),
        [
            share,
            gain,
            backward_exponent.reshape(expo_shape),
            *owns,
            *own_cots,
            *grad_line,
            *out_line,
        ],
    )
    return (
        new_sender_base,
        new_receiver_base,
        layer_out.reshape(2, n, width),
        returned.reshape(2, 1, width_all),
    )


def solution(mesh):
    placed = (
        P(None, ("groups", "dp"), None),
        P(("groups", "dp")),
        P(None, ("groups", "dp"), None),
        P(None, ("groups", "dp"), None),
        P(None, "groups", "dp"),
        P(),
        P(None, "dp"),
        P("dp", None),
        P(None, "groups", "dp"),
        P(None, ("groups", "dp"), None),
    )
    return jax.shard_map(
        functools.partial(on_device, n=mesh.shape["dp"]),
        mesh=mesh,
        in_specs=placed,
        out_specs=(
            P(None, ("groups", "dp"), None),
            P(None, "groups", "dp"),
            P(None, "groups", "dp"),
            P(None, ("groups", "dp"), None),
        ),
        check_vma=False,
    )
```

```python
import functools

import jax
import jax.numpy as jnp
from jax import lax
from jax.experimental import pallas as pl
from jax.experimental.pallas import tpu as pltpu
from jax.sharding import PartitionSpec as P

clip_top = 448.0
eps = 1e-05
LANES = 128
STAGE = 4
FLOPS_PER_MICRO = 1.15e9
f32 = jnp.float32
bf16 = jnp.bfloat16
VMEM = pl.BlockSpec(memory_space=pltpu.VMEM)
SMEM = pl.BlockSpec(memory_space=pltpu.SMEM)


def hbm(x):
    return pltpu.with_memory_space_constraint(x, pltpu.HBM)


def powers(exponent, sign):
    total = jnp.zeros(exponent.shape, f32)
    for level in range(-10, 1):
        total = jnp.where(exponent == level, f32(2.0 ** (sign * level)), total)
    return total


def params(megabytes):
    return pltpu.CompilerParams(vmem_limit_bytes=megabytes << 20)


def flip(bit, by):
    return lax.rem(bit + by, 2)


def place(me):
    return me // 4, lax.rem(me // 2, 2), lax.rem(me, 2)


def owner_of(me, n, part, back):
    along, row, core = place(me)
    at = jnp.bitwise_xor(along, back)
    return 4 * at + 2 * flip(row, part % 2) + flip(core, part // 2)


def block_spot(q, tokens, rows, width):
    per_column = tokens // rows
    r, c = rows * (q % per_column), width + LANES * (q // per_column)
    return slice(r, r + rows), slice(c, c + LANES)


def send_kernel(
    me_ref, ids_ref, act_ref, expo_ref, base_ref, received_ref, cot_ref, gain_ref,
    new_rows_ref, received_out_ref, gain_out_ref, *refs,
):
    *packed_refs, rows_ref = refs
    n, rows, _ = rows_ref.shape
    tokens, share = cot_ref.shape
    width = act_ref.shape[1]
    per_dev = width // LANES // n
    received_out_ref[...] = received_ref[...]
    for j in range(n):
        gain_out_ref[j : j + 1, :] = gain_ref[:, j * share : (j + 1) * share]
    offset = ids_ref[0] - base_ref.shape[1] * me_ref[0]
    first = offset == 0
    down, up = powers(expo_ref[...], -1), powers(expo_ref[...], 1)
    old = [base_ref[p] for p in range(2)]
    chosen = jnp.concatenate([jnp.where(first, o[0:1], o[1:2]) for o in old], axis=0)
    delta = act_ref[...].astype(f32) - chosen
    fill = jnp.full((rows - 2 * per_dev, LANES), offset.astype(f32))
    pieces = []
    for b in range(width // LANES):
        scaled = delta[:, b * LANES : (b + 1) * LANES] * down[:, b : b + 1]
        kept = jnp.clip(scaled, -clip_top, clip_top).astype(bf16).astype(f32) * up[:, b : b + 1]
        d, c = divmod(b, per_dev)
        rows_ref[d, 2 * c : 2 * c + 2, :] = kept
        pieces.append(kept)
    for d in range(n):
        rows_ref[d, 2 * per_dev :, :] = fill
    along, _, _ = place(me_ref[0])
    cot = cot_ref[...]
    for r, packed_ref in enumerate(packed_refs):
        to = jnp.bitwise_xor(along, r)
        packed_ref[:, :share] = cot
        for q in range(4):
            packed_ref[block_spot(q, tokens, rows, share)] = rows_ref[4 * to + q].astype(bf16)
    new_rows_ref[...] = chosen + jnp.concatenate(pieces, axis=1)


def sender_base_kernel(me_ref, ids_ref, rows_ref, base_ref, new_ref):
    first = ids_ref[0] == base_ref.shape[1] * me_ref[0]
    for p in range(2):
        row, old = rows_ref[p : p + 1, :], base_ref[p]
        new_ref[p, 0:1, :] = jnp.where(first, row, old[0:1])
        new_ref[p, 1:2, :] = jnp.where(first, old[1:2], row)


def sort_kernel(me_ref, *refs):
    *packed_refs, line_ref, b0, b1, b2, b3 = refs
    quarter, tokens, share = line_ref.shape
    rows = b0.shape[1]
    _, row, core = place(me_ref[0])
    for r, packed_ref in enumerate(packed_refs):
        line_ref[r] = packed_ref[:, :share]
        block = [packed_ref[block_spot(q, tokens, rows, share)] for q in range(4)]
        for e, out_ref in enumerate((b0, b1, b2, b3)):
            to_row, to_core = flip(row, e // 2), flip(core, e % 2)
            low = jnp.where(to_core == 0, block[0], block[1])
            high = jnp.where(to_core == 0, block[2], block[3])
            out_ref[r] = jnp.where(to_row == 0, low, high)


def rebuild_kernel(me_ref, b0, b1, b2, b3, base_ref, out_ref, rows_ref, slots_ref):
    quarter, rows, _ = b0.shape
    n, width = 4 * quarter, base_ref.shape[2]
    whole = out_ref.shape == base_ref.shape
    for e, block_ref in enumerate((b0, b1, b2, b3)):
        for r in range(quarter):
            sender = owner_of(me_ref[0], n, 2 * (e % 2) + e // 2, r)
            rows_ref[pl.ds(pl.multiple_of(sender * rows, rows), rows), :] = block_ref[r].astype(f32)
    per_dev = width // LANES
    first = rows_ref[pl.ds(2 * per_dev, n, stride=rows), :] == 0.0
    for p in range(2):
        for c in range(per_dev):
            cols = slice(c * LANES, (c + 1) * LANES)
            sent = rows_ref[pl.ds(2 * c + p, n, stride=rows), :]
            at = p * per_dev + c
            slots_ref[at] = base_ref[p, :, cols]
            even = slots_ref[at, pl.ds(0, n, stride=2), :]
            odd = slots_ref[at, pl.ds(1, n, stride=2), :]
            rebuilt = jnp.where(first, even, odd) + sent
            if not whole:
                out_ref[p * n : (p + 1) * n, cols] = rebuilt.astype(bf16)
                continue
            slots_ref[at, pl.ds(0, n, stride=2), :] = jnp.where(first, rebuilt, even)
            slots_ref[at, pl.ds(1, n, stride=2), :] = jnp.where(first, odd, rebuilt)
            out_ref[p, :, cols] = slots_ref[at]


def dot_nt(a, b):
    return lax.dot_general(a, b, (((1,), (1,)), ((), ())), preferred_element_type=f32)


def own_rows(piece_ref, own_ref, me, owner):
    n = piece_ref.shape[0] // 2
    for p in range(2):
        own_ref[pl.ds(p * n + owner, 1), :] = piece_ref[pl.ds(p * n + me, 1), :]


def dot_by_halves(rows, tokens):
    middle = tokens.shape[1] // 2 // LANES * LANES
    if middle == 0:
        return dot_nt(rows, tokens)
    return dot_nt(rows[:, :middle], tokens[:, :middle]) + dot_nt(rows[:, middle:], tokens[:, middle:])


def grad_active_kernel(part, me_ref, cot_ref, weight_ref, acc_ref, own_ref, piece_ref):
    quarter, _, width = cot_ref.shape
    me = me_ref[0]
    own_ref[...] = jnp.zeros_like(own_ref)
    for k in range(quarter):
        owner = owner_of(me, 4 * quarter, part, k)
        piece_ref[...] = cot_ref[k].astype(f32)
        own_rows(piece_ref, own_ref, me, owner)
        columns = pl.ds(pl.multiple_of(owner * width, width), width)
        terms = dot_by_halves(weight_ref[:, columns], cot_ref[k])
        acc_ref[...] = terms if k == 0 else acc_ref[...] + terms


def up_kernel(
    part, me_ref, rest_ref, gain_ref, weight_ref, acc_ref, square_ref, own_ref, piece_ref
):
    quarter, _, width = rest_ref.shape
    me = me_ref[0]
    own_ref[...] = jnp.zeros_like(own_ref)
    for k in range(quarter):
        owner = owner_of(me, 4 * quarter, part, k)
        piece = rest_ref[k].astype(f32)
        piece_ref[...] = piece
        own_rows(piece_ref, own_ref, me, owner)
        squares = piece * piece
        total = sum(squares[:, c * LANES : (c + 1) * LANES] for c in range(width // LANES))
        square_ref[...] = total if k == 0 else square_ref[...] + total
        scaled = (piece * gain_ref[pl.ds(owner, 1), :]).astype(bf16)
        rows = pl.ds(pl.multiple_of(owner * width, width), width)
        terms = jnp.dot(scaled, weight_ref[rows, :], preferred_element_type=f32)
        acc_ref[...] = terms if k == 0 else acc_ref[...] + terms


def activation_kernel(me_ref, rest_ref, gain_ref, weight_ref, *refs):
    ins, refs = refs[:10], refs[10:]
    active_ref, gh_ref, own_ref, acc_ref, square_ref, piece_ref = refs
    up_kernel(3, me_ref, rest_ref, gain_ref, weight_ref, acc_ref, square_ref, own_ref, piece_ref)
    product = acc_ref[...] + (ins[0][...] + ins[1][...] + ins[2][...])
    squares = square_ref[...] + (ins[3][...] + ins[4][...] + ins[5][...])
    total = jnp.sum(squares, axis=1, keepdims=True)
    hidden = lax.rsqrt(total / weight_ref.shape[0] + eps) * product
    sigma = jax.nn.sigmoid(hidden)
    active_ref[...] = (hidden * sigma).astype(bf16)
    grad_active = (ins[6][...] + ins[7][...] + (ins[8][...] + ins[9][...])).T
    gh_ref[...] = (grad_active * sigma * (1.0 + hidden * (1.0 - sigma))).astype(bf16)


def grad_norm_kernel(me_ref, gh_ref, weight_ref, rows_ref):
    chunks = rows_ref.shape[0]
    tokens, width = gh_ref.shape[0], chunks * LANES
    n = tokens // 2
    gh = gh_ref[...]
    for share in range(n):
        block = weight_ref[share * width : (share + 1) * width, :]
        terms = dot_by_halves(block, gh).T
        for p in range(2):
            for c in range(chunks):
                rows_ref[c, pl.ds(p * n + share, n, stride=tokens), :] = terms[
                    p * n : (p + 1) * n, c * LANES : (c + 1) * LANES
                ]


def split_kernel(me_ref, rows_ref, send_ref, keep_ref):
    half, tokens, _ = send_ref.shape
    core = lax.rem(me_ref[0], 2)
    for k in range(half):
        keep_at = pl.multiple_of((2 * k + core) * tokens, tokens)
        send_at = pl.multiple_of((2 * k + 1 - core) * tokens, tokens)
        for c in range(rows_ref.shape[0]):
            cols = slice(c * LANES, (c + 1) * LANES)
            keep_ref[k, :, cols] = rows_ref[c, pl.ds(keep_at, tokens), :].astype(bf16)
            send_ref[k, :, cols] = rows_ref[c, pl.ds(send_at, tokens), :].astype(bf16)


def down_kernel(other, me_ref, active_ref, weight_ref, out_ref):
    half, _, width = out_ref.shape
    core = lax.rem(me_ref[0] + other, 2)

    def share(k):
        columns = pl.ds(pl.multiple_of((2 * k + core) * width, width), width)
        terms = jnp.dot(active_ref[...], weight_ref[:, columns], preferred_element_type=f32)
        out_ref[k] = terms.astype(bf16)

    pl.loop(0, half, unroll=4)(share)


def pair_kernel(me_ref, kept_ref, arrived_ref, send_ref, keep_ref):
    _, row, _ = place(me_ref[0])
    for k in range(send_ref.shape[0]):
        for out_ref, at in ((send_ref, 2 * k + 1 - row), (keep_ref, 2 * k + row)):
            out_ref[k] = (kept_ref[at].astype(f32) + arrived_ref[at].astype(f32)).astype(bf16)


def line_kernel(me_ref, kept_ref, arrived_ref, *refs):
    along, _, _ = place(me_ref[0])
    for r, ref in enumerate(refs):
        at = jnp.bitwise_xor(along, r)
        ref[...] = (kept_ref[at].astype(f32) + arrived_ref[at].astype(f32)).astype(bf16)


def added(refs):
    return functools.reduce(lambda a, b: a + b, [ref[...].astype(f32) for ref in refs])


def final_kernel(width_all, share_ref, gain_ref, expo_ref, *refs):
    *refs, layer_ref, grad_ref = refs
    quarter = (len(refs) - 8) // 2
    own_all, cot_all = added(refs[:4]), added(refs[4:8])
    grad, layer = added(refs[8 : 8 + quarter]), added(refs[8 + quarter :])
    layer_ref[...] = (share_ref[...].astype(f32) + layer).astype(bf16)
    n, width = gain_ref.shape
    down, up = powers(expo_ref[...], -1), powers(expo_ref[...], 1)
    gain = gain_ref[...]
    per_dev = width // LANES
    blocks = n * per_dev
    at_row = lax.broadcasted_iota(jnp.int32, (n, blocks), 0)
    at_lane = lax.broadcasted_iota(jnp.int32, (n, blocks), 1)
    for p in range(2):
        rows = slice(p * n, (p + 1) * n)
        own, norm = own_all[rows, :], grad[rows, :]
        inv_rms = lax.rsqrt(jnp.sum(own * own, keepdims=True) / width_all + eps)
        scaled_in = (own * gain).astype(bf16).astype(f32)
        curvature = inv_rms * jnp.sum(scaled_in * norm, keepdims=True)
        correction = curvature * inv_rms * inv_rms / width_all
        value = cot_all[rows, :] + inv_rms * gain * norm - correction * own
        for c in range(per_dev):
            at = at_lane == at_row * per_dev + c
            shrink = jnp.sum(jnp.where(at, down[p : p + 1], 0.0), axis=1, keepdims=True)
            grow = jnp.sum(jnp.where(at, up[p : p + 1], 0.0), axis=1, keepdims=True)
            scaled = value[:, c * LANES : (c + 1) * LANES] * shrink
            kept = jnp.clip(scaled, -clip_top, clip_top).astype(bf16).astype(f32) * grow
            grad_ref[p, pl.ds(c, n, stride=per_dev), :] = kept


def on_device(
    activations,
    sample_ids,
    forward_exponent,
    sender_base,
    receiver_base,
    norm_gain,
    up_weight,
    down_weight,
    cotangent,
    backward_exponent,
    *,
    n,
):
    half, quarter = n // 2, n // 4
    tokens = 2 * n
    width_all, hidden_dev = up_weight.shape
    width = width_all // n
    me = lax.axis_index("dp").astype(jnp.int32)
    me_in = me.reshape(1)

    def shift(x, r):
        return lax.ppermute(x, "dp", [(d, d ^ (4 * r)) for d in range(n)]) if r else x

    def swap(x, bits):
        return lax.ppermute(x, "dp", [(d, d ^ bits) for d in range(n)])

    struct = jax.ShapeDtypeStruct
    share_shape, hidden_shape = (tokens, width), (tokens, hidden_dev)
    line_shape = (quarter, tokens, width)

    def call(kernel, outs, ins, args, scratch=(), micros=0.5):
        return pl.pallas_call(
            kernel,
            out_shape=outs,
            in_specs=ins,
            out_specs=jax.tree.map(lambda _: VMEM, outs),
            scratch_shapes=list(scratch),
            compiler_params=params(8),
            cost_estimate=pl.CostEstimate(
                flops=int(micros * FLOPS_PER_MICRO), bytes_accessed=0, transcendentals=0
            ),
        )(*args)

    rows = -(-(2 * width // LANES + 1) // 16) * 16
    packed_shape = (tokens, width + LANES * -(-4 * rows // tokens))
    act_shape, expo_shape = (2, width_all), (2, width_all // LANES)
    once = lambda shape: pl.BlockSpec(shape, lambda i: (0,) * len(shape))
    in_shapes = [act_shape, expo_shape, sender_base.shape, receiver_base.shape, share_shape, (1, width_all)]
    outs = (
        struct(act_shape, f32),
        struct(receiver_base.shape, f32),
        struct((n, width), f32),
    ) + (struct(packed_shape, bf16),) * quarter
    new_rows, received, gain, *packed = pl.pallas_call(
        send_kernel,
        out_shape=outs,
        grid=(1,),
        in_specs=[SMEM, SMEM] + [once(x) for x in in_shapes],
        out_specs=(VMEM,) * len(outs),
        scratch_shapes=[pltpu.VMEM((n, rows, LANES), f32)],
        compiler_params=params(8),
    )(
        me_in,
        sample_ids,
        hbm(activations.reshape(act_shape)),
        hbm(forward_exponent.reshape(expo_shape)),
        hbm(sender_base),
        hbm(receiver_base),
        hbm(cotangent.reshape(share_shape)),
        hbm(norm_gain.reshape(1, width_all)),
    )
    packed = [shift(x, r) for r, x in enumerate(packed)]
    cot_line, *blocks = call(
        sort_kernel,
        (struct(line_shape, bf16),) + (struct((quarter, rows, LANES), bf16),) * 4,
        [SMEM] + [VMEM] * quarter,
        [me_in, *packed],
        micros=STAGE,
    )
    blocks = [blocks[0]] + [swap(blocks[e], e) for e in range(1, 4)]
    cots = [cot_line]

    ANY = pl.BlockSpec(memory_space=pl.ANY)
    share_f32 = struct(share_shape, f32)
    sums = (struct(hidden_shape, f32), struct((tokens, LANES), f32))

    def grad_active_part(part):
        return call(
            functools.partial(grad_active_kernel, part),
            (struct((hidden_dev, tokens), f32), share_f32),
            [SMEM, VMEM, VMEM],
            [me_in, cots[part], down_weight],
            [pltpu.VMEM(share_shape, f32)],
            micros=1.6,
        )

    def up_product_part(part):
        return call(
            functools.partial(up_kernel, part),
            sums + (share_f32,),
            [SMEM] + [VMEM] * 3,
            [me_in, rests[part], gain, up_weight],
            [pltpu.VMEM(share_shape, f32)],
            micros=1.2,
        )

    together = lax.optimization_barrier
    def rebuild(out, micros):
        return call(
            rebuild_kernel,
            out,
            [SMEM] + [VMEM] * 5,
            [me_in, *blocks, received],
            [
                pltpu.VMEM((n * rows, LANES), f32),
                pltpu.VMEM((2 * width // LANES, 2 * n, LANES), f32),
            ],
            micros=micros,
        )

    share = rebuild(struct(share_shape, bf16), STAGE)
    lines = [shift(share, r) for r in range(quarter)]
    cot_row = swap(cot_line, 2)
    cot_line, cot_row, share_after = together((cot_line, cot_row, share))
    cots = [cot_line]
    grads = [grad_active_part(0)]
    lines, grads[0] = together((lines, grads[0]))
    rest_line = jnp.stack(lines)
    rest_row = swap(rest_line, 2)
    rests = [rest_line]
    products = [up_product_part(0)]
    rest_line, cot_line, cot_row, products[0] = together((rest_line, cots[0], cot_row, products[0]))
    rest_line_other = swap(rest_line, 1)
    cots += [cot_row, swap(cot_line, 1), swap(cot_row, 1)]
    grads += [grad_active_part(1), grad_active_part(2)]
    new_sender_base = call(
        sender_base_kernel,
        struct(sender_base.shape, f32),
        [SMEM, SMEM] + [VMEM] * 2,
        [me_in, sample_ids, new_rows, sender_base],
    )
    rest_row, grads[1], grads[2], new_sender_base = together(
        (rest_row, grads[1], grads[2], new_sender_base)
    )
    rests += [rest_row, rest_line_other, swap(rest_row, 1)]
    grads.append(grad_active_part(3))
    products += [up_product_part(1), up_product_part(2)]
    gas, own_cots = zip(*grads)
    accs, squares, owns = map(list, zip(*products))

    half_out = struct((half, tokens, width), bf16)
    active, grad_hidden, own = call(
        activation_kernel,
        (struct(hidden_shape, bf16), struct(hidden_shape, bf16), share_f32),
        [SMEM] + [VMEM] * 13,
        [me_in, rests[3], gain, up_weight, *accs, *squares, *gas],
        [pltpu.VMEM(x.shape, x.dtype) for x in sums] + [pltpu.VMEM(share_shape, f32)],
        micros=1.5,
    )
    owns.append(own)

    def down_terms(other, active):
        return call(
            functools.partial(down_kernel, other),
            half_out,
            [SMEM] + [VMEM] * 2,
            [me_in, active, down_weight],
            micros=1.5,
        )

    def pair_sum(kept, arrived):
        return call(
            pair_kernel,
            (struct(line_shape, bf16),) * 2,
            [SMEM] + [VMEM] * 2,
            [me_in, kept, arrived],
        )

    def line_sum(kept, arrived):
        shares = call(
            line_kernel,
            (struct(share_shape, bf16),) * quarter,
            [SMEM] + [VMEM] * 2,
            [me_in, kept, arrived],
        )
        far_first = [shift(shares[r], r) for r in reversed(range(quarter))]
        return far_first

    out_send = down_terms(1, active)
    out_in = swap(out_send, 1)
    active, out_send = together((active, out_send))
    out_send, out_row = pair_sum(down_terms(0, active), out_in)
    out_row_in = swap(out_send, 2)
    grad_hidden, out_row = together((grad_hidden, out_row))
    rows_out = struct((width // LANES, n * tokens, LANES), f32)
    grad_rows = call(
        grad_norm_kernel,
        rows_out,
        [SMEM] + [VMEM] * 2,
        [me_in, grad_hidden, up_weight],
        micros=4.5,
    )
    grad_rows, out_row_in = together((grad_rows, out_row_in))
    grad_send, grad_keep = call(
        split_kernel, (half_out, half_out), [SMEM, VMEM], [me_in, grad_rows], micros=0.4
    )
    grad_in = swap(grad_send, 1)
    received, blocks, grad_send = together((received, blocks, grad_send))
    new_receiver_base = rebuild(struct(receiver_base.shape, f32), 0.7)
    grad_in, new_receiver_base = together((grad_in, new_receiver_base))
    grad_send, grad_row = pair_sum(grad_keep, grad_in)
    grad_row_in = swap(grad_send, 2)
    out_row, grad_row = together((out_row, grad_row))
    out_line = line_sum(out_row, out_row_in)
    grad_line = line_sum(grad_row, grad_row_in)
    layer_out, returned = call(
        functools.partial(final_kernel, width_all),
        (struct(share_shape, bf16), struct((2, width_all // LANES, LANES), f32)),
        [VMEM] * (11 + 2 * quarter),
        [
            share,
            gain,
            backward_exponent.reshape(expo_shape),
            *owns,
            *own_cots,
            *grad_line,
            *out_line,
        ],
    )
    return (
        new_sender_base,
        new_receiver_base,
        layer_out.reshape(2, n, width),
        returned.reshape(2, 1, width_all),
    )


def solution(mesh):
    placed = (
        P(None, ("groups", "dp"), None),
        P(("groups", "dp")),
        P(None, ("groups", "dp"), None),
        P(None, ("groups", "dp"), None),
        P(None, "groups", "dp"),
        P(),
        P(None, "dp"),
        P("dp", None),
        P(None, "groups", "dp"),
        P(None, ("groups", "dp"), None),
    )
    return jax.shard_map(
        functools.partial(on_device, n=mesh.shape["dp"]),
        mesh=mesh,
        in_specs=placed,
        out_specs=(
            P(None, ("groups", "dp"), None),
            P(None, "groups", "dp"),
            P(None, "groups", "dp"),
            P(None, ("groups", "dp"), None),
        ),
        check_vma=False,
    )
```

```python
import functools

import jax
import jax.numpy as jnp
from jax import lax
from jax.experimental import pallas as pl
from jax.experimental.pallas import tpu as pltpu
from jax.sharding import PartitionSpec as P

clip_top = 448.0
eps = 1e-05
LANES = 128
STAGE = 4
FLOPS_PER_MICRO = 1.15e9
f32 = jnp.float32
bf16 = jnp.bfloat16
VMEM = pl.BlockSpec(memory_space=pltpu.VMEM)
SMEM = pl.BlockSpec(memory_space=pltpu.SMEM)


def hbm(x):
    return pltpu.with_memory_space_constraint(x, pltpu.HBM)


def powers(exponent, sign):
    total = jnp.zeros(exponent.shape, f32)
    for level in range(-10, 1):
        total = jnp.where(exponent == level, f32(2.0 ** (sign * level)), total)
    return total


def params(megabytes):
    return pltpu.CompilerParams(vmem_limit_bytes=megabytes << 20)


def flip(bit, by):
    return lax.rem(bit + by, 2)


def place(me):
    return me // 4, lax.rem(me // 2, 2), lax.rem(me, 2)


def owner_of(me, n, part, back):
    along, row, core = place(me)
    at = jnp.bitwise_xor(along, back)
    return 4 * at + 2 * flip(row, part % 2) + flip(core, part // 2)


def block_spot(q, tokens, rows, width):
    per_column = tokens // rows
    r, c = rows * (q % per_column), width + LANES * (q // per_column)
    return slice(r, r + rows), slice(c, c + LANES)


def send_kernel(
    me_ref, ids_ref, act_ref, expo_ref, base_ref, received_ref, cot_ref, gain_ref,
    new_rows_ref, received_out_ref, gain_out_ref, *refs,
):
    *packed_refs, rows_ref = refs
    n, rows, _ = rows_ref.shape
    tokens, share = cot_ref.shape
    width = act_ref.shape[1]
    per_dev = width // LANES // n
    received_out_ref[...] = received_ref[...]
    for j in range(n):
        gain_out_ref[j : j + 1, :] = gain_ref[:, j * share : (j + 1) * share]
    offset = ids_ref[0] - base_ref.shape[1] * me_ref[0]
    first = offset == 0
    down, up = powers(expo_ref[...], -1), powers(expo_ref[...], 1)
    old = [base_ref[p] for p in range(2)]
    chosen = jnp.concatenate([jnp.where(first, o[0:1], o[1:2]) for o in old], axis=0)
    delta = act_ref[...].astype(f32) - chosen
    fill = jnp.full((rows - 2 * per_dev, LANES), offset.astype(f32))
    pieces = []
    for b in range(width // LANES):
        scaled = delta[:, b * LANES : (b + 1) * LANES] * down[:, b : b + 1]
        kept = jnp.clip(scaled, -clip_top, clip_top).astype(bf16).astype(f32) * up[:, b : b + 1]
        d, c = divmod(b, per_dev)
        rows_ref[d, 2 * c : 2 * c + 2, :] = kept
        pieces.append(kept)
    for d in range(n):
        rows_ref[d, 2 * per_dev :, :] = fill
    along, _, _ = place(me_ref[0])
    cot = cot_ref[...]
    for r, packed_ref in enumerate(packed_refs):
        to = jnp.bitwise_xor(along, r)
        packed_ref[:, :share] = cot
        for q in range(4):
            packed_ref[block_spot(q, tokens, rows, share)] = rows_ref[4 * to + q].astype(bf16)
    new_rows_ref[...] = chosen + jnp.concatenate(pieces, axis=1)


def sender_base_kernel(me_ref, ids_ref, rows_ref, base_ref, new_ref):
    first = ids_ref[0] == base_ref.shape[1] * me_ref[0]
    for p in range(2):
        row, old = rows_ref[p : p + 1, :], base_ref[p]
        new_ref[p, 0:1, :] = jnp.where(first, row, old[0:1])
        new_ref[p, 1:2, :] = jnp.where(first, old[1:2], row)


def sort_kernel(me_ref, *refs):
    *packed_refs, line_ref, b0, b1, b2, b3 = refs
    quarter, tokens, share = line_ref.shape
    rows = b0.shape[1]
    _, row, core = place(me_ref[0])
    for r, packed_ref in enumerate(packed_refs):
        line_ref[r] = packed_ref[:, :share]
        block = [packed_ref[block_spot(q, tokens, rows, share)] for q in range(4)]
        for e, out_ref in enumerate((b0, b1, b2, b3)):
            to_row, to_core = flip(row, e // 2), flip(core, e % 2)
            low = jnp.where(to_core == 0, block[0], block[1])
            high = jnp.where(to_core == 0, block[2], block[3])
            out_ref[r] = jnp.where(to_row == 0, low, high)


def rebuild_kernel(me_ref, b0, b1, b2, b3, base_ref, out_ref, rows_ref, slots_ref):
    quarter, rows, _ = b0.shape
    n, width = 4 * quarter, base_ref.shape[2]
    whole = out_ref.shape == base_ref.shape
    for e, block_ref in enumerate((b0, b1, b2, b3)):
        for r in range(quarter):
            sender = owner_of(me_ref[0], n, 2 * (e % 2) + e // 2, r)
            rows_ref[pl.ds(pl.multiple_of(sender * rows, rows), rows), :] = block_ref[r].astype(f32)
    per_dev = width // LANES
    first = rows_ref[pl.ds(2 * per_dev, n, stride=rows), :] == 0.0
    for p in range(2):
        for c in range(per_dev):
            cols = slice(c * LANES, (c + 1) * LANES)
            sent = rows_ref[pl.ds(2 * c + p, n, stride=rows), :]
            at = p * per_dev + c
            slots_ref[at] = base_ref[p, :, cols]
            even = slots_ref[at, pl.ds(0, n, stride=2), :]
            odd = slots_ref[at, pl.ds(1, n, stride=2), :]
            rebuilt = jnp.where(first, even, odd) + sent
            if not whole:
                out_ref[p * n : (p + 1) * n, cols] = rebuilt.astype(bf16)
                continue
            slots_ref[at, pl.ds(0, n, stride=2), :] = jnp.where(first, rebuilt, even)
            slots_ref[at, pl.ds(1, n, stride=2), :] = jnp.where(first, odd, rebuilt)
            out_ref[p, :, cols] = slots_ref[at]


def dot_nt(a, b):
    return lax.dot_general(a, b, (((1,), (1,)), ((), ())), preferred_element_type=f32)


def own_rows(piece_ref, own_ref, me, owner):
    n = piece_ref.shape[0] // 2
    for p in range(2):
        own_ref[pl.ds(p * n + owner, 1), :] = piece_ref[pl.ds(p * n + me, 1), :]


def dot_by_halves(rows, tokens):
    middle = tokens.shape[1] // 2 // LANES * LANES
    if middle == 0:
        return dot_nt(rows, tokens)
    return dot_nt(rows[:, :middle], tokens[:, :middle]) + dot_nt(rows[:, middle:], tokens[:, middle:])


def grad_active_kernel(part, me_ref, cot_ref, weight_ref, acc_ref, own_ref, piece_ref):
    quarter, _, width = cot_ref.shape
    me = me_ref[0]
    own_ref[...] = jnp.zeros_like(own_ref)
    for k in range(quarter):
        owner = owner_of(me, 4 * quarter, part, k)
        piece_ref[...] = cot_ref[k].astype(f32)
        own_rows(piece_ref, own_ref, me, owner)
    total = 0.0
    for k in range(quarter):
        owner = owner_of(me, 4 * quarter, part, k)
        columns = pl.ds(pl.multiple_of(owner * width, width), width)
        total = total + dot_by_halves(weight_ref[:, columns], cot_ref[k])
    acc_ref[...] = total


def up_kernel(
    part, me_ref, rest_ref, gain_ref, weight_ref, acc_ref, square_ref, own_ref, piece_ref
):
    quarter, _, width = rest_ref.shape
    me = me_ref[0]
    own_ref[...] = jnp.zeros_like(own_ref)
    products = 0.0
    for k in range(quarter):
        owner = owner_of(me, 4 * quarter, part, k)
        piece = rest_ref[k].astype(f32)
        piece_ref[...] = piece
        own_rows(piece_ref, own_ref, me, owner)
        squares = piece * piece
        total = sum(squares[:, c * LANES : (c + 1) * LANES] for c in range(width // LANES))
        square_ref[...] = total if k == 0 else square_ref[...] + total
        scaled = (piece * gain_ref[pl.ds(owner, 1), :]).astype(bf16)
        rows = pl.ds(pl.multiple_of(owner * width, width), width)
        products = products + jnp.dot(scaled, weight_ref[rows, :], preferred_element_type=f32)
    acc_ref[...] = products


def activation_kernel(me_ref, rest_ref, gain_ref, weight_ref, *refs):
    ins, refs = refs[:10], refs[10:]
    active_ref, gh_ref, own_ref, acc_ref, square_ref, piece_ref = refs
    up_kernel(3, me_ref, rest_ref, gain_ref, weight_ref, acc_ref, square_ref, own_ref, piece_ref)
    product = acc_ref[...] + (ins[0][...] + ins[1][...] + ins[2][...])
    squares = square_ref[...] + (ins[3][...] + ins[4][...] + ins[5][...])
    total = jnp.sum(squares, axis=1, keepdims=True)
    hidden = lax.rsqrt(total / weight_ref.shape[0] + eps) * product
    sigma = jax.nn.sigmoid(hidden)
    active_ref[...] = (hidden * sigma).astype(bf16)
    grad_active = (ins[6][...] + ins[7][...] + (ins[8][...] + ins[9][...])).T
    gh_ref[...] = (grad_active * sigma * (1.0 + hidden * (1.0 - sigma))).astype(bf16)


def grad_norm_kernel(me_ref, gh_ref, weight_ref, rows_ref):
    chunks = rows_ref.shape[0]
    tokens, width = gh_ref.shape[0], chunks * LANES
    n = tokens // 2
    gh = gh_ref[...]
    step = n // 4
    for first in range(0, n, step):
        block = weight_ref[first * width : (first + step) * width, :]
        terms = dot_by_halves(block, gh).T
        for p in range(2):
            for at in range(step * chunks):
                share, c = first + at // chunks, at % chunks
                rows_ref[c, pl.ds(p * n + share, n, stride=tokens), :] = terms[
                    p * n : (p + 1) * n, at * LANES : (at + 1) * LANES
                ]


def split_kernel(me_ref, rows_ref, send_ref, keep_ref):
    half, tokens, _ = send_ref.shape
    core = lax.rem(me_ref[0], 2)
    for k in range(half):
        keep_at = pl.multiple_of((2 * k + core) * tokens, tokens)
        send_at = pl.multiple_of((2 * k + 1 - core) * tokens, tokens)
        for c in range(rows_ref.shape[0]):
            cols = slice(c * LANES, (c + 1) * LANES)
            keep_ref[k, :, cols] = rows_ref[c, pl.ds(keep_at, tokens), :].astype(bf16)
            send_ref[k, :, cols] = rows_ref[c, pl.ds(send_at, tokens), :].astype(bf16)


def down_kernel(other, me_ref, active_ref, weight_ref, out_ref):
    half, _, width = out_ref.shape
    core = lax.rem(me_ref[0] + other, 2)

    def share(k):
        columns = pl.ds(pl.multiple_of((2 * k + core) * width, width), width)
        terms = jnp.dot(active_ref[...], weight_ref[:, columns], preferred_element_type=f32)
        out_ref[k] = terms.astype(bf16)

    pl.loop(0, half, unroll=8)(share)


def pair_kernel(me_ref, kept_ref, arrived_ref, send_ref, keep_ref):
    _, row, _ = place(me_ref[0])
    for k in range(send_ref.shape[0]):
        for out_ref, at in ((send_ref, 2 * k + 1 - row), (keep_ref, 2 * k + row)):
            out_ref[k] = (kept_ref[at].astype(f32) + arrived_ref[at].astype(f32)).astype(bf16)


def line_kernel(me_ref, kept_ref, arrived_ref, *refs):
    along, _, _ = place(me_ref[0])
    for r, ref in enumerate(refs):
        at = jnp.bitwise_xor(along, r)
        ref[...] = (kept_ref[at].astype(f32) + arrived_ref[at].astype(f32)).astype(bf16)


def added(refs):
    return functools.reduce(lambda a, b: a + b, [ref[...].astype(f32) for ref in refs])


def final_kernel(width_all, share_ref, gain_ref, expo_ref, *refs):
    *refs, layer_ref, grad_ref = refs
    quarter = (len(refs) - 8) // 2
    own_all, cot_all = added(refs[:4]), added(refs[4:8])
    grad, layer = added(refs[8 : 8 + quarter]), added(refs[8 + quarter :])
    layer_ref[...] = (share_ref[...].astype(f32) + layer).astype(bf16)
    n, width = gain_ref.shape
    down, up = powers(expo_ref[...], -1), powers(expo_ref[...], 1)
    gain = gain_ref[...]
    per_dev = width // LANES
    blocks = n * per_dev
    at_row = lax.broadcasted_iota(jnp.int32, (n, blocks), 0)
    at_lane = lax.broadcasted_iota(jnp.int32, (n, blocks), 1)
    for p in range(2):
        rows = slice(p * n, (p + 1) * n)
        own, norm = own_all[rows, :], grad[rows, :]
        inv_rms = lax.rsqrt(jnp.sum(own * own, keepdims=True) / width_all + eps)
        scaled_in = (own * gain).astype(bf16).astype(f32)
        curvature = inv_rms * jnp.sum(scaled_in * norm, keepdims=True)
        correction = curvature * inv_rms * inv_rms / width_all
        value = cot_all[rows, :] + inv_rms * gain * norm - correction * own
        for c in range(per_dev):
            at = at_lane == at_row * per_dev + c
            shrink = jnp.sum(jnp.where(at, down[p : p + 1], 0.0), axis=1, keepdims=True)
            grow = jnp.sum(jnp.where(at, up[p : p + 1], 0.0), axis=1, keepdims=True)
            scaled = value[:, c * LANES : (c + 1) * LANES] * shrink
            kept = jnp.clip(scaled, -clip_top, clip_top).astype(bf16).astype(f32) * grow
            grad_ref[p, pl.ds(c, n, stride=per_dev), :] = kept


def on_device(
    activations,
    sample_ids,
    forward_exponent,
    sender_base,
    receiver_base,
    norm_gain,
    up_weight,
    down_weight,
    cotangent,
    backward_exponent,
    *,
    n,
):
    half, quarter = n // 2, n // 4
    tokens = 2 * n
    width_all, hidden_dev = up_weight.shape
    width = width_all // n
    me = lax.axis_index("dp").astype(jnp.int32)
    me_in = me.reshape(1)

    def shift(x, r):
        return lax.ppermute(x, "dp", [(d, d ^ (4 * r)) for d in range(n)]) if r else x

    def swap(x, bits):
        return lax.ppermute(x, "dp", [(d, d ^ bits) for d in range(n)])

    struct = jax.ShapeDtypeStruct
    share_shape, hidden_shape = (tokens, width), (tokens, hidden_dev)
    line_shape = (quarter, tokens, width)

    def call(kernel, outs, ins, args, scratch=(), micros=0.5):
        return pl.pallas_call(
            kernel,
            out_shape=outs,
            in_specs=ins,
            out_specs=jax.tree.map(lambda _: VMEM, outs),
            scratch_shapes=list(scratch),
            compiler_params=params(8),
            cost_estimate=pl.CostEstimate(
                flops=int(micros * FLOPS_PER_MICRO), bytes_accessed=0, transcendentals=0
            ),
        )(*args)

    rows = -(-(2 * width // LANES + 1) // 16) * 16
    packed_shape = (tokens, width + LANES * -(-4 * rows // tokens))
    act_shape, expo_shape = (2, width_all), (2, width_all // LANES)
    once = lambda shape: pl.BlockSpec(shape, lambda i: (0,) * len(shape))
    in_shapes = [act_shape, expo_shape, sender_base.shape, receiver_base.shape, share_shape, (1, width_all)]
    outs = (
        struct(act_shape, f32),
        struct(receiver_base.shape, f32),
        struct((n, width), f32),
    ) + (struct(packed_shape, bf16),) * quarter
    new_rows, received, gain, *packed = pl.pallas_call(
        send_kernel,
        out_shape=outs,
        grid=(1,),
        in_specs=[SMEM, SMEM] + [once(x) for x in in_shapes],
        out_specs=(VMEM,) * len(outs),
        scratch_shapes=[pltpu.VMEM((n, rows, LANES), f32)],
        compiler_params=params(8),
    )(
        me_in,
        sample_ids,
        hbm(activations.reshape(act_shape)),
        hbm(forward_exponent.reshape(expo_shape)),
        hbm(sender_base),
        hbm(receiver_base),
        hbm(cotangent.reshape(share_shape)),
        hbm(norm_gain.reshape(1, width_all)),
    )
    packed = [shift(x, r) for r, x in enumerate(packed)]
    cot_line, *blocks = call(
        sort_kernel,
        (struct(line_shape, bf16),) + (struct((quarter, rows, LANES), bf16),) * 4,
        [SMEM] + [VMEM] * quarter,
        [me_in, *packed],
        micros=STAGE,
    )
    blocks = [blocks[0]] + [swap(blocks[e], e) for e in range(1, 4)]
    cots = [cot_line]

    ANY = pl.BlockSpec(memory_space=pl.ANY)
    share_f32 = struct(share_shape, f32)
    sums = (struct(hidden_shape, f32), struct((tokens, LANES), f32))

    def grad_active_part(part):
        return call(
            functools.partial(grad_active_kernel, part),
            (struct((hidden_dev, tokens), f32), share_f32),
            [SMEM, VMEM, VMEM],
            [me_in, cots[part], down_weight],
            [pltpu.VMEM(share_shape, f32)],
            micros=1.6,
        )

    def up_product_part(part):
        return call(
            functools.partial(up_kernel, part),
            sums + (share_f32,),
            [SMEM] + [VMEM] * 3,
            [me_in, rests[part], gain, up_weight],
            [pltpu.VMEM(share_shape, f32)],
            micros=1.2,
        )

    together = lax.optimization_barrier
    def rebuild(out, micros):
        return call(
            rebuild_kernel,
            out,
            [SMEM] + [VMEM] * 5,
            [me_in, *blocks, received],
            [
                pltpu.VMEM((n * rows, LANES), f32),
                pltpu.VMEM((2 * width // LANES, 2 * n, LANES), f32),
            ],
            micros=micros,
        )

    share = rebuild(struct(share_shape, bf16), STAGE)
    lines = [shift(share, r) for r in range(quarter)]
    cot_row = swap(cot_line, 2)
    cot_line, cot_row, share_after = together((cot_line, cot_row, share))
    cots = [cot_line]
    grads = [grad_active_part(0)]
    lines, grads[0] = together((lines, grads[0]))
    rest_line = jnp.stack(lines)
    rest_row = swap(rest_line, 2)
    rests = [rest_line]
    products = [up_product_part(0)]
    rest_line, cot_line, cot_row, products[0] = together((rest_line, cots[0], cot_row, products[0]))
    rest_line_other = swap(rest_line, 1)
    cots += [cot_row, swap(cot_line, 1), swap(cot_row, 1)]
    grads += [grad_active_part(1), grad_active_part(2)]
    new_sender_base = call(
        sender_base_kernel,
        struct(sender_base.shape, f32),
        [SMEM, SMEM] + [VMEM] * 2,
        [me_in, sample_ids, new_rows, sender_base],
    )
    rest_row, grads[1], grads[2], new_sender_base = together(
        (rest_row, grads[1], grads[2], new_sender_base)
    )
    rests += [rest_row, rest_line_other, swap(rest_row, 1)]
    grads.append(grad_active_part(3))
    products += [up_product_part(1), up_product_part(2)]
    gas, own_cots = zip(*grads)
    accs, squares, owns = map(list, zip(*products))

    half_out = struct((half, tokens, width), bf16)
    active, grad_hidden, own = call(
        activation_kernel,
        (struct(hidden_shape, bf16), struct(hidden_shape, bf16), share_f32),
        [SMEM] + [VMEM] * 13,
        [me_in, rests[3], gain, up_weight, *accs, *squares, *gas],
        [pltpu.VMEM(x.shape, x.dtype) for x in sums] + [pltpu.VMEM(share_shape, f32)],
        micros=1.5,
    )
    owns.append(own)

    def down_terms(other, active):
        return call(
            functools.partial(down_kernel, other),
            half_out,
            [SMEM] + [VMEM] * 2,
            [me_in, active, down_weight],
            micros=1.5,
        )

    def pair_sum(kept, arrived):
        return call(
            pair_kernel,
            (struct(line_shape, bf16),) * 2,
            [SMEM] + [VMEM] * 2,
            [me_in, kept, arrived],
        )

    def line_sum(kept, arrived):
        shares = call(
            line_kernel,
            (struct(share_shape, bf16),) * quarter,
            [SMEM] + [VMEM] * 2,
            [me_in, kept, arrived],
        )
        far_first = [shift(shares[r], r) for r in reversed(range(quarter))]
        return far_first

    out_send = down_terms(1, active)
    out_in = swap(out_send, 1)
    active, out_send = together((active, out_send))
    out_send, out_row = pair_sum(down_terms(0, active), out_in)
    out_row_in = swap(out_send, 2)
    grad_hidden, out_row = together((grad_hidden, out_row))
    rows_out = struct((width // LANES, n * tokens, LANES), f32)
    grad_rows = call(
        grad_norm_kernel,
        rows_out,
        [SMEM] + [VMEM] * 2,
        [me_in, grad_hidden, up_weight],
        micros=4.5,
    )
    grad_rows, out_row_in = together((grad_rows, out_row_in))
    grad_send, grad_keep = call(
        split_kernel, (half_out, half_out), [SMEM, VMEM], [me_in, grad_rows], micros=0.4
    )
    grad_in = swap(grad_send, 1)
    received, blocks, grad_send = together((received, blocks, grad_send))
    new_receiver_base = rebuild(struct(receiver_base.shape, f32), 0.7)
    grad_in, new_receiver_base = together((grad_in, new_receiver_base))
    grad_send, grad_row = pair_sum(grad_keep, grad_in)
    grad_row_in = swap(grad_send, 2)
    out_row, grad_row = together((out_row, grad_row))
    out_line = line_sum(out_row, out_row_in)
    grad_line = line_sum(grad_row, grad_row_in)
    layer_out, returned = call(
        functools.partial(final_kernel, width_all),
        (struct(share_shape, bf16), struct((2, width_all // LANES, LANES), f32)),
        [VMEM] * (11 + 2 * quarter),
        [
            share,
            gain,
            backward_exponent.reshape(expo_shape),
            *owns,
            *own_cots,
            *grad_line,
            *out_line,
        ],
    )
    return (
        new_sender_base,
        new_receiver_base,
        layer_out.reshape(2, n, width),
        returned.reshape(2, 1, width_all),
    )


def solution(mesh):
    placed = (
        P(None, ("groups", "dp"), None),
        P(("groups", "dp")),
        P(None, ("groups", "dp"), None),
        P(None, ("groups", "dp"), None),
        P(None, "groups", "dp"),
        P(),
        P(None, "dp"),
        P("dp", None),
        P(None, "groups", "dp"),
        P(None, ("groups", "dp"), None),
    )
    return jax.shard_map(
        functools.partial(on_device, n=mesh.shape["dp"]),
        mesh=mesh,
        in_specs=placed,
        out_specs=(
            P(None, ("groups", "dp"), None),
            P(None, "groups", "dp"),
            P(None, "groups", "dp"),
            P(None, ("groups", "dp"), None),
        ),
        check_vma=False,
    )
```

```python
import functools

import jax
import jax.numpy as jnp
from jax import lax
from jax.experimental import pallas as pl
from jax.experimental.pallas import tpu as pltpu
from jax.sharding import PartitionSpec as P

clip_top = 448.0
eps = 1e-05
LANES = 128
STAGE = 4
FLOPS_PER_MICRO = 1.15e9
f32 = jnp.float32
bf16 = jnp.bfloat16
VMEM = pl.BlockSpec(memory_space=pltpu.VMEM)
SMEM = pl.BlockSpec(memory_space=pltpu.SMEM)


def hbm(x):
    return pltpu.with_memory_space_constraint(x, pltpu.HBM)


def powers(exponent, sign):
    total = jnp.zeros(exponent.shape, f32)
    for level in range(-10, 1):
        total = jnp.where(exponent == level, f32(2.0 ** (sign * level)), total)
    return total


def params(megabytes):
    return pltpu.CompilerParams(vmem_limit_bytes=megabytes << 20)


def flip(bit, by):
    return lax.rem(bit + by, 2)


def place(me):
    return me // 4, lax.rem(me // 2, 2), lax.rem(me, 2)


def owner_of(me, n, part, back):
    along, row, core = place(me)
    at = jnp.bitwise_xor(along, back)
    return 4 * at + 2 * flip(row, part % 2) + flip(core, part // 2)


def block_spot(q, tokens, rows, width):
    per_column = tokens // rows
    r, c = rows * (q % per_column), width + LANES * (q // per_column)
    return slice(r, r + rows), slice(c, c + LANES)


def send_kernel(
    me_ref, ids_ref, act_ref, expo_ref, base_ref, received_ref, cot_ref, gain_ref,
    new_rows_ref, received_out_ref, gain_out_ref, *refs,
):
    *packed_refs, rows_ref = refs
    n, rows, _ = rows_ref.shape
    tokens, share = cot_ref.shape
    width = act_ref.shape[1]
    per_dev = width // LANES // n
    received_out_ref[...] = received_ref[...]
    for j in range(n):
        gain_out_ref[j : j + 1, :] = gain_ref[:, j * share : (j + 1) * share]
    offset = ids_ref[0] - base_ref.shape[1] * me_ref[0]
    first = offset == 0
    down, up = powers(expo_ref[...], -1), powers(expo_ref[...], 1)
    old = [base_ref[p] for p in range(2)]
    chosen = jnp.concatenate([jnp.where(first, o[0:1], o[1:2]) for o in old], axis=0)
    delta = act_ref[...].astype(f32) - chosen
    fill = jnp.full((rows - 2 * per_dev, LANES), offset.astype(f32))
    pieces = []
    for b in range(width // LANES):
        scaled = delta[:, b * LANES : (b + 1) * LANES] * down[:, b : b + 1]
        kept = jnp.clip(scaled, -clip_top, clip_top).astype(bf16).astype(f32) * up[:, b : b + 1]
        d, c = divmod(b, per_dev)
        rows_ref[d, 2 * c : 2 * c + 2, :] = kept
        pieces.append(kept)
    for d in range(n):
        rows_ref[d, 2 * per_dev :, :] = fill
    along, _, _ = place(me_ref[0])
    cot = cot_ref[...]
    for r, packed_ref in enumerate(packed_refs):
        to = jnp.bitwise_xor(along, r)
        packed_ref[:, :share] = cot
        for q in range(4):
            packed_ref[block_spot(q, tokens, rows, share)] = rows_ref[4 * to + q].astype(bf16)
    new_rows_ref[...] = chosen + jnp.concatenate(pieces, axis=1)


def sender_base_kernel(me_ref, ids_ref, rows_ref, base_ref, new_ref):
    first = ids_ref[0] == base_ref.shape[1] * me_ref[0]
    for p in range(2):
        row, old = rows_ref[p : p + 1, :], base_ref[p]
        new_ref[p, 0:1, :] = jnp.where(first, row, old[0:1])
        new_ref[p, 1:2, :] = jnp.where(first, old[1:2], row)


def sort_kernel(me_ref, *refs):
    *packed_refs, line_ref, b0, b1, b2, b3 = refs
    quarter, tokens, share = line_ref.shape
    rows = b0.shape[1]
    _, row, core = place(me_ref[0])
    for r, packed_ref in enumerate(packed_refs):
        line_ref[r] = packed_ref[:, :share]
        block = [packed_ref[block_spot(q, tokens, rows, share)] for q in range(4)]
        for e, out_ref in enumerate((b0, b1, b2, b3)):
            to_row, to_core = flip(row, e // 2), flip(core, e % 2)
            low = jnp.where(to_core == 0, block[0], block[1])
            high = jnp.where(to_core == 0, block[2], block[3])
            out_ref[r] = jnp.where(to_row == 0, low, high)


def rebuild_kernel(me_ref, b0, b1, b2, b3, base_ref, out_ref, rows_ref, slots_ref):
    quarter, rows, _ = b0.shape
    n, width = 4 * quarter, base_ref.shape[2]
    whole = out_ref.shape == base_ref.shape
    for e, block_ref in enumerate((b0, b1, b2, b3)):
        for r in range(quarter):
            sender = owner_of(me_ref[0], n, 2 * (e % 2) + e // 2, r)
            rows_ref[pl.ds(pl.multiple_of(sender * rows, rows), rows), :] = block_ref[r].astype(f32)
    per_dev = width // LANES
    first = rows_ref[pl.ds(2 * per_dev, n, stride=rows), :] == 0.0
    for p in range(2):
        for c in range(per_dev):
            cols = slice(c * LANES, (c + 1) * LANES)
            sent = rows_ref[pl.ds(2 * c + p, n, stride=rows), :]
            at = p * per_dev + c
            slots_ref[at] = base_ref[p, :, cols]
            even = slots_ref[at, pl.ds(0, n, stride=2), :]
            odd = slots_ref[at, pl.ds(1, n, stride=2), :]
            rebuilt = jnp.where(first, even, odd) + sent
            if not whole:
                out_ref[p * n : (p + 1) * n, cols] = rebuilt.astype(bf16)
                continue
            slots_ref[at, pl.ds(0, n, stride=2), :] = jnp.where(first, rebuilt, even)
            slots_ref[at, pl.ds(1, n, stride=2), :] = jnp.where(first, odd, rebuilt)
            out_ref[p, :, cols] = slots_ref[at]


def dot_nt(a, b):
    return lax.dot_general(a, b, (((1,), (1,)), ((), ())), preferred_element_type=f32)


def own_rows(piece_ref, own_ref, me, owner):
    n = piece_ref.shape[0] // 2
    for p in range(2):
        own_ref[pl.ds(p * n + owner, 1), :] = piece_ref[pl.ds(p * n + me, 1), :]


def dot_by_halves(rows, tokens):
    middle = tokens.shape[1] // 2 // LANES * LANES
    if middle == 0:
        return dot_nt(rows, tokens)
    return dot_nt(rows[:, :middle], tokens[:, :middle]) + dot_nt(rows[:, middle:], tokens[:, middle:])


def grad_active_kernel(part, me_ref, cot_ref, weight_ref, acc_ref, own_ref, piece_ref):
    quarter, _, width = cot_ref.shape
    me = me_ref[0]
    own_ref[...] = jnp.zeros_like(own_ref)
    for k in range(quarter):
        owner = owner_of(me, 4 * quarter, part, k)
        piece_ref[...] = cot_ref[k].astype(f32)
        own_rows(piece_ref, own_ref, me, owner)
    total = 0.0
    for k in range(quarter):
        owner = owner_of(me, 4 * quarter, part, k)
        columns = pl.ds(pl.multiple_of(owner * width, width), width)
        total = total + dot_by_halves(weight_ref[:, columns], cot_ref[k])
    acc_ref[...] = total


def up_kernel(
    part, me_ref, rest_ref, gain_ref, weight_ref, acc_ref, square_ref, own_ref, piece_ref
):
    quarter, _, width = rest_ref.shape
    me = me_ref[0]
    own_ref[...] = jnp.zeros_like(own_ref)
    products = 0.0
    for k in range(quarter):
        owner = owner_of(me, 4 * quarter, part, k)
        piece = rest_ref[k].astype(f32)
        piece_ref[...] = piece
        own_rows(piece_ref, own_ref, me, owner)
        squares = piece * piece
        total = sum(squares[:, c * LANES : (c + 1) * LANES] for c in range(width // LANES))
        square_ref[...] = total if k == 0 else square_ref[...] + total
        scaled = (piece * gain_ref[pl.ds(owner, 1), :]).astype(bf16)
        rows = pl.ds(pl.multiple_of(owner * width, width), width)
        products = products + jnp.dot(scaled, weight_ref[rows, :], preferred_element_type=f32)
    acc_ref[...] = products


def activation_kernel(me_ref, rest_ref, gain_ref, weight_ref, *refs):
    ins, refs = refs[:10], refs[10:]
    active_ref, gh_ref, own_ref, acc_ref, square_ref, piece_ref = refs
    up_kernel(3, me_ref, rest_ref, gain_ref, weight_ref, acc_ref, square_ref, own_ref, piece_ref)
    product = acc_ref[...] + (ins[0][...] + ins[1][...] + ins[2][...])
    squares = square_ref[...] + (ins[3][...] + ins[4][...] + ins[5][...])
    total = jnp.sum(squares, axis=1, keepdims=True)
    hidden = lax.rsqrt(total / weight_ref.shape[0] + eps) * product
    sigma = jax.nn.sigmoid(hidden)
    active_ref[...] = (hidden * sigma).astype(bf16)
    grad_active = (ins[6][...] + ins[7][...] + (ins[8][...] + ins[9][...])).T
    gh_ref[...] = (grad_active * sigma * (1.0 + hidden * (1.0 - sigma))).astype(bf16)


def grad_norm_kernel(me_ref, gh_ref, weight_ref, rows_ref):
    chunks = rows_ref.shape[0]
    tokens, width = gh_ref.shape[0], chunks * LANES
    n = tokens // 2
    gh = gh_ref[...]
    step = 1
    for first in range(0, n, step):
        block = weight_ref[first * width : (first + step) * width, :]
        terms = dot_by_halves(block, gh).T
        for p in range(2):
            for at in range(step * chunks):
                share, c = first + at // chunks, at % chunks
                rows_ref[c, pl.ds(p * n + share, n, stride=tokens), :] = terms[
                    p * n : (p + 1) * n, at * LANES : (at + 1) * LANES
                ]


def split_kernel(me_ref, rows_ref, send_ref, keep_ref):
    half, tokens, _ = send_ref.shape
    core = lax.rem(me_ref[0], 2)
    for k in range(half):
        keep_at = pl.multiple_of((2 * k + core) * tokens, tokens)
        send_at = pl.multiple_of((2 * k + 1 - core) * tokens, tokens)
        for c in range(rows_ref.shape[0]):
            cols = slice(c * LANES, (c + 1) * LANES)
            keep_ref[k, :, cols] = rows_ref[c, pl.ds(keep_at, tokens), :].astype(bf16)
            send_ref[k, :, cols] = rows_ref[c, pl.ds(send_at, tokens), :].astype(bf16)


def down_kernel(other, me_ref, active_ref, weight_ref, out_ref):
    half, _, width = out_ref.shape
    core = lax.rem(me_ref[0] + other, 2)

    def share(k):
        columns = pl.ds(pl.multiple_of((2 * k + core) * width, width), width)
        terms = jnp.dot(active_ref[...], weight_ref[:, columns], preferred_element_type=f32)
        out_ref[k] = terms.astype(bf16)

    pl.loop(0, half, unroll=8)(share)


def pair_kernel(me_ref, kept_ref, arrived_ref, send_ref, keep_ref):
    _, row, _ = place(me_ref[0])
    for k in range(send_ref.shape[0]):
        for out_ref, at in ((send_ref, 2 * k + 1 - row), (keep_ref, 2 * k + row)):
            out_ref[k] = (kept_ref[at].astype(f32) + arrived_ref[at].astype(f32)).astype(bf16)


def line_kernel(me_ref, kept_ref, arrived_ref, *refs):
    along, _, _ = place(me_ref[0])
    for r, ref in enumerate(refs):
        at = jnp.bitwise_xor(along, r)
        ref[...] = (kept_ref[at].astype(f32) + arrived_ref[at].astype(f32)).astype(bf16)


def added(refs):
    return functools.reduce(lambda a, b: a + b, [ref[...].astype(f32) for ref in refs])


def layer_kernel(share_ref, *refs):
    *refs, layer_ref, own_ref, cot_ref = refs
    own_ref[...], cot_ref[...] = added(refs[:4]), added(refs[4:8])
    layer_ref[...] = (share_ref[...].astype(f32) + added(refs[8:])).astype(bf16)


def final_kernel(width_all, own_ref, cot_ref, gain_ref, expo_ref, *refs):
    *refs, grad_ref = refs
    own_all, cot_all, grad = own_ref[...], cot_ref[...], added(refs)
    n, width = gain_ref.shape
    down, up = powers(expo_ref[...], -1), powers(expo_ref[...], 1)
    gain = gain_ref[...]
    per_dev = width // LANES
    blocks = n * per_dev
    at_row = lax.broadcasted_iota(jnp.int32, (n, blocks), 0)
    at_lane = lax.broadcasted_iota(jnp.int32, (n, blocks), 1)
    for p in range(2):
        rows = slice(p * n, (p + 1) * n)
        own, norm = own_all[rows, :], grad[rows, :]
        inv_rms = lax.rsqrt(jnp.sum(own * own, keepdims=True) / width_all + eps)
        scaled_in = (own * gain).astype(bf16).astype(f32)
        curvature = inv_rms * jnp.sum(scaled_in * norm, keepdims=True)
        correction = curvature * inv_rms * inv_rms / width_all
        value = cot_all[rows, :] + inv_rms * gain * norm - correction * own
        for c in range(per_dev):
            at = at_lane == at_row * per_dev + c
            shrink = jnp.sum(jnp.where(at, down[p : p + 1], 0.0), axis=1, keepdims=True)
            grow = jnp.sum(jnp.where(at, up[p : p + 1], 0.0), axis=1, keepdims=True)
            scaled = value[:, c * LANES : (c + 1) * LANES] * shrink
            kept = jnp.clip(scaled, -clip_top, clip_top).astype(bf16).astype(f32) * grow
            grad_ref[p, pl.ds(c, n, stride=per_dev), :] = kept


def on_device(
    activations,
    sample_ids,
    forward_exponent,
    sender_base,
    receiver_base,
    norm_gain,
    up_weight,
    down_weight,
    cotangent,
    backward_exponent,
    *,
    n,
):
    half, quarter = n // 2, n // 4
    tokens = 2 * n
    width_all, hidden_dev = up_weight.shape
    width = width_all // n
    me = lax.axis_index("dp").astype(jnp.int32)
    me_in = me.reshape(1)

    def shift(x, r):
        return lax.ppermute(x, "dp", [(d, d ^ (4 * r)) for d in range(n)]) if r else x

    def swap(x, bits):
        return lax.ppermute(x, "dp", [(d, d ^ bits) for d in range(n)])

    struct = jax.ShapeDtypeStruct
    share_shape, hidden_shape = (tokens, width), (tokens, hidden_dev)
    line_shape = (quarter, tokens, width)

    def call(kernel, outs, ins, args, scratch=(), micros=0.5):
        return pl.pallas_call(
            kernel,
            out_shape=outs,
            in_specs=ins,
            out_specs=jax.tree.map(lambda _: VMEM, outs),
            scratch_shapes=list(scratch),
            compiler_params=params(8),
            cost_estimate=pl.CostEstimate(
                flops=int(micros * FLOPS_PER_MICRO), bytes_accessed=0, transcendentals=0
            ),
        )(*args)

    rows = -(-(2 * width // LANES + 1) // 16) * 16
    packed_shape = (tokens, width + LANES * -(-4 * rows // tokens))
    act_shape, expo_shape = (2, width_all), (2, width_all // LANES)
    once = lambda shape: pl.BlockSpec(shape, lambda i: (0,) * len(shape))
    in_shapes = [act_shape, expo_shape, sender_base.shape, receiver_base.shape, share_shape, (1, width_all)]
    outs = (
        struct(act_shape, f32),
        struct(receiver_base.shape, f32),
        struct((n, width), f32),
    ) + (struct(packed_shape, bf16),) * quarter
    new_rows, received, gain, *packed = pl.pallas_call(
        send_kernel,
        out_shape=outs,
        grid=(1,),
        in_specs=[SMEM, SMEM] + [once(x) for x in in_shapes],
        out_specs=(VMEM,) * len(outs),
        scratch_shapes=[pltpu.VMEM((n, rows, LANES), f32)],
        compiler_params=params(8),
    )(
        me_in,
        sample_ids,
        hbm(activations.reshape(act_shape)),
        hbm(forward_exponent.reshape(expo_shape)),
        hbm(sender_base),
        hbm(receiver_base),
        hbm(cotangent.reshape(share_shape)),
        hbm(norm_gain.reshape(1, width_all)),
    )
    packed = [shift(x, r) for r, x in enumerate(packed)]
    cot_line, *blocks = call(
        sort_kernel,
        (struct(line_shape, bf16),) + (struct((quarter, rows, LANES), bf16),) * 4,
        [SMEM] + [VMEM] * quarter,
        [me_in, *packed],
        micros=STAGE,
    )
    blocks = [blocks[0]] + [swap(blocks[e], e) for e in range(1, 4)]
    cots = [cot_line]

    ANY = pl.BlockSpec(memory_space=pl.ANY)
    share_f32 = struct(share_shape, f32)
    sums = (struct(hidden_shape, f32), struct((tokens, LANES), f32))

    def grad_active_part(part):
        return call(
            functools.partial(grad_active_kernel, part),
            (struct((hidden_dev, tokens), f32), share_f32),
            [SMEM, VMEM, VMEM],
            [me_in, cots[part], down_weight],
            [pltpu.VMEM(share_shape, f32)],
            micros=1.6,
        )

    def up_product_part(part):
        return call(
            functools.partial(up_kernel, part),
            sums + (share_f32,),
            [SMEM] + [VMEM] * 3,
            [me_in, rests[part], gain, up_weight],
            [pltpu.VMEM(share_shape, f32)],
            micros=1.2,
        )

    together = lax.optimization_barrier
    def rebuild(out, micros):
        return call(
            rebuild_kernel,
            out,
            [SMEM] + [VMEM] * 5,
            [me_in, *blocks, received],
            [
                pltpu.VMEM((n * rows, LANES), f32),
                pltpu.VMEM((2 * width // LANES, 2 * n, LANES), f32),
            ],
            micros=micros,
        )

    share = rebuild(struct(share_shape, bf16), STAGE)
    lines = [shift(share, r) for r in range(quarter)]
    cot_row = swap(cot_line, 2)
    cot_line, cot_row, share_after = together((cot_line, cot_row, share))
    cots = [cot_line]
    grads = [grad_active_part(0)]
    lines, grads[0] = together((lines, grads[0]))
    rest_line = jnp.stack(lines)
    rest_row = swap(rest_line, 2)
    rests = [rest_line]
    products = [up_product_part(0)]
    rest_line, cot_line, cot_row, products[0] = together((rest_line, cots[0], cot_row, products[0]))
    rest_line_other = swap(rest_line, 1)
    cots += [cot_row, swap(cot_line, 1), swap(cot_row, 1)]
    grads += [grad_active_part(part) for part in (1, 2, 3)]
    new_sender_base = call(
        sender_base_kernel,
        struct(sender_base.shape, f32),
        [SMEM, SMEM] + [VMEM] * 2,
        [me_in, sample_ids, new_rows, sender_base],
    )
    rest_row, grads, new_sender_base = together((rest_row, grads, new_sender_base))
    rests += [rest_row, rest_line_other, swap(rest_row, 1)]
    products += [up_product_part(1), up_product_part(2)]
    gas, own_cots = zip(*grads)
    accs, squares, owns = map(list, zip(*products))

    half_out = struct((half, tokens, width), bf16)
    active, grad_hidden, own = call(
        activation_kernel,
        (struct(hidden_shape, bf16), struct(hidden_shape, bf16), share_f32),
        [SMEM] + [VMEM] * 13,
        [me_in, rests[3], gain, up_weight, *accs, *squares, *gas],
        [pltpu.VMEM(x.shape, x.dtype) for x in sums] + [pltpu.VMEM(share_shape, f32)],
        micros=1.5,
    )
    owns.append(own)

    def down_terms(other, active):
        return call(
            functools.partial(down_kernel, other),
            half_out,
            [SMEM] + [VMEM] * 2,
            [me_in, active, down_weight],
            micros=1.5,
        )

    def pair_sum(kept, arrived):
        return call(
            pair_kernel,
            (struct(line_shape, bf16),) * 2,
            [SMEM] + [VMEM] * 2,
            [me_in, kept, arrived],
        )

    def line_sum(kept, arrived):
        shares = call(
            line_kernel,
            (struct(share_shape, bf16),) * quarter,
            [SMEM] + [VMEM] * 2,
            [me_in, kept, arrived],
        )
        far_first = [shift(shares[r], r) for r in reversed(range(quarter))]
        return far_first

    out_send = down_terms(1, active)
    out_in = swap(out_send, 1)
    active, out_send = together((active, out_send))
    out_send, out_row = pair_sum(down_terms(0, active), out_in)
    out_row_in = swap(out_send, 2)
    grad_hidden, out_row = together((grad_hidden, out_row))
    rows_out = struct((width // LANES, n * tokens, LANES), f32)
    grad_rows = call(
        grad_norm_kernel,
        rows_out,
        [SMEM] + [VMEM] * 2,
        [me_in, grad_hidden, up_weight],
        micros=4.5,
    )
    grad_rows, out_row_in = together((grad_rows, out_row_in))
    grad_send, grad_keep = call(
        split_kernel, (half_out, half_out), [SMEM, VMEM], [me_in, grad_rows], micros=0.4
    )
    grad_in = swap(grad_send, 1)
    received, blocks, grad_send = together((received, blocks, grad_send))
    new_receiver_base = rebuild(struct(receiver_base.shape, f32), 0.7)
    grad_in, new_receiver_base = together((grad_in, new_receiver_base))
    grad_send, grad_row = pair_sum(grad_keep, grad_in)
    grad_row_in = swap(grad_send, 2)
    out_row, grad_row = together((out_row, grad_row))
    out_line = line_sum(out_row, out_row_in)
    grad_line = line_sum(grad_row, grad_row_in)
    layer_out, own, own_cot = call(
        layer_kernel,
        (struct(share_shape, bf16), share_f32, share_f32),
        [VMEM] * (9 + quarter),
        [share, *owns, *own_cots, *out_line],
    )
    grad_line, layer_out, own, own_cot = together((grad_line, layer_out, own, own_cot))
    returned = call(
        functools.partial(final_kernel, width_all),
        struct((2, width_all // LANES, LANES), f32),
        [VMEM] * (4 + quarter),
        [own, own_cot, gain, backward_exponent.reshape(expo_shape), *grad_line],
    )
    return (
        new_sender_base,
        new_receiver_base,
        layer_out.reshape(2, n, width),
        returned.reshape(2, 1, width_all),
    )


def solution(mesh):
    placed = (
        P(None, ("groups", "dp"), None),
        P(("groups", "dp")),
        P(None, ("groups", "dp"), None),
        P(None, ("groups", "dp"), None),
        P(None, "groups", "dp"),
        P(),
        P(None, "dp"),
        P("dp", None),
        P(None, "groups", "dp"),
        P(None, ("groups", "dp"), None),
    )
    return jax.shard_map(
        functools.partial(on_device, n=mesh.shape["dp"]),
        mesh=mesh,
        in_specs=placed,
        out_specs=(
            P(None, ("groups", "dp"), None),
            P(None, "groups", "dp"),
            P(None, "groups", "dp"),
            P(None, ("groups", "dp"), None),
        ),
        check_vma=False,
    )
```
